128 devices in a mesh: sp: 8 (over x, y_lo), dp: 16 (over z, y_hi, core).
Axes of the slice: x: 4, y: 4 (y_hi: 2, y_lo: 2; y = y_hi * 2 + y_lo), z: 4, core: 2. Of those that a mesh axis runs over, the one named last changes fastest.
Arguments:
- queries: bfloat16 [16, 2048, 3072], P('dp', 'sp'), may hold values from -6 to 6
- keys: bfloat16 [16, 2048, 3072], P('dp', 'sp'), may hold values from -6 to 6
- values: bfloat16 [16, 2048, 3072], P('dp', 'sp'), may hold values from -6 to 6
- latents: float32 [16, 2048, 64], P('dp', 'sp'), may hold values from -6 to 6
- noise: float32 [16, 2048, 64], P('dp', 'sp'), may hold values from -6 to 6
- head_weight: bfloat16 [3072, 64], replicated, may hold values from -0.4375 to 0.4375
- adapter_down: bfloat16 [3072, 128], P(('sp', 'dp')), may hold values from -0.109375 to 0.109375
- adapter_up: bfloat16 [128, 64], replicated, may hold values from -0.5 to 0.5
- advantages: float32 [16], replicated, may hold values from -6 to 6
- lengths: int32 [16], replicated, may hold values from 1024 to 2048, as said below
- timesteps: int32 [16], replicated, may hold values from 0 to 15
- destinations: int32 [16, 8, 16, 1], P('dp', 'sp'), may hold values from 0 to 15; in each aligned block of 16 rows (0 to 15, 16 to 31, ..., all dimensions but the last counted through in order) at most 2 rows name the same one
Outputs:
- next_latents: float32 [16, 2048, 64], P('dp', 'sp')
- learner_delta: float32 [16, 8, 512, 64], P('dp', 'sp')
- ratios: float32 [16], replicated
- grad_adapter_down: float32 [3072, 128], P(('sp', 'dp'))
The draws below stay inside these ranges and needn't reach their ends.
Inputs may be any that keep to these rules, and one draw needn't show every extreme that they name: `lengths`: every video has at least 1024 valid tokens; some video has exactly 2048. `destinations`: among the 16 blocks of one device no learner index appears more than 2 times, and some device reaches 2.
All inputs are finite; a program needn't handle non-finite values.
Results may differ from the reference program's by a relative error of at most 0.014.
Values may be sent and summed in bfloat16 or wider, within the bound.
A program may use at most 64 MiB of HBM per device.

```python
import math
from functools import partial
import jax
import jax.numpy as jnp
import numpy as np
from jax import lax

D = 3072
HEAD_DIM = 128
CHANNELS = 64
RANK = 128
ROWS_BLK = 16
STEPS = 16
HEADS = 24
SEQ = 2048
VIDEOS = 16
NBLK = 16
CAP = 2
SLOT_ROWS = 512
N_SP = 8
N_DP = 16


FRACTIONS = (0.4, 0.7, 1.0)


def draw_lengths(key, part):
    key = jax.random.fold_in(key, 7)
    first_key, second_key = jax.random.split(key)
    counts = jax.random.randint(first_key, (VIDEOS,), SEQ // 2, SEQ + 1)
    chosen = jax.random.randint(second_key, (), 0, VIDEOS)
    return jnp.where(jnp.arange(VIDEOS) == chosen, SEQ, counts).astype(jnp.int32)


def choose_rows(seed_key, span, count):
    return jax.random.permutation(seed_key, span)[:count].astype(jnp.int32)


def drawn(key):
    count = len(FRACTIONS)
    query_key, row_key, head_key, sign_key = jax.random.split(key, 4)
    query_rows = jax.vmap(partial(choose_rows, span=SEQ, count=count))(jax.random.split(query_key, VIDEOS))
    key_rows = jax.vmap(partial(choose_rows, span=SEQ // 2, count=2 * count))(jax.random.split(row_key, VIDEOS))
    key_rows = key_rows.reshape(VIDEOS, count, 2)
    heads = jax.random.randint(head_key, (VIDEOS, count), 0, HEADS).astype(jnp.int32)
    signs = (2 * jax.random.randint(sign_key, (VIDEOS, count, HEAD_DIM), 0, 2) - 1).astype(jnp.float32)
    highest = min(300.0, 34.0 * math.sqrt(HEAD_DIM))
    strengths = jnp.array(FRACTIONS, jnp.float32) * highest
    amplitude = jnp.sqrt(strengths / math.sqrt(HEAD_DIM))
    per_entry = strengths / HEAD_DIM
    dropped = jnp.maximum(1.0, jnp.floor(2.0 / per_entry + 0.5))
    return (query_rows, key_rows, heads, signs, amplitude, dropped)


def place_rows(field, rows, heads, planted_values):
    video_index = jnp.arange(VIDEOS).astype(jnp.int32)[:, None, None]
    feature_index = heads[:, :, None] * HEAD_DIM + jnp.arange(HEAD_DIM).astype(jnp.int32)[None, None, :]
    row_index = rows[:, :, None] + 0 * feature_index
    video_full = video_index + 0 * feature_index
    return field.at[video_full, row_index, feature_index].set(planted_values)


def draw_queries(key, part):
    shared = drawn(key)
    key = jax.random.fold_in(key, 11)
    field = jax.random.truncated_normal(key, -6.0, 6.0, (VIDEOS, SEQ, D), jnp.float32)
    query_rows, key_rows, heads, signs, amplitude, dropped = shared
    planted_values = amplitude[None, :, None] * signs
    return place_rows(field, query_rows, heads, planted_values).astype(jnp.bfloat16)


def draw_keys(key, part):
    shared = drawn(key)
    key = jax.random.fold_in(key, 13)
    field = jax.random.truncated_normal(key, -6.0, 6.0, (VIDEOS, SEQ, D), jnp.float32)
    query_rows, key_rows, heads, signs, amplitude, dropped = shared
    first_values = amplitude[None, :, None] * signs
    kept = (jnp.arange(HEAD_DIM).astype(jnp.float32)[None, None, :] >= dropped[None, :, None]).astype(jnp.float32)
    second_values = first_values * kept
    field = place_rows(field, key_rows[:, :, 0], heads, first_values)
    field = place_rows(field, key_rows[:, :, 1], heads, second_values)
    return field.astype(jnp.bfloat16)


def set_ends(result, rng, smallest, largest):
    place = [jax.random.randint(jax.random.fold_in(rng, axis), (), 0, length) for axis, length in enumerate(result.shape)]
    main_axis = result.shape.index(max(result.shape))
    neighbour = place[:main_axis] + [(place[main_axis] + 1) % result.shape[main_axis]] + place[main_axis + 1:]
    return result.at[tuple(place)].set(smallest).at[tuple(neighbour)].set(largest)


def level_of(key, shape, cuts, smallest, high):
    factor_of, own = 1.0, jax.random.fold_in(key, 6)
    for axis_at, blocks in cuts:
        draws = jnp.exp(jax.random.uniform(jax.random.fold_in(own, axis_at), (blocks,), jnp.float32, smallest / len(cuts), high / len(cuts)))
        factor_of = factor_of * jnp.repeat(draws, shape[axis_at] // blocks).reshape([-1 if axis == axis_at else 1 for axis in range(len(shape))])
    return factor_of


def shared_out(key, own, number, rows, number_of, top, most, skew):
    order = jax.random.permutation(key, number_of)
    packed, usual = portions_of(number_of, rows * top, most, skew, True), portions_of(number_of, rows * top, most, skew, False)
    places = jnp.arange(number_of)

    def named(sizes, rotation):
        used = int((sizes > 0).sum())
        fixed = max(1, used // 4)
        passed = fixed + (places - fixed + rotation * (used - fixed)) % max(1, number_of - fixed)
        return jnp.zeros((number_of,), jnp.int32).at[order[jnp.where(places < fixed, places, passed)]].set(jnp.asarray(sizes, jnp.int32))

    sizes = jnp.where(number % 4 == 0, named(packed, number // 4), named(usual, number - number // 4 - 1))
    mixed = jax.random.permutation(jax.random.fold_in(own, 3), number_of)
    donor, sink = mixed[0:number_of // 2 * 2:2], mixed[1:number_of // 2 * 2:2]
    margin = jnp.minimum(sizes[donor] - 1, most - sizes[sink]) // 2
    margin = jnp.where((donor == order[0]) | (sink == order[0]) | (sizes[sink] == 0), 0, jnp.maximum(margin, 0))
    passed = jax.random.randint(jax.random.fold_in(own, 4), (number_of // 2,), 0, 1 << 20) % (margin + 1)
    sizes = sizes.at[donor].add(-passed).at[sink].add(passed)
    items = jnp.searchsorted(jnp.cumsum(sizes), jnp.arange(rows * top), side="right").astype(jnp.int32)
    grid = items.reshape(top, rows).T
    grid = grid[jax.random.permutation(jax.random.fold_in(own, 1), rows)]
    rotation = jax.random.randint(jax.random.fold_in(own, 2), (rows, 1), 0, top)
    return jnp.take_along_axis(grid, (jnp.arange(top)[None, :] + rotation) % top, axis=1)


def portions_of(count, total, bound, slope, full):
    weights = [(1 << 20) // math.isqrt(rank ** slope) + 1 for rank in range(1, count + 1)]
    largest = bound if full else min(bound, max(-(-total // count), total * weights[0] // sum(weights)))
    least = 1 if total - largest >= count - 1 else 0
    given, spare = [largest] + [least] * (count - 1), total - largest - least * (count - 1)
    while spare > 0:
        movable = [i for i in range(1, count) if given[i] < largest] or [i for i in range(1, count) if given[i] < bound]
        whole, left = sum([weights[i] for i in movable]), spare
        for i in movable:
            addition = min(bound - given[i], max(1, left * weights[i] // whole), spare)
            given[i] = given[i] + addition
            spare = spare - addition
    return np.array(given)


def normal_values(own_key, shape, width, limit, shards=(), held_as=jnp.bfloat16):
    level = level_of(own_key, shape, shards, -0.22, 0.18) if shards else 1.0
    values = jax.random.normal(own_key, shape, jnp.float32) * width * level
    return jnp.minimum(jnp.maximum(values, -limit), limit).astype(held_as)


def setup_inputs(seed: int = 0) -> dict:
    key_list = jax.random.split(jax.random.key(seed), 13)
    queries = draw_queries(jax.random.fold_in(key_list[12], 71), 0)
    keys = draw_keys(jax.random.fold_in(key_list[12], 71), 0)
    values = normal_values(key_list[2], (VIDEOS, SEQ, D), 1.0, 6.0, ((0, 16), (1, 8)))
    latents = normal_values(key_list[3], (VIDEOS, SEQ, CHANNELS), 1.0, 6.0, ((0, 16), (1, 8)), jnp.float32)
    noise = normal_values(key_list[4], (VIDEOS, SEQ, CHANNELS), 1.0, 6.0, ((0, 16), (1, 8)), jnp.float32)
    head_weight = normal_values(key_list[5], (D, CHANNELS), (D // 16) ** -0.5, 0.4375)
    adapter_down = normal_values(key_list[6], (D, RANK), D ** -0.5, 0.109375, ((0, 128),))
    adapter_up = normal_values(key_list[7], (RANK, CHANNELS), RANK ** -0.5, 0.5)
    advantages = normal_values(key_list[8], (VIDEOS,), 1.0, 6.0, (), jnp.float32)
    lengths = draw_lengths(jax.random.fold_in(key_list[12], 71), 0)
    timesteps = set_ends(jax.random.randint(key_list[10], (VIDEOS,), 0, STEPS), jax.random.fold_in(key_list[10], 1), 0, STEPS - 1).astype(jnp.int32)
    destinations_keys = jax.random.split(jax.random.fold_in(key_list[11], 1), VIDEOS * N_SP * NBLK // NBLK)
    destinations_turns = jax.random.permutation(jax.random.fold_in(key_list[11], 3), VIDEOS * N_SP * NBLK // NBLK)
    destinations = jax.vmap(lambda own, number: shared_out(jax.random.fold_in(key_list[11], 2), own, number, NBLK, N_DP, 1, CAP, 0))(destinations_keys, destinations_turns).reshape((VIDEOS, N_SP, NBLK, 1))
    return dict(queries=queries, keys=keys, values=values, latents=latents, noise=noise, head_weight=head_weight, adapter_down=adapter_down, adapter_up=adapter_up, advantages=advantages, lengths=lengths, timesteps=timesteps, destinations=destinations)


ETA = 0.3
CLIP = 0.2
LOSS_SCALE = 4096.0
NORM_EPS = 1e-06

def plan(moments):
    level = 1.0 - moments.astype(jnp.float32) / STEPS
    step_size = jnp.float32(1.0 / STEPS)
    noise_scale = ETA * jnp.sqrt(step_size) * (0.5 + level)
    return (step_size, noise_scale)

def attend_head(query_head, key_head, value_head, live_keys):
    sequence = query_head.shape[0]
    block_rows = min(512, sequence)
    stacked = query_head.reshape(sequence // block_rows, block_rows, query_head.shape[1])

    def one_block(query_block):
        scores = jnp.dot(query_block, key_head.T, preferred_element_type=jnp.float32) * query_head.shape[1] ** (-0.5)
        scores = jnp.where(live_keys[None, :], scores, -1e+30)
        highest = lax.optimization_barrier(jnp.max(scores, axis=1, keepdims=True))
        weights = jnp.exp(scores - highest)
        totals = lax.optimization_barrier(jnp.sum(weights, axis=1, keepdims=True))
        mixed_block = jnp.dot(weights.astype(jnp.bfloat16), value_head, preferred_element_type=jnp.float32) / totals
        return mixed_block.astype(jnp.bfloat16)
    return lax.map(one_block, stacked).reshape(sequence, query_head.shape[1])

def normalize(feature_rows):
    wide = feature_rows.astype(jnp.float32)
    centre = lax.optimization_barrier(jnp.mean(wide, axis=-1, keepdims=True))
    spread = lax.optimization_barrier(jnp.mean((wide - centre) * (wide - centre), axis=-1, keepdims=True))
    return ((wide - centre) * lax.rsqrt(spread + NORM_EPS)).astype(jnp.bfloat16)

def objective(log_gains, advantages):
    ratios = jnp.exp(log_gains)
    clipped = jnp.clip(ratios, 1.0 - CLIP, 1.0 + CLIP)
    active = (ratios * advantages <= clipped * advantages).astype(jnp.float32)
    pull_video = -(LOSS_SCALE / advantages.shape[0]) * advantages * ratios * active
    return (ratios, pull_video)

def reference(queries, keys, values, latents, noise, head_weight, adapter_down, adapter_up, advantages, lengths, timesteps, destinations):
    step_size, noise_scale = plan(timesteps)
    positions = jnp.arange(SEQ)

    def video_attention(inputs):
        query_video, key_video, value_video, length = inputs
        live_keys = positions < length
        query_heads = query_video.reshape(SEQ, HEADS, HEAD_DIM)
        key_heads = key_video.reshape(SEQ, HEADS, HEAD_DIM)
        value_heads = value_video.reshape(SEQ, HEADS, HEAD_DIM)

        def per_head(query_head, key_head, value_head):
            return attend_head(query_head, key_head, value_head, live_keys)
        mixed = jax.vmap(per_head, in_axes=(1, 1, 1), out_axes=1)(query_heads, key_heads, value_heads)
        return mixed.reshape(SEQ, D)
    attention = lax.map(video_attention, (queries, keys, values, lengths))
    flat_attention = attention.reshape(VIDEOS * SEQ, D)
    velocity = jnp.dot(flat_attention, head_weight, preferred_element_type=jnp.float32).reshape(VIDEOS, SEQ, CHANNELS)
    mean_old = latents - step_size * velocity
    next_latents = mean_old + noise_scale[:, None, None] * noise
    offset_rows = next_latents - mean_old
    normed = normalize(flat_attention)
    adapter_codes = jnp.dot(normed, adapter_down, preferred_element_type=jnp.float32).astype(jnp.bfloat16)
    adapter_delta = jnp.dot(adapter_codes, adapter_up, preferred_element_type=jnp.float32).reshape(VIDEOS, SEQ, CHANNELS)
    live_rows = (positions[None, :] < lengths[:, None]).astype(jnp.float32)
    row_weight = live_rows / (lengths.astype(jnp.float32)[:, None] * CHANNELS)
    inverse = 1.0 / (2.0 * noise_scale * noise_scale)
    new_offset = offset_rows - step_size * adapter_delta
    row_terms = row_weight * inverse[:, None] * lax.optimization_barrier(jnp.sum(offset_rows * offset_rows - new_offset * new_offset, axis=2))
    log_gains = lax.optimization_barrier(jnp.sum(row_terms, axis=1))
    ratios, pull_video = objective(log_gains, advantages)
    grad_delta = ((pull_video[:, None] * row_weight * inverse[:, None] * 2.0 * step_size)[:, :, None] * new_offset).astype(jnp.bfloat16)
    flat_grad = grad_delta.reshape(VIDEOS * SEQ, CHANNELS)
    grad_codes = jnp.dot(flat_grad, adapter_up.T, preferred_element_type=jnp.float32).astype(jnp.bfloat16)
    grad_adapter_down = jnp.dot(normed.T, grad_codes, preferred_element_type=jnp.float32)
    target = destinations[..., 0]
    block_order = jnp.arange(NBLK)
    before = (target[..., None, :] == target[..., :, None]) & (block_order[None, :] < block_order[:, None])
    slot_rank = lax.optimization_barrier(jnp.sum(before.astype(jnp.int32), axis=-1))
    to_learner = target[..., None] == jnp.arange(VIDEOS).astype(jnp.int32)[None, None, None, :]
    to_slot = slot_rank[..., None] == jnp.arange(CAP).astype(jnp.int32)[None, None, None, :]
    placing = (to_learner[..., :, None] & to_slot[..., None, :]).astype(jnp.float32)
    delta_blocks = adapter_delta.reshape(VIDEOS, N_SP, NBLK, ROWS_BLK, CHANNELS)
    learner_delta = jnp.einsum('ijbkr,ijbtc->kjirtc', placing, delta_blocks, precision=lax.Precision.HIGHEST)
    learner_delta = learner_delta.reshape(VIDEOS, N_SP, SLOT_ROWS, CHANNELS)
    return (next_latents, learner_delta, ratios, grad_adapter_down)
```

```python
import functools

import jax
import jax.numpy as jnp
from jax import lax
from jax.experimental import pallas as pl
from jax.experimental.pallas import tpu as pltpu
from jax.sharding import PartitionSpec as P

MESH = pl.DeviceIdType.MESH
F32 = jnp.float32
BF16 = jnp.bfloat16

HD = 128
CH = 64
STEPS = 16
ETA = 0.3
CLIP = 0.2
LOSS_SCALE = 4096.0
NORM_EPS = 1e-06
NSP = 8
NDP = 16
ROWS = 256
SEQ = 2048
HEADS = 3
FEAT = HEADS * HD
OWN = 24
LOG2E = 1.4426950408889634
STEP = 1.0 / STEPS

OFFSETS = ((2, 1), (2, 0), (1, 1), (3, 1), (1, 0), (3, 0), (0, 1))
NP = len(OFFSETS)


def nt(a, b):
    return lax.dot_general(a, b, (((1,), (1,)), ((), ())), preferred_element_type=F32)


def tn(a, b):
    return lax.dot_general(a, b, (((0,), (0,)), ((), ())), preferred_element_type=F32)


def nn(a, b):
    return jnp.dot(a, b, preferred_element_type=F32)


def kernel(
    q_hbm, k_hbm, v_hbm, lat_hbm, noise_hbm, hw_hbm, ad_ref, up_ref, adv_ref, len_ref, time_ref, dest_ref,
    next_ref, learn_ref, ratio_ref, grad_ref,
    qland, kland, vland, att, lat, noise, wt, hw, piece, wg, cs_out, cs_in, csb, hwb,
    r1s, r1r, r2, slots, learn_in, g_out, g_in,
    loc_sem, s0, r0, sa, ra, sc, rc, s1, r1, s2, rr2, sl, rl, s3, r3,
):
    me = lax.axis_index("sp")
    vid = lax.axis_index("dp")
    mx, my = me // 2, me % 2

    def peer(i):
        dx, dy = OFFSETS[i]
        return ((mx + dx) % 4) * 2 + (my + dy) % 2

    def source(i):
        dx, dy = OFFSETS[i]
        return ((mx + 4 - dx) % 4) * 2 + (my + 2 - dy) % 2

    def dp_peer(e):
        return (vid + e) % NDP

    def dp_source(e):
        return (vid + NDP - e) % NDP

    def rows_of(s):
        return pl.ds(pl.multiple_of(s * ROWS, ROWS), ROWS)

    def columns_of(s, h):
        return pl.ds(pl.multiple_of(s * FEAT + h * HD, HD), HD)

    barrier = pltpu.get_barrier_semaphore()
    for i in range(NP):
        pl.semaphore_signal(barrier, inc=1, device_id=(peer(i), vid), device_id_type=MESH)
    for e in range(1, NDP):
        pl.semaphore_signal(barrier, inc=1, device_id=(me, dp_peer(e)), device_id_type=MESH)

    sources = (k_hbm, q_hbm, v_hbm)

    def landing(t, h, s):
        if t == 2:
            return vland.at[h, rows_of(s), pl.ds(0, HD)]
        return (kland, qland)[t].at[h, rows_of(s), :]

    local = []
    for g in range(9):
        h, t = g // 3, g % 3
        local.append(
            pltpu.make_async_copy(sources[t].at[0, :, columns_of(me, h)], landing(t, h, me), loc_sem.at[g])
        )
    hw_copy = pltpu.make_async_copy(
        hw_hbm.at[:, pl.ds(pl.multiple_of(me * FEAT, HD), FEAT)], hw, loc_sem.at[9]
    )
    lat_copy = pltpu.make_async_copy(lat_hbm, lat, loc_sem.at[10])
    noise_copy = pltpu.make_async_copy(noise_hbm, noise, loc_sem.at[11])
    extra = [hw_copy, lat_copy, noise_copy]

    pl.semaphore_wait(barrier, NP + NDP - 1)

    order = (0, 1, 2, 3, 4, 5, 6, 8, 7)
    groups = []
    for g in order:
        h, t = g // 3, g % 3
        groups.append(
            [
                pltpu.make_async_remote_copy(
                    src_ref=sources[t].at[0, :, columns_of(peer(i), h)],
                    dst_ref=landing(t, h, me),
                    send_sem=s0.at[g, i],
                    recv_sem=r0.at[g, i],
                    device_id=(peer(i), vid),
                    device_id_type=MESH,
                )
                for i in range(NP)
            ]
        )

    def issue(n):
        for c in groups[n]:
            c.start()

    def sent(n):
        for c in groups[n]:
            c.wait_send()

    def arrived(n):
        for c in groups[n]:
            c.wait_recv()

    for n in range(3):
        issue(n)
    for c in local + extra:
        c.start()

    up = up_ref[...]
    up_low = jnp.concatenate([jnp.zeros_like(up), up], axis=0)
    piece[...] = nt(ad_ref[...], up_low)
    own_rows = pl.ds(pl.multiple_of(vid * OWN, 8), OWN)
    gather = [
        pltpu.make_async_remote_copy(
            src_ref=piece,
            dst_ref=wg.at[own_rows, :],
            send_sem=sa.at[e],
            recv_sem=ra.at[e],
            device_id=(me, dp_peer(e)),
            device_id_type=MESH,
        )
        for e in range(1, NDP)
    ]
    for c in gather:
        c.start()
    wg[own_rows, :] = piece[...]
    for h in range(HEADS):
        vland[h, :, HD:] = jnp.ones((SEQ, HD), BF16)
    hw_copy.wait()
    for c in gather:
        c.wait()
    wt[0:CH, :] = hw[...]
    wt[CH:, :] = jnp.transpose(wg[...])[CH:, :].astype(BF16)
    ones = jnp.ones((16, FEAT), BF16)
    cs_out[...] = nt(ones, wt[...])[0:8]
    cs_copies = [
        pltpu.make_async_remote_copy(
            src_ref=cs_out,
            dst_ref=cs_in.at[i],
            send_sem=sc.at[i],
            recv_sem=rc.at[i],
            device_id=(peer(i), vid),
            device_id_type=MESH,
        )
        for i in range(NP)
    ]
    for c in cs_copies:
        c.start()
    cs_in[NP] = cs_out[...]
    for c in cs_copies:
        c.wait()
    for i in range(NP + 1):
        spread = jnp.transpose(jnp.broadcast_to(cs_in[i][0:1], (HD, HD)))
        csb[i] = spread[CH:]
        if i == NP:
            hwb[...] = spread[:CH]

    length = len_ref[vid]
    moment = time_ref[vid].astype(F32)
    noise_scale = jnp.full((1, ROWS), (ETA * 0.25) * (0.5 + (1.0 - moment * STEP)), F32)
    inverse = 1.0 / (2.0 * noise_scale * noise_scale)
    token = me * ROWS + lax.broadcasted_iota(jnp.int32, (1, ROWS), 1)
    live = jnp.where(token < length, 1.0, 0.0).astype(F32)
    row_weight = live / (jnp.full((1, ROWS), length.astype(F32), F32) * CH)
    gain = row_weight * inverse
    key_at = SEQ // 2 + lax.broadcasted_iota(jnp.int32, (1, SEQ // 2), 1)
    cap = jnp.where(key_at < length, 3e38, -1e30).astype(F32)

    def attend(h, rows):
        scores = nt(qland[h, rows, :], kland[h]) * (LOG2E * HD**-0.5)
        first = scores[:, : SEQ // 2]
        second = jnp.minimum(scores[:, SEQ // 2 :], cap)
        highest = jnp.maximum(
            jnp.max(first, axis=1, keepdims=True), jnp.max(second, axis=1, keepdims=True)
        )
        low = jnp.exp2(first - highest).astype(BF16)
        high = jnp.exp2(second - highest).astype(BF16)
        mixed = nn(jnp.concatenate([low, high], axis=1), vland[h])
        att[rows, h * HD : (h + 1) * HD] = (mixed[:, :HD] / mixed[:, HD:]).astype(BF16)

    def attend_all(h):
        @pl.loop(0, NSP)
        def _(b):
            attend(h, rows_of(b))

    for c in local + [lat_copy, noise_copy]:
        c.wait()
    for h in range(2):
        for t in range(3):
            n = h * 3 + t
            sent(n)
            issue(n + 3)
            arrived(n)
        attend_all(h)

    for n in (6, 7):
        arrived(n)

    def partial_sums(rows):
        feature = att[rows, :]
        wide = feature.astype(F32)
        centred = wide - jnp.sum(wide, axis=1, keepdims=True) * (1.0 / FEAT)
        sums = nt(wt[...], centred.astype(BF16))
        mean = nt(ones, feature) * (1.0 / FEAT)
        square = nt(ones, (centred * centred).astype(BF16))
        spread = jnp.concatenate([hwb[...], hwb[...]], axis=1)
        velocity = sums[:CH] + spread * mean[0:1]
        line = lax.broadcasted_iota(jnp.int32, (16, ROWS), 0)
        mean_high = mean.astype(BF16).astype(F32)
        square_high = square.astype(BF16).astype(F32)
        stats = jnp.where(
            line == 0,
            mean_high,
            jnp.where(line == 1, mean - mean_high, jnp.where(line == 2, square_high, square - square_high)),
        )
        return jnp.concatenate([velocity, sums[CH:], stats], axis=0).astype(BF16)

    part_copies = [
        pltpu.make_async_remote_copy(
            src_ref=r1s.at[i],
            dst_ref=r1r.at[i],
            send_sem=s1.at[i],
            recv_sem=r1.at[i],
            device_id=(peer(i), vid),
            device_id_type=MESH,
        )
        for i in range(NP)
    ]
    opposite = [OFFSETS.index(((4 - dx) % 4, (2 - dy) % 2)) for dx, dy in OFFSETS]
    for i in range(NP):
        groups[8][opposite[i]].wait_recv()
        rows = rows_of(peer(i))
        attend(2, rows)
        r1s[i] = partial_sums(rows)
        part_copies[i].start()
    attend(2, rows_of(me))
    r1r[NP] = partial_sums(rows_of(me))
    for n in (6, 7, 8):
        sent(n)
    for c in part_copies:
        c.wait()

    parts = [r1r[i].astype(F32) for i in range(NP + 1)]
    total = parts[0][: 2 * CH]
    for p in parts[1:]:
        total = total + p[: 2 * CH]
    means = [p[128:129] + p[129:130] for p in parts]
    squares = [p[130:131] + p[131:132] for p in parts]
    mean = functools.reduce(jnp.add, means) * (1.0 / NSP)
    gaps = [m - mean for m in means]
    variance = functools.reduce(jnp.add, squares) + FEAT * functools.reduce(jnp.add, [g * g for g in gaps])
    rstd = lax.rsqrt(variance * (1.0 / (FEAT * NSP)) + NORM_EPS)
    inner = total[CH:]
    for i in range(NP + 1):
        inner = inner + jnp.concatenate([csb[i], csb[i]], axis=1) * gaps[i]
    delta = inner * rstd
    offset = noise_scale * noise[...]
    gap = offset - STEP * delta
    unit = (gap * (gain * (2.0 * STEP) * rstd)).astype(BF16)
    terms = gain * jnp.sum(offset * offset - gap * gap, axis=0, keepdims=True)
    line = lax.broadcasted_iota(jnp.int32, (16, ROWS), 0)
    mean_high = mean.astype(BF16).astype(F32)
    terms_high = terms.astype(BF16).astype(F32)
    terms_rest = terms - terms_high
    terms_mid = terms_rest.astype(BF16).astype(F32)
    side = jnp.where(line == 0, mean_high, jnp.where(line == 1, mean - mean_high, 0.0))
    side = jnp.where(line == 2, terms_high, side)
    side = jnp.where(line == 3, terms_mid, jnp.where(line == 4, terms_rest - terms_mid, side))
    r2[me, 0:CH] = unit
    r2[me, CH : CH + 16] = side.astype(BF16)
    unit_copies = [
        pltpu.make_async_remote_copy(
            src_ref=r2.at[me],
            dst_ref=r2.at[me],
            send_sem=s2.at[i],
            recv_sem=rr2.at[i],
            device_id=(peer(i), vid),
            device_id_type=MESH,
        )
        for i in range(NP)
    ]
    for c in unit_copies:
        c.start()

    lane = lax.broadcasted_iota(jnp.int32, (1, ROWS), 1)
    targets = [dest_ref[0, b] for b in range(16)]
    place = jnp.zeros((1, ROWS), jnp.int32)
    for b in range(16):
        rank = jnp.int32(0)
        for a in range(b):
            rank = rank + jnp.where(targets[a] == targets[b], 1, 0)
        place = jnp.where(lane // 16 == b, targets[b] * 2 + rank, place)
    place = place * 16 + lane % 16
    placing = (lax.broadcasted_iota(jnp.int32, (512, ROWS), 0) == place).astype(F32).astype(BF16)
    delta_low = delta.astype(BF16)
    slots[...] = nt(placing, jnp.concatenate([delta_low, jnp.zeros_like(delta_low)], axis=0)).astype(BF16)
    mine = pl.ds(pl.multiple_of(vid * 32, 32), 32)
    learn_copies = [
        pltpu.make_async_remote_copy(
            src_ref=slots.at[pl.ds(pl.multiple_of(dp_peer(e) * 32, 32), 32), :],
            dst_ref=learn_in.at[mine, :],
            send_sem=sl.at[e],
            recv_sem=rl.at[e],
            device_id=(me, dp_peer(e)),
            device_id_type=MESH,
        )
        for e in range(1, NDP)
    ]
    for c in learn_copies:
        c.start()
    learn_in[mine, :] = slots[mine, :]
    next_ref[...] = (lat[...] - STEP * total[:CH]) + offset

    def grad_part(s):
        u = r2[s, 0:CH]
        side = r2[s, CH : CH + 16]
        shift = nt(u, side)
        return nn(u, att[rows_of(s), :]) - (shift[:, 0:1] + shift[:, 1:2])

    grad = grad_part(me)
    for i in range(NP):
        unit_copies[i].wait_recv()
        grad = grad + grad_part(source(i))
    sides = r2[0, CH : CH + 16].astype(F32)
    for s in range(1, NSP):
        sides = sides + r2[s, CH : CH + 16].astype(F32)
    log_gain = jnp.sum(sides[2:3] + sides[3:4] + sides[4:5], axis=1, keepdims=True)
    log_gain = jnp.broadcast_to(log_gain, (8, HD))
    ratio = jnp.exp(log_gain)
    advantage = adv_ref[vid]
    clipped = jnp.clip(ratio, 1.0 - CLIP, 1.0 + CLIP)
    active = jnp.where(ratio * advantage <= clipped * advantage, 1.0, 0.0)
    pull = -(LOSS_SCALE / NDP) * advantage * ratio * active
    grad_high = grad.astype(BF16)
    grad_rest = (grad - grad_high.astype(F32)).astype(BF16)
    product = tn(jnp.concatenate([grad_high, grad_rest], axis=0), jnp.concatenate([up, up], axis=0))
    product = product * pull[0:1]
    for k in range(NDP):
        g_out[k, 0:OWN] = product[k * OWN : (k + 1) * OWN]
        g_out[k, OWN : OWN + 8] = log_gain
    grad_copies = [
        pltpu.make_async_remote_copy(
            src_ref=g_out.at[dp_peer(e)],
            dst_ref=g_in.at[vid],
            send_sem=s3.at[e],
            recv_sem=r3.at[e],
            device_id=(me, dp_peer(e)),
            device_id_type=MESH,
        )
        for e in range(1, NDP)
    ]
    for c in grad_copies:
        c.start()
    g_in[vid] = g_out[vid]

    for c in learn_copies:
        c.wait()
    select = lax.broadcasted_iota(jnp.int32, (CH, HD), 0) == lax.broadcasted_iota(jnp.int32, (CH, HD), 1)
    learn_ref[...] = nt(select.astype(F32).astype(BF16), learn_in[...])
    for c in unit_copies:
        c.wait_send()

    for c in grad_copies:
        c.wait()
    summed = g_in[0, 0:OWN]
    for k in range(1, NDP):
        summed = summed + g_in[k, 0:OWN]
    grad_ref[...] = summed
    column = lax.broadcasted_iota(jnp.int32, (8, HD), 1)
    gains = jnp.zeros((8, HD), F32)
    for k in range(NDP):
        gains = jnp.where(column == k, g_in[k, OWN : OWN + 8], gains)
    ratio_ref[...] = jnp.exp(gains)


def on_device(
    queries, keys, values, latents, noise, head_weight, adapter_down, adapter_up, advantages, lengths, timesteps,
    destinations,
):
    hbm = pl.BlockSpec(memory_space=pl.ANY)
    vmem = pl.BlockSpec(memory_space=pltpu.VMEM)
    smem = pl.BlockSpec(memory_space=pltpu.SMEM)
    dma = pltpu.SemaphoreType.DMA
    nxt, learn, ratio, grad = pl.pallas_call(
        kernel,
        out_shape=(
            jax.ShapeDtypeStruct((CH, ROWS), F32),
            jax.ShapeDtypeStruct((CH, 512), F32),
            jax.ShapeDtypeStruct((8, HD), F32),
            jax.ShapeDtypeStruct((OWN, HD), F32),
        ),
        in_specs=[hbm] * 6 + [vmem] * 2 + [smem] * 4,
        out_specs=(vmem,) * 4,
        scratch_shapes=[
            pltpu.VMEM((HEADS, SEQ, HD), BF16),
            pltpu.VMEM((HEADS, SEQ, HD), BF16),
            pltpu.VMEM((HEADS, SEQ, 2 * HD), BF16),
            pltpu.VMEM((SEQ, FEAT), BF16),
            pltpu.VMEM((CH, ROWS), F32),
            pltpu.VMEM((CH, ROWS), F32),
            pltpu.VMEM((2 * CH, FEAT), BF16),
            pltpu.VMEM((CH, FEAT), BF16),
            pltpu.VMEM((OWN, HD), F32),
            pltpu.VMEM((FEAT, HD), F32),
            pltpu.VMEM((8, HD), F32),
            pltpu.VMEM((NSP, 8, HD), F32),
            pltpu.VMEM((NSP, CH, HD), F32),
            pltpu.VMEM((CH, HD), F32),
            pltpu.VMEM((NP, 144, ROWS), BF16),
            pltpu.VMEM((NSP, 144, ROWS), BF16),
            pltpu.VMEM((NSP, CH + 16, ROWS), BF16),
            pltpu.VMEM((512, HD), BF16),
            pltpu.VMEM((512, HD), BF16),
            pltpu.VMEM((NDP, OWN + 8, HD), F32),
            pltpu.VMEM((NDP, OWN + 8, HD), F32),
            dma((12,)),
            dma((9, NP)), dma((9, NP)),
            dma((NDP,)), dma((NDP,)),
            dma((NP,)), dma((NP,)),
            dma((NP,)), dma((NP,)),
            dma((NP,)), dma((NP,)),
            dma((NDP,)), dma((NDP,)),
            dma((NDP,)), dma((NDP,)),
        ],
        compiler_params=pltpu.CompilerParams(
            collective_id=0, has_side_effects=True, vmem_limit_bytes=56 * 2**20
        ),
        cost_estimate=pl.CostEstimate(
            flops=7 * 10**9, bytes_accessed=6 * 10**6, transcendentals=13 * 10**6
        ),
        name="policy_step",
    )(
        queries, keys, values, latents[0].T, noise[0].T, head_weight.T, adapter_down, adapter_up.T, advantages,
        lengths, timesteps, destinations.reshape(1, 16),
    )
    return nxt.T[None], learn.T[None, None], ratio[0, :NDP], grad


def solution(mesh):
    wide = P("dp", "sp", None)
    in_specs = (
        wide, wide, wide, wide, wide, P(), P(("sp", "dp"), None), P(), P(), P(), P(), P("dp", "sp", None, None),
    )
    out_specs = (wide, P("dp", "sp", None, None), P(), P(("sp", "dp"), None))
    return jax.shard_map(on_device, mesh=mesh, in_specs=in_specs, out_specs=out_specs, check_vma=False)
```

```python
import functools

import jax
import jax.numpy as jnp
from jax import lax
from jax.experimental import pallas as pl
from jax.experimental.pallas import tpu as pltpu
from jax.sharding import PartitionSpec as P

MESH = pl.DeviceIdType.MESH
F32 = jnp.float32
BF16 = jnp.bfloat16

HD = 128
CH = 64
STEPS = 16
ETA = 0.3
CLIP = 0.2
LOSS_SCALE = 4096.0
NORM_EPS = 1e-06
NSP = 8
NDP = 16
ROWS = 256
SEQ = 2048
HEADS = 3
FEAT = HEADS * HD
OWN = 24
LOG2E = 1.4426950408889634
STEP = 1.0 / STEPS

OFFSETS = ((2, 1), (2, 0), (1, 1), (3, 1), (1, 0), (3, 0), (0, 1))
NP = len(OFFSETS)


def nt(a, b):
    return lax.dot_general(a, b, (((1,), (1,)), ((), ())), preferred_element_type=F32)


def tn(a, b):
    return lax.dot_general(a, b, (((0,), (0,)), ((), ())), preferred_element_type=F32)


def nn(a, b):
    return jnp.dot(a, b, preferred_element_type=F32)


def kernel(
    q_hbm, k_hbm, v_hbm, lat_hbm, noise_hbm, hw_hbm, ad_ref, up_ref, adv_ref, len_ref, time_ref, dest_ref,
    next_ref, learn_ref, ratio_ref, grad_ref,
    qland, kland, vland, att, lat, noise, wt, hw, piece, wg, cs_out, cs_in, csb, hwb,
    held, r1s, r1r, r2, slots, learn_in, g_out, g_in,
    loc_sem, s0, r0, sa, ra, sc, rc, s1, r1, s2, rr2, sl, rl, s3, r3,
):
    me = lax.axis_index("sp")
    vid = lax.axis_index("dp")
    mx, my = me // 2, me % 2

    def peer(i):
        dx, dy = OFFSETS[i]
        return ((mx + dx) % 4) * 2 + (my + dy) % 2

    def source(i):
        dx, dy = OFFSETS[i]
        return ((mx + 4 - dx) % 4) * 2 + (my + 2 - dy) % 2

    def dp_peer(e):
        return (vid + e) % NDP

    def dp_source(e):
        return (vid + NDP - e) % NDP

    def rows_of(s):
        return pl.ds(pl.multiple_of(s * ROWS, ROWS), ROWS)

    def columns_of(s, h):
        return pl.ds(pl.multiple_of(s * FEAT + h * HD, HD), HD)

    barrier = pltpu.get_barrier_semaphore()
    for i in range(NP):
        pl.semaphore_signal(barrier, inc=1, device_id=(peer(i), vid), device_id_type=MESH)
    for e in range(1, NDP):
        pl.semaphore_signal(barrier, inc=1, device_id=(me, dp_peer(e)), device_id_type=MESH)

    sources = (k_hbm, q_hbm, v_hbm)

    def landing(t, h, s):
        if t == 2:
            return vland.at[h, rows_of(s), pl.ds(0, HD)]
        return (kland, qland)[t].at[h, rows_of(s), :]

    local = []
    for g in range(9):
        h, t = g // 3, g % 3
        local.append(
            pltpu.make_async_copy(sources[t].at[0, :, columns_of(me, h)], landing(t, h, me), loc_sem.at[g])
        )
    hw_copy = pltpu.make_async_copy(
        hw_hbm.at[:, pl.ds(pl.multiple_of(me * FEAT, HD), FEAT)], hw, loc_sem.at[9]
    )
    lat_copy = pltpu.make_async_copy(lat_hbm, lat, loc_sem.at[10])
    noise_copy = pltpu.make_async_copy(noise_hbm, noise, loc_sem.at[11])
    extra = [hw_copy, lat_copy, noise_copy]

    pl.semaphore_wait(barrier, NP + NDP - 1)

    order = (0, 1, 2, 3, 4, 5, 6, 8, 7)
    groups = []
    for g in order:
        h, t = g // 3, g % 3
        groups.append(
            [
                pltpu.make_async_remote_copy(
                    src_ref=sources[t].at[0, :, columns_of(peer(i), h)],
                    dst_ref=landing(t, h, me),
                    send_sem=s0.at[g, i],
                    recv_sem=r0.at[g, i],
                    device_id=(peer(i), vid),
                    device_id_type=MESH,
                )
                for i in range(NP)
            ]
        )

    def issue(n):
        for c in groups[n]:
            c.start()

    def sent(n):
        for c in groups[n]:
            c.wait_send()

    def arrived(n):
        for c in groups[n]:
            c.wait_recv()

    for n in range(3):
        issue(n)
    for c in local + extra:
        c.start()

    up = up_ref[...]
    up_low = jnp.concatenate([jnp.zeros_like(up), up], axis=0)
    piece[...] = nt(ad_ref[...], up_low)
    own_rows = pl.ds(pl.multiple_of(vid * OWN, 8), OWN)
    gather = [
        pltpu.make_async_remote_copy(
            src_ref=piece,
            dst_ref=wg.at[own_rows, :],
            send_sem=sa.at[e],
            recv_sem=ra.at[e],
            device_id=(me, dp_peer(e)),
            device_id_type=MESH,
        )
        for e in range(1, NDP)
    ]
    for c in gather:
        c.start()
    wg[own_rows, :] = piece[...]
    for h in range(HEADS):
        vland[h, :, HD:] = jnp.ones((SEQ, HD), BF16)
    ones = jnp.ones((16, FEAT), BF16)

    length = len_ref[vid]
    moment = time_ref[vid].astype(F32)
    noise_scale = jnp.full((1, ROWS), (ETA * 0.25) * (0.5 + (1.0 - moment * STEP)), F32)
    inverse = 1.0 / (2.0 * noise_scale * noise_scale)
    token = me * ROWS + lax.broadcasted_iota(jnp.int32, (1, ROWS), 1)
    live = jnp.where(token < length, 1.0, 0.0).astype(F32)
    row_weight = live / (jnp.full((1, ROWS), length.astype(F32), F32) * CH)
    gain = row_weight * inverse
    key_at = SEQ // 2 + lax.broadcasted_iota(jnp.int32, (1, SEQ // 2), 1)
    cap = jnp.where(key_at < length, 3e38, -1e30).astype(F32)

    def score(h, rows):
        return nt(qland[h, rows, :], kland[h]) * (LOG2E * HD**-0.5)

    def attend(h, rows, scores):
        first = scores[:, : SEQ // 2]
        second = jnp.minimum(scores[:, SEQ // 2 :], cap)
        highest = jnp.maximum(
            jnp.max(first, axis=1, keepdims=True), jnp.max(second, axis=1, keepdims=True)
        )
        low = jnp.exp2(first - highest).astype(BF16)
        high = jnp.exp2(second - highest).astype(BF16)
        mixed = nn(jnp.concatenate([low, high], axis=1), vland[h])
        att[rows, h * HD : (h + 1) * HD] = (mixed[:, :HD] / mixed[:, HD:]).astype(BF16)

    def attend_all(h):
        held[0] = score(h, rows_of(0))

        @pl.loop(0, NSP // 2)
        def _(pair):
            for half in range(2):
                b = 2 * pair + half
                held[1 - half] = score(h, rows_of((b + 1) % NSP))
                attend(h, rows_of(b), held[half])

    for c in local + [lat_copy, noise_copy, hw_copy]:
        c.wait()
    for n in range(3):
        sent(n)
        issue(n + 3)
    for n in range(3):
        arrived(n)
    attend_all(0)

    for c in gather:
        c.wait()
    wt[0:CH, :] = hw[...]
    wt[CH:, :] = jnp.transpose(wg[...])[CH:, :].astype(BF16)
    cs_out[...] = nt(ones, wt[...])[0:8]
    cs_copies = [
        pltpu.make_async_remote_copy(
            src_ref=cs_out,
            dst_ref=cs_in.at[i],
            send_sem=sc.at[i],
            recv_sem=rc.at[i],
            device_id=(peer(i), vid),
            device_id_type=MESH,
        )
        for i in range(NP)
    ]
    for c in cs_copies:
        c.start()
    cs_in[NP] = cs_out[...]
    for n in range(3, 6):
        sent(n)
        issue(n + 3)
    for n in range(3, 6):
        arrived(n)
    attend_all(1)

    for c in cs_copies:
        c.wait()
    for i in range(NP + 1):
        spread = jnp.transpose(jnp.broadcast_to(cs_in[i][0:1], (HD, HD)))
        csb[i] = spread[CH:]
        if i == NP:
            hwb[...] = spread[:CH]

    for n in (6, 7):
        arrived(n)

    def partial_sums(rows):
        feature = att[rows, :]
        wide = feature.astype(F32)
        centred = wide - jnp.sum(wide, axis=1, keepdims=True) * (1.0 / FEAT)
        sums = nt(wt[...], centred.astype(BF16))
        mean = nt(ones, feature) * (1.0 / FEAT)
        square = nt(ones, (centred * centred).astype(BF16))
        spread = jnp.concatenate([hwb[...], hwb[...]], axis=1)
        velocity = sums[:CH] + spread * mean[0:1]
        line = lax.broadcasted_iota(jnp.int32, (16, ROWS), 0)
        mean_high = mean.astype(BF16).astype(F32)
        square_high = square.astype(BF16).astype(F32)
        stats = jnp.where(
            line == 0,
            mean_high,
            jnp.where(line == 1, mean - mean_high, jnp.where(line == 2, square_high, square - square_high)),
        )
        return jnp.concatenate([velocity, sums[CH:], stats], axis=0).astype(BF16)

    part_copies = [
        pltpu.make_async_remote_copy(
            src_ref=r1s.at[i],
            dst_ref=r1r.at[i],
            send_sem=s1.at[i],
            recv_sem=r1.at[i],
            device_id=(peer(i), vid),
            device_id_type=MESH,
        )
        for i in range(NP)
    ]
    opposite = [OFFSETS.index(((4 - dx) % 4, (2 - dy) % 2)) for dx, dy in OFFSETS]
    turn = [rows_of(me)] + [rows_of(peer(i)) for i in range(NP)]
    held[0] = score(2, turn[0])
    for n in range(NSP + 1):
        if n < NP:
            groups[8][opposite[n]].wait_recv()
        if n + 1 < NSP:
            held[(n + 1) % 2] = score(2, turn[n + 1])
        if n < NSP:
            attend(2, turn[n], held[n % 2])
        if n == 1:
            r1r[NP] = partial_sums(turn[0])
        if n > 1:
            r1s[n - 2] = partial_sums(turn[n - 1])
            part_copies[n - 2].start()
    for n in (6, 7, 8):
        sent(n)
    for c in part_copies:
        c.wait()

    parts = [r1r[i].astype(F32) for i in range(NP + 1)]
    total = parts[0][: 2 * CH]
    for p in parts[1:]:
        total = total + p[: 2 * CH]
    means = [p[128:129] + p[129:130] for p in parts]
    squares = [p[130:131] + p[131:132] for p in parts]
    mean = functools.reduce(jnp.add, means) * (1.0 / NSP)
    gaps = [m - mean for m in means]
    variance = functools.reduce(jnp.add, squares) + FEAT * functools.reduce(jnp.add, [g * g for g in gaps])
    rstd = lax.rsqrt(variance * (1.0 / (FEAT * NSP)) + NORM_EPS)
    inner = total[CH:]
    for i in range(NP + 1):
        inner = inner + jnp.concatenate([csb[i], csb[i]], axis=1) * gaps[i]
    delta = inner * rstd
    offset = noise_scale * noise[...]
    gap = offset - STEP * delta
    unit = (gap * (gain * (2.0 * STEP) * rstd)).astype(BF16)
    terms = gain * jnp.sum(offset * offset - gap * gap, axis=0, keepdims=True)
    line = lax.broadcasted_iota(jnp.int32, (16, ROWS), 0)
    mean_high = mean.astype(BF16).astype(F32)
    terms_high = terms.astype(BF16).astype(F32)
    terms_rest = terms - terms_high
    terms_mid = terms_rest.astype(BF16).astype(F32)
    side = jnp.where(line == 0, mean_high, jnp.where(line == 1, mean - mean_high, 0.0))
    side = jnp.where(line == 2, terms_high, side)
    side = jnp.where(line == 3, terms_mid, jnp.where(line == 4, terms_rest - terms_mid, side))
    r2[me, 0:CH] = unit
    r2[me, CH : CH + 16] = side.astype(BF16)
    unit_copies = [
        pltpu.make_async_remote_copy(
            src_ref=r2.at[me],
            dst_ref=r2.at[me],
            send_sem=s2.at[i],
            recv_sem=rr2.at[i],
            device_id=(peer(i), vid),
            device_id_type=MESH,
        )
        for i in range(NP)
    ]
    for c in unit_copies:
        c.start()

    lane = lax.broadcasted_iota(jnp.int32, (1, ROWS), 1)
    targets = [dest_ref[0, b] for b in range(16)]
    place = jnp.zeros((1, ROWS), jnp.int32)
    for b in range(16):
        rank = jnp.int32(0)
        for a in range(b):
            rank = rank + jnp.where(targets[a] == targets[b], 1, 0)
        place = jnp.where(lane // 16 == b, targets[b] * 2 + rank, place)
    place = place * 16 + lane % 16
    placing = (lax.broadcasted_iota(jnp.int32, (512, ROWS), 0) == place).astype(F32).astype(BF16)
    delta_low = delta.astype(BF16)
    slots[...] = nt(placing, jnp.concatenate([delta_low, jnp.zeros_like(delta_low)], axis=0)).astype(BF16)
    mine = pl.ds(pl.multiple_of(vid * 32, 32), 32)
    learn_copies = [
        pltpu.make_async_remote_copy(
            src_ref=slots.at[pl.ds(pl.multiple_of(dp_peer(e) * 32, 32), 32), :],
            dst_ref=learn_in.at[mine, :],
            send_sem=sl.at[e],
            recv_sem=rl.at[e],
            device_id=(me, dp_peer(e)),
            device_id_type=MESH,
        )
        for e in range(1, NDP)
    ]
    for c in learn_copies:
        c.start()
    learn_in[mine, :] = slots[mine, :]
    next_ref[...] = (lat[...] - STEP * total[:CH]) + offset

    def grad_part(s):
        u = r2[s, 0:CH]
        side = r2[s, CH : CH + 16]
        shift = nt(u, side)
        return nn(u, att[rows_of(s), :]) - (shift[:, 0:1] + shift[:, 1:2])

    grad = grad_part(me)
    for i in range(NP):
        unit_copies[i].wait_recv()
        grad = grad + grad_part(source(i))
    sides = r2[0, CH : CH + 16].astype(F32)
    for s in range(1, NSP):
        sides = sides + r2[s, CH : CH + 16].astype(F32)
    log_gain = jnp.sum(sides[2:3] + sides[3:4] + sides[4:5], axis=1, keepdims=True)
    log_gain = jnp.broadcast_to(log_gain, (8, HD))
    ratio = jnp.exp(log_gain)
    advantage = adv_ref[vid]
    clipped = jnp.clip(ratio, 1.0 - CLIP, 1.0 + CLIP)
    active = jnp.where(ratio * advantage <= clipped * advantage, 1.0, 0.0)
    pull = -(LOSS_SCALE / NDP) * advantage * ratio * active
    grad_high = grad.astype(BF16)
    grad_rest = (grad - grad_high.astype(F32)).astype(BF16)
    product = tn(jnp.concatenate([grad_high, grad_rest], axis=0), jnp.concatenate([up, up], axis=0))
    product = product * pull[0:1]
    high = log_gain.astype(BF16).astype(F32)
    middle = (log_gain - high).astype(BF16).astype(F32)
    line = lax.broadcasted_iota(jnp.int32, (8, HD), 0)
    gain_rows = jnp.where(line == 0, high, jnp.where(line == 1, middle, jnp.where(line == 2, log_gain - high - middle, 0.0)))
    for k in range(NDP):
        g_out[k] = jnp.concatenate([product[k * OWN : (k + 1) * OWN], gain_rows], axis=0).astype(BF16)
    grad_copies = [
        pltpu.make_async_remote_copy(
            src_ref=g_out.at[dp_peer(e)],
            dst_ref=g_in.at[vid],
            send_sem=s3.at[e],
            recv_sem=r3.at[e],
            device_id=(me, dp_peer(e)),
            device_id_type=MESH,
        )
        for e in range(1, NDP)
    ]
    for c in grad_copies:
        c.start()
    g_in[vid] = g_out[vid]

    for c in learn_copies:
        c.wait()
    select = lax.broadcasted_iota(jnp.int32, (CH, HD), 0) == lax.broadcasted_iota(jnp.int32, (CH, HD), 1)
    learn_ref[...] = nt(select.astype(F32).astype(BF16), learn_in[...])
    for c in unit_copies:
        c.wait_send()

    for c in grad_copies:
        c.wait()
    summed = g_in[0].astype(F32)
    column = lax.broadcasted_iota(jnp.int32, (8, HD), 1)
    gains = jnp.where(column == 0, summed[OWN:], 0.0)
    for k in range(1, NDP):
        block = g_in[k].astype(F32)
        summed = summed + block
        gains = jnp.where(column == k, block[OWN:], gains)
    grad_ref[...] = summed[:OWN]
    ratio_ref[...] = jnp.exp(jnp.broadcast_to(gains[0:1] + gains[1:2] + gains[2:3], (8, HD)))


def hand_over(next_in, learn_in, ratio_in, grad_in, next_out, learn_out, ratio_out, grad_out, sem):
    copies = [
        pltpu.make_async_copy(next_in, next_out, sem.at[0]),
        pltpu.make_async_copy(learn_in, learn_out, sem.at[1]),
        pltpu.make_async_copy(grad_in, grad_out, sem.at[2]),
    ]
    for c in copies:
        c.start()
    ratio_out[...] = ratio_in[0, :NDP]
    for c in copies:
        c.wait()


def on_device(
    queries, keys, values, latents, noise, head_weight, adapter_down, adapter_up, advantages, lengths, timesteps,
    destinations,
):
    hbm = pl.BlockSpec(memory_space=pl.ANY)
    vmem = pl.BlockSpec(memory_space=pltpu.VMEM)
    smem = pl.BlockSpec(memory_space=pltpu.SMEM)
    dma = pltpu.SemaphoreType.DMA
    nxt, learn, ratio, grad = pl.pallas_call(
        kernel,
        out_shape=(
            jax.ShapeDtypeStruct((CH, ROWS), F32),
            jax.ShapeDtypeStruct((CH, 512), F32),
            jax.ShapeDtypeStruct((8, HD), F32),
            jax.ShapeDtypeStruct((OWN, HD), F32),
        ),
        in_specs=[hbm] * 6 + [vmem] * 2 + [smem] * 4,
        out_specs=(vmem,) * 4,
        scratch_shapes=[
            pltpu.VMEM((HEADS, SEQ, HD), BF16),
            pltpu.VMEM((HEADS, SEQ, HD), BF16),
            pltpu.VMEM((HEADS, SEQ, 2 * HD), BF16),
            pltpu.VMEM((SEQ, FEAT), BF16),
            pltpu.VMEM((CH, ROWS), F32),
            pltpu.VMEM((CH, ROWS), F32),
            pltpu.VMEM((2 * CH, FEAT), BF16),
            pltpu.VMEM((CH, FEAT), BF16),
            pltpu.VMEM((OWN, HD), F32),
            pltpu.VMEM((FEAT, HD), F32),
            pltpu.VMEM((8, HD), F32),
            pltpu.VMEM((NSP, 8, HD), F32),
            pltpu.VMEM((NSP, CH, HD), F32),
            pltpu.VMEM((CH, HD), F32),
            pltpu.VMEM((2, ROWS, SEQ), F32),
            pltpu.VMEM((NP, 144, ROWS), BF16),
            pltpu.VMEM((NSP, 144, ROWS), BF16),
            pltpu.VMEM((NSP, CH + 16, ROWS), BF16),
            pltpu.VMEM((512, HD), BF16),
            pltpu.VMEM((512, HD), BF16),
            pltpu.VMEM((NDP, OWN + 8, HD), BF16),
            pltpu.VMEM((NDP, OWN + 8, HD), BF16),
            dma((12,)),
            dma((9, NP)), dma((9, NP)),
            dma((NDP,)), dma((NDP,)),
            dma((NP,)), dma((NP,)),
            dma((NP,)), dma((NP,)),
            dma((NP,)), dma((NP,)),
            dma((NDP,)), dma((NDP,)),
            dma((NDP,)), dma((NDP,)),
        ],
        compiler_params=pltpu.CompilerParams(
            collective_id=0, has_side_effects=True, vmem_limit_bytes=60 * 2**20
        ),
        cost_estimate=pl.CostEstimate(
            flops=7 * 10**9, bytes_accessed=6 * 10**6, transcendentals=13 * 10**6
        ),
        name="policy_step",
    )(
        queries, keys, values, latents[0].T, noise[0].T, head_weight.T, adapter_down, adapter_up.T, advantages,
        lengths, timesteps, destinations.reshape(1, 16),
    )
    nxt, learn, ratio, grad = pl.pallas_call(
        hand_over,
        out_shape=(
            jax.ShapeDtypeStruct((CH, ROWS), F32),
            jax.ShapeDtypeStruct((CH, 512), F32),
            jax.ShapeDtypeStruct((NDP,), F32),
            jax.ShapeDtypeStruct((OWN, HD), F32),
        ),
        in_specs=[hbm, hbm, vmem, hbm],
        out_specs=(hbm, hbm, vmem, hbm),
        scratch_shapes=[dma((3,))],
        name="hand_over",
    )(nxt, learn, ratio, grad)
    return nxt.T[None], learn.T[None, None], ratio, grad


def solution(mesh):
    wide = P("dp", "sp", None)
    in_specs = (
        wide, wide, wide, wide, wide, P(), P(("sp", "dp"), None), P(), P(), P(), P(), P("dp", "sp", None, None),
    )
    out_specs = (wide, P("dp", "sp", None, None), P(), P(("sp", "dp"), None))
    return jax.shard_map(on_device, mesh=mesh, in_specs=in_specs, out_specs=out_specs, check_vma=False)
```

```python
import functools

import jax
import jax.numpy as jnp
from jax import lax
from jax.experimental import pallas as pl
from jax.experimental.pallas import tpu as pltpu
from jax.sharding import PartitionSpec as P

MESH = pl.DeviceIdType.MESH
F32 = jnp.float32
BF16 = jnp.bfloat16

HD = 128
CH = 64
STEPS = 16
ETA = 0.3
CLIP = 0.2
LOSS_SCALE = 4096.0
NORM_EPS = 1e-06
NSP = 8
NDP = 16
ROWS = 256
SEQ = 2048
HEADS = 3
FEAT = HEADS * HD
OWN = 24
LOG2E = 1.4426950408889634
STEP = 1.0 / STEPS

OFFSETS = ((2, 1), (2, 0), (1, 1), (3, 1), (1, 0), (3, 0), (0, 1))
NP = len(OFFSETS)


def nt(a, b):
    return lax.dot_general(a, b, (((1,), (1,)), ((), ())), preferred_element_type=F32)


def tn(a, b):
    return lax.dot_general(a, b, (((0,), (0,)), ((), ())), preferred_element_type=F32)


def nn(a, b):
    return jnp.dot(a, b, preferred_element_type=F32)


def kernel(
    q_hbm, k_hbm, v_hbm, lat_hbm, noise_hbm, hw_hbm, ad_ref, up_hbm, adv_hbm, len_hbm, time_hbm, dest_hbm,
    next_hbm, learn_hbm, ratio_hbm, grad_hbm,
    qland, kland, vland, att, prob, held, lat, noise, hw, up_ref, adv_ref, len_ref, time_ref, dest_ref,
    next_ref, learn_ref, ratio_ref, grad_ref,
    weight, early, stat, piece, wg, cs_out, cs_in, csb, offs, placing,
    r1s, r1r, r2, slots, learn_in, g_out, g_in,
    loc_sem, s0, r0, sa, ra, sc, rc, s1, r1, s2, rr2, sl, rl, s3, r3,
):
    me = lax.axis_index("sp")
    vid = lax.axis_index("dp")
    mx, my = me // 2, me % 2

    def peer(i):
        dx, dy = OFFSETS[i]
        return ((mx + dx) % 4) * 2 + (my + dy) % 2

    def source(i):
        dx, dy = OFFSETS[i]
        return ((mx + 4 - dx) % 4) * 2 + (my + 2 - dy) % 2

    def dp_peer(e):
        return (vid + e) % NDP

    def dp_source(e):
        return (vid + NDP - e) % NDP

    def rows_of(s):
        return pl.ds(pl.multiple_of(s * ROWS, ROWS), ROWS)

    def columns_of(s, h):
        return pl.ds(pl.multiple_of(s * FEAT + h * HD, HD), HD)

    barrier = pltpu.get_barrier_semaphore()
    for i in range(NP):
        pl.semaphore_signal(barrier, inc=1, device_id=(peer(i), vid), device_id_type=MESH)
    for e in range(1, NDP):
        pl.semaphore_signal(barrier, inc=1, device_id=(me, dp_peer(e)), device_id_type=MESH)

    sources = (k_hbm, q_hbm, v_hbm)

    def landing(t, h, s):
        if t == 2:
            return vland.at[h, rows_of(s), pl.ds(0, HD)]
        return (kland, qland)[t].at[h, rows_of(s), :]

    local = []
    for g in range(9):
        h, t = g // 3, g % 3
        local.append(
            pltpu.make_async_copy(sources[t].at[0, :, columns_of(me, h)], landing(t, h, me), loc_sem.at[g])
        )
    hw_copy = pltpu.make_async_copy(
        hw_hbm.at[:, pl.ds(pl.multiple_of(me * FEAT, HD), FEAT)], hw, loc_sem.at[9]
    )
    small = [
        pltpu.make_async_copy(src, dst, loc_sem.at[10 + n])
        for n, (src, dst) in enumerate(
            (
                (up_hbm, up_ref),
                (lat_hbm, lat),
                (noise_hbm, noise),
                (adv_hbm, adv_ref),
                (len_hbm, len_ref),
                (time_hbm, time_ref),
                (dest_hbm, dest_ref),
            )
        )
    ]
    for c in small + [hw_copy]:
        c.start()

    pl.semaphore_wait(barrier, NP + NDP - 1)

    order = (0, 1, 2, 3, 4, 5, 7, 6, 8)
    groups = []
    for g in order:
        h, t = g // 3, g % 3
        groups.append(
            [
                pltpu.make_async_remote_copy(
                    src_ref=sources[t].at[0, :, columns_of(peer(i), h)],
                    dst_ref=landing(t, h, me),
                    send_sem=s0.at[g, i],
                    recv_sem=r0.at[g, i],
                    device_id=(peer(i), vid),
                    device_id_type=MESH,
                )
                for i in range(NP)
            ]
        )

    def issue(n):
        for c in groups[n]:
            c.start()

    def sent(n):
        for c in groups[n]:
            c.wait_send()

    def arrived(n):
        for c in groups[n]:
            c.wait_recv()

    for n in range(3):
        issue(n)
    for c in local:
        c.start()
    for c in small:
        c.wait()

    up = up_ref[...]
    up_low = jnp.concatenate([jnp.zeros_like(up), up], axis=0)
    piece[...] = nt(ad_ref[...], up_low)
    own_rows = pl.ds(pl.multiple_of(vid * OWN, 8), OWN)
    gather = [
        pltpu.make_async_remote_copy(
            src_ref=piece,
            dst_ref=wg.at[own_rows, :],
            send_sem=sa.at[e],
            recv_sem=ra.at[e],
            device_id=(me, dp_peer(e)),
            device_id_type=MESH,
        )
        for e in range(1, NDP)
    ]
    for c in gather:
        c.start()
    wg[own_rows, :] = piece[...]
    for h in range(HEADS):
        vland[h, :, HD:] = jnp.ones((SEQ, HD), BF16)

    length = len_ref[vid]
    moment = time_ref[vid].astype(F32)
    noise_scale = jnp.full((1, ROWS), (ETA * 0.25) * (0.5 + (1.0 - moment * STEP)), F32)
    inverse = 1.0 / (2.0 * noise_scale * noise_scale)
    token = me * ROWS + lax.broadcasted_iota(jnp.int32, (1, ROWS), 1)
    live = jnp.where(token < length, 1.0, 0.0).astype(F32)
    row_weight = live / (jnp.full((1, ROWS), length.astype(F32), F32) * CH)
    gain = row_weight * inverse
    offs[...] = noise_scale * noise[...]
    lane = lax.broadcasted_iota(jnp.int32, (1, ROWS), 1)
    targets = [dest_ref[0, b] for b in range(16)]
    place = jnp.zeros((1, ROWS), jnp.int32)
    for b in range(16):
        rank = jnp.int32(0)
        for a in range(b):
            rank = rank + jnp.where(targets[a] == targets[b], 1, 0)
        place = jnp.where(lane // 16 == b, targets[b] * 2 + rank, place)
    place = place * 16 + lane % 16
    placing[...] = (lax.broadcasted_iota(jnp.int32, (512, ROWS), 0) == place).astype(F32).astype(BF16)
    key_at = SEQ // 2 + lax.broadcasted_iota(jnp.int32, (1, SEQ // 2), 1)
    cap = jnp.where(key_at < length, 3e38, -1e30).astype(F32)

    def score(h, rows):
        return nt(qland[h, rows, :], kland[h]) * (LOG2E * HD**-0.5)

    def soften(scores):
        first = scores[:, : SEQ // 2]
        second = jnp.minimum(scores[:, SEQ // 2 :], cap)
        highest = jnp.maximum(
            jnp.max(first, axis=1, keepdims=True), jnp.max(second, axis=1, keepdims=True)
        )
        low = jnp.exp2(first - highest).astype(BF16)
        high = jnp.exp2(second - highest).astype(BF16)
        return jnp.concatenate([low, high], axis=1)

    def finish(h, rows, mixed):
        feature = (mixed[:, :HD] / mixed[:, HD:]).astype(BF16)
        att[rows, h * HD : (h + 1) * HD] = feature
        return feature

    def moments(feature):
        wide = feature.astype(F32)
        average = jnp.sum(wide, axis=1, keepdims=True) * (1.0 / feature.shape[1])
        centred = wide - average
        return average, jnp.sum(centred * centred, axis=1, keepdims=True)

    stat_lane = lax.broadcasted_iota(jnp.int32, (ROWS, HD), 1)

    def block(h, rows, scores):
        chances = soften(scores)
        if h == 2:
            prob[rows, :] = chances
            return
        finish(h, rows, nn(chances, vland[h]))
        if h == 1:
            feature = att[rows, 0 : 2 * HD]
            early[rows, :] = nn(feature, weight[0 : 2 * HD, :])
            average, square = moments(feature)
            stat[rows, :] = jnp.where(stat_lane == 0, average, jnp.where(stat_lane == 1, square, 0.0))

    def attend_all(h):
        held[0] = score(h, rows_of(0))

        @pl.loop(0, NSP // 2)
        def _(pair):
            for half in range(2):
                b = 2 * pair + half
                held[1 - half] = score(h, rows_of((b + 1) % NSP))
                block(h, rows_of(b), held[half])

    for c in local + [hw_copy]:
        c.wait()
    for n in range(3):
        sent(n)
        issue(n + 3)
    for n in range(3):
        arrived(n)
    attend_all(0)

    for c in gather:
        c.wait()
    wide_head = jnp.concatenate([hw[...].astype(F32), jnp.zeros((CH, FEAT), F32)], axis=0)
    weight[...] = (jnp.transpose(wide_head) + wg[...]).astype(BF16)
    cs_out[...] = nn(jnp.ones((16, FEAT), BF16), weight[...])[0:8]
    cs_copies = [
        pltpu.make_async_remote_copy(
            src_ref=cs_out,
            dst_ref=cs_in.at[i],
            send_sem=sc.at[i],
            recv_sem=rc.at[i],
            device_id=(peer(i), vid),
            device_id_type=MESH,
        )
        for i in range(NP)
    ]
    for c in cs_copies:
        c.start()
    cs_in[NP] = cs_out[...]
    for n in range(3, 6):
        sent(n)
        issue(n + 3)
    for n in range(3, 6):
        arrived(n)
    attend_all(1)

    for c in cs_copies:
        c.wait()
    for i in range(NP + 1):
        spread = jnp.transpose(jnp.broadcast_to(cs_in[i][0:1], (HD, HD)))
        csb[i] = jnp.concatenate([spread[CH:], spread[CH:]], axis=1)

    for n in (6, 7):
        arrived(n)
    attend_all(2)
    arrived(8)

    def partial_sums(rows, mixed):
        feature = finish(2, rows, mixed)
        sums = early[rows, :] + nn(feature, weight[2 * HD :, :])
        average, square = moments(feature)
        columns = stat[rows, :] + jnp.where(stat_lane == 2, average, jnp.where(stat_lane == 3, square, 0.0))
        lines = jnp.transpose(columns)
        apart = lines[0:1] - lines[2:3]
        mean = lines[0:1] - apart * (1.0 / 3.0)
        square = lines[1:2] + lines[3:4] + apart * apart * (2.0 * HD / 3.0)
        sums = jnp.transpose(sums)
        line = lax.broadcasted_iota(jnp.int32, (16, ROWS), 0)
        mean_high = mean.astype(BF16).astype(F32)
        square_high = square.astype(BF16).astype(F32)
        stats = jnp.where(line == 0, mean_high, jnp.where(line == 1, mean - mean_high, 0.0))
        stats = jnp.where(line == 2, square_high, jnp.where(line == 3, square - square_high, stats))
        return jnp.concatenate([sums[:CH], sums[CH:] - csb[NP] * mean, stats], axis=0).astype(BF16)

    part_copies = [
        pltpu.make_async_remote_copy(
            src_ref=r1s.at[i],
            dst_ref=r1r.at[i],
            send_sem=s1.at[i],
            recv_sem=r1.at[i],
            device_id=(peer(i), vid),
            device_id_type=MESH,
        )
        for i in range(NP)
    ]
    turn = [rows_of(peer(i)) for i in range(NP)] + [rows_of(me)]
    mixed = nn(prob[turn[0], :], vland[2])
    for n in range(NSP):
        if n < NP:
            following = nn(prob[turn[n + 1], :], vland[2])
            r1s[n] = partial_sums(turn[n], mixed)
            part_copies[n].start()
            mixed = following
        else:
            r1r[NP] = partial_sums(turn[n], mixed)
    for n in (6, 7, 8):
        sent(n)
    for c in part_copies:
        c.wait()

    parts = [r1r[i].astype(F32) for i in range(NP + 1)]
    total = functools.reduce(jnp.add, [p[: 2 * CH] for p in parts])
    means = [p[128:129] + p[129:130] for p in parts]
    squares = [p[130:131] + p[131:132] for p in parts]
    mean = functools.reduce(jnp.add, means) * (1.0 / NSP)
    gaps = [m - mean for m in means]
    variance = functools.reduce(jnp.add, squares) + FEAT * functools.reduce(jnp.add, [g * g for g in gaps])
    rstd = lax.rsqrt(variance * (1.0 / (FEAT * NSP)) + NORM_EPS)
    inner = total[CH:]
    for i in range(NP + 1):
        inner = inner + csb[i] * gaps[i]
    delta = inner * rstd
    offset = offs[...]
    gap = offset - STEP * delta
    unit = (gap * (gain * (2.0 * STEP) * rstd)).astype(BF16)
    terms = gain * jnp.sum(offset * offset - gap * gap, axis=0, keepdims=True)
    line = lax.broadcasted_iota(jnp.int32, (16, ROWS), 0)
    mean_high = mean.astype(BF16).astype(F32)
    terms_high = terms.astype(BF16).astype(F32)
    terms_rest = terms - terms_high
    terms_mid = terms_rest.astype(BF16).astype(F32)
    side = jnp.where(line == 0, mean_high, jnp.where(line == 1, mean - mean_high, 0.0))
    side = jnp.where(line == 2, terms_high, side)
    side = jnp.where(line == 3, terms_mid, jnp.where(line == 4, terms_rest - terms_mid, side))
    r2[me, 0:CH] = unit
    r2[me, CH : CH + 16] = side.astype(BF16)
    unit_copies = [
        pltpu.make_async_remote_copy(
            src_ref=r2.at[me],
            dst_ref=r2.at[me],
            send_sem=s2.at[i],
            recv_sem=rr2.at[i],
            device_id=(peer(i), vid),
            device_id_type=MESH,
        )
        for i in range(NP)
    ]
    for c in unit_copies:
        c.start()

    delta_low = delta.astype(BF16)
    slots[...] = nt(placing[...], jnp.concatenate([delta_low, jnp.zeros_like(delta_low)], axis=0)).astype(BF16)
    mine = pl.ds(pl.multiple_of(vid * 32, 32), 32)
    learn_copies = [
        pltpu.make_async_remote_copy(
            src_ref=slots.at[pl.ds(pl.multiple_of(dp_peer(e) * 32, 32), 32), :],
            dst_ref=learn_in.at[mine, :],
            send_sem=sl.at[e],
            recv_sem=rl.at[e],
            device_id=(me, dp_peer(e)),
            device_id_type=MESH,
        )
        for e in range(1, NDP)
    ]
    for c in learn_copies:
        c.start()
    learn_in[mine, :] = slots[mine, :]
    next_ref[...] = (lat[...] - STEP * total[:CH]) + offset
    outward = [
        pltpu.make_async_copy(src, dst, loc_sem.at[18 + n])
        for n, (src, dst) in enumerate(
            ((next_ref, next_hbm), (learn_ref, learn_hbm), (ratio_ref, ratio_hbm), (grad_ref, grad_hbm))
        )
    ]
    outward[0].start()

    def grad_part(s):
        u = r2[s, 0:CH]
        side = r2[s, CH : CH + 16]
        shift = nt(u, side)
        return nn(u, att[rows_of(s), :]) - (shift[:, 0:1] + shift[:, 1:2])

    grad = grad_part(me)
    for i in range(NP):
        unit_copies[i].wait_recv()
        grad = grad + grad_part(source(i))
    sides = r2[0, CH : CH + 16].astype(F32)
    for s in range(1, NSP):
        sides = sides + r2[s, CH : CH + 16].astype(F32)
    log_gain = jnp.sum(sides[2:3] + sides[3:4] + sides[4:5], axis=1, keepdims=True)
    log_gain = jnp.broadcast_to(log_gain, (8, HD))
    ratio = jnp.exp(log_gain)
    advantage = adv_ref[vid]
    clipped = jnp.clip(ratio, 1.0 - CLIP, 1.0 + CLIP)
    active = jnp.where(ratio * advantage <= clipped * advantage, 1.0, 0.0)
    pull = -(LOSS_SCALE / NDP) * advantage * ratio * active
    grad_high = grad.astype(BF16)
    grad_rest = (grad - grad_high.astype(F32)).astype(BF16)
    product = tn(jnp.concatenate([grad_high, grad_rest], axis=0), jnp.concatenate([up, up], axis=0))
    product = product * pull[0:1]
    high = log_gain.astype(BF16).astype(F32)
    middle = (log_gain - high).astype(BF16).astype(F32)
    line = lax.broadcasted_iota(jnp.int32, (8, HD), 0)
    gain_rows = jnp.where(line == 0, high, jnp.where(line == 1, middle, jnp.where(line == 2, log_gain - high - middle, 0.0)))
    for k in range(NDP):
        g_out[k] = jnp.concatenate([product[k * OWN : (k + 1) * OWN], gain_rows], axis=0).astype(BF16)
    grad_copies = [
        pltpu.make_async_remote_copy(
            src_ref=g_out.at[dp_peer(e)],
            dst_ref=g_in.at[vid],
            send_sem=s3.at[e],
            recv_sem=r3.at[e],
            device_id=(me, dp_peer(e)),
            device_id_type=MESH,
        )
        for e in range(1, NDP)
    ]
    for c in grad_copies:
        c.start()
    g_in[vid] = g_out[vid]

    for c in learn_copies:
        c.wait()
    select = lax.broadcasted_iota(jnp.int32, (CH, HD), 0) == lax.broadcasted_iota(jnp.int32, (CH, HD), 1)
    learn_ref[...] = nt(select.astype(F32).astype(BF16), learn_in[...])
    outward[1].start()
    for c in unit_copies:
        c.wait_send()

    for c in grad_copies:
        c.wait()
    summed = g_in[0].astype(F32)
    column = lax.broadcasted_iota(jnp.int32, (8, HD), 1)
    gains = jnp.where(column == 0, summed[OWN:], 0.0)
    for k in range(1, NDP):
        block = g_in[k].astype(F32)
        summed = summed + block
        gains = jnp.where(column == k, block[OWN:], gains)
    grad_ref[...] = summed[:OWN]
    outward[3].start()
    ratio_ref[...] = jnp.exp(jnp.broadcast_to(gains[0:1] + gains[1:2] + gains[2:3], (8, HD)))
    outward[2].start()
    for c in outward:
        c.wait()


def hand_over(next_in, learn_in, ratio_in, grad_in, next_out, learn_out, ratio_out, grad_out):
    next_out[...] = next_in[...]
    learn_out[...] = learn_in[...]
    grad_out[...] = grad_in[...]
    ratio_out[...] = ratio_in[0, :NDP]


def on_device(
    queries, keys, values, latents, noise, head_weight, adapter_down, adapter_up, advantages, lengths, timesteps,
    destinations,
):
    hbm = pl.BlockSpec(memory_space=pl.ANY)
    vmem = pl.BlockSpec(memory_space=pltpu.VMEM)
    dma = pltpu.SemaphoreType.DMA
    nxt, learn, ratio, grad = pl.pallas_call(
        kernel,
        out_shape=(
            jax.ShapeDtypeStruct((CH, ROWS), F32),
            jax.ShapeDtypeStruct((CH, 512), F32),
            jax.ShapeDtypeStruct((8, HD), F32),
            jax.ShapeDtypeStruct((OWN, HD), F32),
        ),
        in_specs=[hbm] * 6 + [vmem] + [hbm] * 5,
        out_specs=(hbm,) * 4,
        scratch_shapes=[
            pltpu.VMEM((HEADS, SEQ, HD), BF16),
            pltpu.VMEM((HEADS, SEQ, HD), BF16),
            pltpu.VMEM((HEADS, SEQ, 2 * HD), BF16),
            pltpu.VMEM((SEQ, FEAT), BF16),
            pltpu.VMEM((SEQ, SEQ), BF16),
            pltpu.VMEM((2, ROWS, SEQ), F32),
            pltpu.VMEM((CH, ROWS), F32),
            pltpu.VMEM((CH, ROWS), F32),
            pltpu.VMEM((CH, FEAT), BF16),
            pltpu.VMEM((CH, HD), BF16),
            pltpu.SMEM((NDP,), F32),
            pltpu.SMEM((NDP,), jnp.int32),
            pltpu.SMEM((NDP,), jnp.int32),
            pltpu.SMEM((1, 16), jnp.int32),
            pltpu.VMEM((CH, ROWS), F32),
            pltpu.VMEM((CH, 512), F32),
            pltpu.VMEM((8, HD), F32),
            pltpu.VMEM((OWN, HD), F32),
            pltpu.VMEM((FEAT, HD), BF16),
            pltpu.VMEM((SEQ, HD), F32),
            pltpu.VMEM((SEQ, HD), F32),
            pltpu.VMEM((OWN, HD), F32),
            pltpu.VMEM((FEAT, HD), F32),
            pltpu.VMEM((8, HD), F32),
            pltpu.VMEM((NSP, 8, HD), F32),
            pltpu.VMEM((NSP, CH, ROWS), F32),
            pltpu.VMEM((CH, ROWS), F32),
            pltpu.VMEM((512, ROWS), BF16),
            pltpu.VMEM((NP, 144, ROWS), BF16),
            pltpu.VMEM((NSP, 144, ROWS), BF16),
            pltpu.VMEM((NSP, CH + 16, ROWS), BF16),
            pltpu.VMEM((512, HD), BF16),
            pltpu.VMEM((512, HD), BF16),
            pltpu.VMEM((NDP, OWN + 8, HD), BF16),
            pltpu.VMEM((NDP, OWN + 8, HD), BF16),
            dma((22,)),
            dma((9, NP)), dma((9, NP)),
            dma((NDP,)), dma((NDP,)),
            dma((NP,)), dma((NP,)),
            dma((NP,)), dma((NP,)),
            dma((NP,)), dma((NP,)),
            dma((NDP,)), dma((NDP,)),
            dma((NDP,)), dma((NDP,)),
        ],
        compiler_params=pltpu.CompilerParams(
            collective_id=0, has_side_effects=True, vmem_limit_bytes=60 * 2**20
        ),
        cost_estimate=pl.CostEstimate(
            flops=7 * 10**9, bytes_accessed=6 * 10**6, transcendentals=13 * 10**6
        ),
        name="policy_step",
    )(
        queries, keys, values, latents[0].T, noise[0].T, head_weight.T, adapter_down, adapter_up.T, advantages,
        lengths, timesteps, destinations.reshape(1, 16),
    )
    nxt, learn, ratio, grad = pl.pallas_call(
        hand_over,
        out_shape=(
            jax.ShapeDtypeStruct((CH, ROWS), F32),
            jax.ShapeDtypeStruct((CH, 512), F32),
            jax.ShapeDtypeStruct((NDP,), F32),
            jax.ShapeDtypeStruct((OWN, HD), F32),
        ),
        in_specs=[vmem] * 4,
        out_specs=(vmem,) * 4,
        name="hand_over",
    )(nxt, learn, ratio, grad)
    return nxt.T[None], learn.T[None, None], ratio, grad


def solution(mesh):
    wide = P("dp", "sp", None)
    in_specs = (
        wide, wide, wide, wide, wide, P(), P(("sp", "dp"), None), P(), P(), P(), P(), P("dp", "sp", None, None),
    )
    out_specs = (wide, P("dp", "sp", None, None), P(), P(("sp", "dp"), None))
    return jax.shard_map(on_device, mesh=mesh, in_specs=in_specs, out_specs=out_specs, check_vma=False)
```

```python
import functools

import jax
import jax.numpy as jnp
from jax import lax
from jax.experimental import pallas as pl
from jax.experimental.pallas import tpu as pltpu
from jax.sharding import PartitionSpec as P

MESH = pl.DeviceIdType.MESH
F32 = jnp.float32
BF16 = jnp.bfloat16

HD = 128
CH = 64
STEPS = 16
ETA = 0.3
CLIP = 0.2
LOSS_SCALE = 4096.0
NORM_EPS = 1e-06
NSP = 8
NDP = 16
ROWS = 256
HALF = 128
SEQ = 2048
HEADS = 3
FEAT = HEADS * HD
OWN = 24
LOG2E = 1.4426950408889634
STEP = 1.0 / STEPS

OFFSETS = ((2, 1), (2, 0), (1, 1), (3, 1), (1, 0), (3, 0), (0, 1))
NP = len(OFFSETS)


def nt(a, b):
    return lax.dot_general(a, b, (((1,), (1,)), ((), ())), preferred_element_type=F32)


def tn(a, b):
    return lax.dot_general(a, b, (((0,), (0,)), ((), ())), preferred_element_type=F32)


def nn(a, b):
    return jnp.dot(a, b, preferred_element_type=F32)


def kernel(
    q_hbm, k_hbm, v_hbm, lat_hbm, noise_hbm, hw_hbm, ad_ref, up_hbm, adv_hbm, len_hbm, time_hbm, dest_hbm,
    next_hbm, learn_hbm, ratio_hbm, grad_hbm,
    qland, kland, vland, att, prob, held, lat, noise, hw, up_ref, adv_ref, len_ref, time_ref, dest_ref,
    next_ref, learn_ref, ratio_ref, grad_ref,
    weight, early, early_square, piece, wg, cs_out, cs_in, csb, offs, placing,
    r1s, r1r, r2, slots, learn_in, g_out, g_in,
    loc_sem, s0, r0, sa, ra, sc, rc, s1, r1, s2, rr2, sl, rl, s3, r3,
):
    me = lax.axis_index("sp")
    vid = lax.axis_index("dp")
    mx, my = me // 2, me % 2

    def peer(i):
        dx, dy = OFFSETS[i]
        return ((mx + dx) % 4) * 2 + (my + dy) % 2

    def source(i):
        dx, dy = OFFSETS[i]
        return ((mx + 4 - dx) % 4) * 2 + (my + 2 - dy) % 2

    def dp_peer(e):
        return (vid + e) % NDP

    def dp_source(e):
        return (vid + NDP - e) % NDP

    def rows_of(s):
        return pl.ds(pl.multiple_of(s * ROWS, ROWS), ROWS)

    def columns_of(s, h):
        return pl.ds(pl.multiple_of(s * FEAT + h * HD, HD), HD)

    barrier = pltpu.get_barrier_semaphore()
    for i in range(NP):
        pl.semaphore_signal(barrier, inc=1, device_id=(peer(i), vid), device_id_type=MESH)
    for e in range(1, NDP):
        pl.semaphore_signal(barrier, inc=1, device_id=(me, dp_peer(e)), device_id_type=MESH)

    sources = (k_hbm, q_hbm, v_hbm)

    def landing(t, h, s):
        if t == 2:
            return vland.at[h, rows_of(s), pl.ds(0, HD)]
        return (kland, qland)[t].at[h, rows_of(s), :]

    local = []
    for g in range(9):
        h, t = g // 3, g % 3
        local.append(
            pltpu.make_async_copy(sources[t].at[0, :, columns_of(me, h)], landing(t, h, me), loc_sem.at[g])
        )
    hw_copy = pltpu.make_async_copy(
        hw_hbm.at[:, pl.ds(pl.multiple_of(me * FEAT, HD), FEAT)], hw, loc_sem.at[9]
    )
    small = [
        pltpu.make_async_copy(src, dst, loc_sem.at[10 + n])
        for n, (src, dst) in enumerate(
            (
                (up_hbm, up_ref),
                (lat_hbm, lat),
                (noise_hbm, noise),
                (adv_hbm, adv_ref),
                (len_hbm, len_ref),
                (time_hbm, time_ref),
                (dest_hbm, dest_ref),
            )
        )
    ]
    for c in small + [hw_copy]:
        c.start()

    pl.semaphore_wait(barrier, NP + NDP - 1)

    order = (0, 1, 2, 3, 4, 5, 7, 6, 8)
    groups = []
    for g in order:
        h, t = g // 3, g % 3
        groups.append(
            [
                pltpu.make_async_remote_copy(
                    src_ref=sources[t].at[0, :, columns_of(peer(i), h)],
                    dst_ref=landing(t, h, me),
                    send_sem=s0.at[g, i],
                    recv_sem=r0.at[g, i],
                    device_id=(peer(i), vid),
                    device_id_type=MESH,
                )
                for i in range(NP)
            ]
        )

    def issue(n):
        for c in groups[n]:
            c.start()

    def sent(n):
        for c in groups[n]:
            c.wait_send()

    def arrived(n):
        for c in groups[n]:
            c.wait_recv()

    for n in range(3):
        issue(n)
    for c in local:
        c.start()
    for c in small:
        c.wait()

    up = up_ref[...]
    up_low = jnp.concatenate([jnp.zeros_like(up), up], axis=0)
    piece[...] = nt(ad_ref[...], up_low)
    own_rows = pl.ds(pl.multiple_of(vid * OWN, 8), OWN)
    gather = [
        pltpu.make_async_remote_copy(
            src_ref=piece,
            dst_ref=wg.at[own_rows, :],
            send_sem=sa.at[e],
            recv_sem=ra.at[e],
            device_id=(me, dp_peer(e)),
            device_id_type=MESH,
        )
        for e in range(1, NDP)
    ]
    for c in gather:
        c.start()
    wg[own_rows, :] = piece[...]
    for h in range(HEADS):
        vland[h, :, HD:] = jnp.ones((SEQ, HD), BF16)

    length = len_ref[vid]
    moment = time_ref[vid].astype(F32)
    noise_scale = jnp.full((1, ROWS), (ETA * 0.25) * (0.5 + (1.0 - moment * STEP)), F32)
    inverse = 1.0 / (2.0 * noise_scale * noise_scale)
    token = me * ROWS + lax.broadcasted_iota(jnp.int32, (1, ROWS), 1)
    live = jnp.where(token < length, 1.0, 0.0).astype(F32)
    row_weight = live / (jnp.full((1, ROWS), length.astype(F32), F32) * CH)
    gain = row_weight * inverse
    offs[...] = noise_scale * noise[...]
    lane = lax.broadcasted_iota(jnp.int32, (1, ROWS), 1)
    targets = [dest_ref[0, b] for b in range(16)]
    place = jnp.zeros((1, ROWS), jnp.int32)
    for b in range(16):
        rank = jnp.int32(0)
        for a in range(b):
            rank = rank + jnp.where(targets[a] == targets[b], 1, 0)
        place = jnp.where(lane // 16 == b, targets[b] * 2 + rank, place)
    place = place * 16 + lane % 16
    placing[...] = (lax.broadcasted_iota(jnp.int32, (512, ROWS), 0) == place).astype(F32).astype(BF16)
    key_at = SEQ // 2 + lax.broadcasted_iota(jnp.int32, (1, SEQ // 2), 1)
    cap = jnp.where(key_at < length, 3e38, -1e30).astype(F32)

    def score(h, rows):
        return nt(qland[h, rows, :], kland[h]) * (LOG2E * HD**-0.5)

    def soften(scores):
        first = scores[:, : SEQ // 2]
        second = jnp.minimum(scores[:, SEQ // 2 :], cap)
        highest = jnp.maximum(
            jnp.max(first, axis=1, keepdims=True), jnp.max(second, axis=1, keepdims=True)
        )
        low = jnp.exp2(first - highest).astype(BF16)
        high = jnp.exp2(second - highest).astype(BF16)
        return jnp.concatenate([low, high], axis=1)

    def finish(h, rows, mixed):
        feature = (mixed[:, :HD] / mixed[:, HD:]).astype(BF16)
        att[rows, h * HD : (h + 1) * HD] = feature
        return feature

    def squares_of(feature):
        wide = feature.astype(F32)
        average = jnp.sum(wide, axis=1, keepdims=True) * (1.0 / feature.shape[1])
        centred = wide - average
        return nt(jnp.ones((16, feature.shape[1]), BF16), (centred * centred).astype(BF16))

    def block(h, b, scores):
        rows = rows_of(b)
        chances = soften(scores)
        if h == 2:
            prob[rows, :] = chances
            return
        finish(h, rows, nn(chances, vland[h]))
        if h == 1:
            feature = att[rows, 0 : 2 * HD]
            early[b] = nt(weight[:, 0 : 2 * HD], feature)
            early_square[b] = squares_of(feature)[0:8]

    def attend_all(h):
        held[0] = score(h, rows_of(0))

        @pl.loop(0, NSP // 2)
        def _(pair):
            for half in range(2):
                b = 2 * pair + half
                held[1 - half] = score(h, rows_of((b + 1) % NSP))
                block(h, b, held[half])

    for c in local + [hw_copy]:
        c.wait()
    for n in range(3):
        sent(n)
        issue(n + 3)
    for n in range(3):
        arrived(n)
    attend_all(0)

    for c in gather:
        c.wait()
    weight[0:CH, :] = hw[...]
    weight[CH : 2 * CH, :] = jnp.transpose(wg[...])[CH:, :].astype(BF16)
    weight[2 * CH :, :] = jnp.ones((16, FEAT), BF16)
    cs_out[...] = nt(jnp.ones((16, FEAT), BF16), weight[0 : 2 * CH, :])[0:8]
    cs_copies = [
        pltpu.make_async_remote_copy(
            src_ref=cs_out,
            dst_ref=cs_in.at[i],
            send_sem=sc.at[i],
            recv_sem=rc.at[i],
            device_id=(peer(i), vid),
            device_id_type=MESH,
        )
        for i in range(NP)
    ]
    for c in cs_copies:
        c.start()
    cs_in[NP] = cs_out[...]
    for n in range(3, 6):
        sent(n)
        issue(n + 3)
    for n in range(3, 6):
        arrived(n)
    attend_all(1)

    for c in cs_copies:
        c.wait()
    for i in range(NP + 1):
        spread = jnp.transpose(jnp.broadcast_to(cs_in[i][0:1], (HD, HD)))
        csb[i] = spread[CH:]

    for n in (6, 7):
        arrived(n)
    attend_all(2)
    arrived(8)

    owners = [peer(i) for i in range(NP)] + [me]
    part_copies = [
        [
            pltpu.make_async_remote_copy(
                src_ref=r1s.at[half, i],
                dst_ref=r1r.at[half, i],
                send_sem=s1.at[half, i],
                recv_sem=r1.at[half, i],
                device_id=(peer(i), vid),
                device_id_type=MESH,
            )
            for i in range(NP)
        ]
        for half in range(2)
    ]

    def tokens_of(s, half):
        return pl.ds(pl.multiple_of(s * ROWS + half * HALF, HALF), HALF)

    def mix(half, pair):
        chances = [prob[tokens_of(owners[2 * pair + one], half), :] for one in range(2)]
        return nn(jnp.concatenate(chances, axis=0), vland[2])

    row16 = lax.broadcasted_iota(jnp.int32, (16, HALF), 0)

    def partial_sums(half, pair, mixed):
        feature = (mixed[:, :HD] / mixed[:, HD:]).astype(BF16)
        sums = nt(weight[:, 2 * HD :], feature)
        late_square = squares_of(feature)
        for one in range(2):
            n = 2 * pair + one
            part = slice(one * HALF, (one + 1) * HALF)
            span = slice(half * HALF, (half + 1) * HALF)
            att[tokens_of(owners[n], half), 2 * HD :] = feature[part, :]
            before = early[owners[n], :, span]
            late = sums[:, part]
            whole = before + late
            mean = whole[2 * CH : 2 * CH + 1] * (1.0 / FEAT)
            apart = before[2 * CH : 2 * CH + 1] * (0.5 / HD) - late[2 * CH : 2 * CH + 1] * (1.0 / HD)
            square = early_square[owners[n], 0:1, span] + late_square[0:1, part]
            square = square + apart * apart * (2.0 * HD / 3.0)
            mean_high = mean.astype(BF16).astype(F32)
            square_high = square.astype(BF16).astype(F32)
            stats = jnp.where(row16 == 0, mean_high, jnp.where(row16 == 1, mean - mean_high, 0.0))
            stats = jnp.where(row16 == 2, square_high, jnp.where(row16 == 3, square - square_high, stats))
            message = jnp.concatenate([whole[:CH], whole[CH : 2 * CH] - csb[NP] * mean, stats], axis=0).astype(BF16)
            if n < NP:
                r1s[half, n] = message
                part_copies[half][n].start()
            else:
                r1r[half, NP] = message

    steps = [(half, pair) for half in range(2) for pair in range(NSP // 2)]
    mixed = mix(*steps[0])
    for n, step in enumerate(steps):
        following = mix(*steps[n + 1]) if n + 1 < len(steps) else None
        partial_sums(*step, mixed)
        mixed = following
    for n in (6, 7, 8):
        sent(n)

    def own_tokens(half):
        for c in part_copies[half]:
            c.wait_recv()
        span = slice(half * HALF, (half + 1) * HALF)
        parts = [r1r[half, i].astype(F32) for i in range(NP + 1)]
        total = functools.reduce(jnp.add, [p[: 2 * CH] for p in parts])
        means = [p[128:129] + p[129:130] for p in parts]
        squares = [p[130:131] + p[131:132] for p in parts]
        mean = functools.reduce(jnp.add, means) * (1.0 / NSP)
        gaps = [m - mean for m in means]
        variance = functools.reduce(jnp.add, squares) + FEAT * functools.reduce(jnp.add, [g * g for g in gaps])
        rstd = lax.rsqrt(variance * (1.0 / (FEAT * NSP)) + NORM_EPS)
        inner = total[CH:]
        for i in range(NP + 1):
            inner = inner + csb[i] * gaps[i]
        delta = inner * rstd
        offset = offs[:, span]
        gap = offset - STEP * delta
        unit = (gap * (gain[:, span] * (2.0 * STEP) * rstd)).astype(BF16)
        terms = gain[:, span] * jnp.sum(offset * offset - gap * gap, axis=0, keepdims=True)
        mean_high = mean.astype(BF16).astype(F32)
        terms_high = terms.astype(BF16).astype(F32)
        terms_rest = terms - terms_high
        terms_mid = terms_rest.astype(BF16).astype(F32)
        side = jnp.where(row16 == 0, mean_high, jnp.where(row16 == 1, mean - mean_high, 0.0))
        side = jnp.where(row16 == 2, terms_high, side)
        side = jnp.where(row16 == 3, terms_mid, jnp.where(row16 == 4, terms_rest - terms_mid, side))
        r2[half, me] = jnp.concatenate([unit.astype(F32), side], axis=0).astype(BF16)
        copies = [
            pltpu.make_async_remote_copy(
                src_ref=r2.at[half, me],
                dst_ref=r2.at[half, me],
                send_sem=s2.at[half, i],
                recv_sem=rr2.at[half, i],
                device_id=(peer(i), vid),
                device_id_type=MESH,
            )
            for i in range(NP)
        ]
        for c in copies:
            c.start()
        next_ref[:, span] = (lat[:, span] - STEP * total[:CH]) + offset
        return delta.astype(BF16), copies

    delta_first, copies_first = own_tokens(0)
    delta_second, copies_second = own_tokens(1)
    unit_copies = [copies_first, copies_second]

    delta_low = jnp.concatenate([delta_first, delta_second], axis=1)
    slots[...] = nt(placing[...], jnp.concatenate([delta_low, jnp.zeros_like(delta_low)], axis=0)).astype(BF16)
    mine = pl.ds(pl.multiple_of(vid * 32, 32), 32)
    learn_copies = [
        pltpu.make_async_remote_copy(
            src_ref=slots.at[pl.ds(pl.multiple_of(dp_peer(e) * 32, 32), 32), :],
            dst_ref=learn_in.at[mine, :],
            send_sem=sl.at[e],
            recv_sem=rl.at[e],
            device_id=(me, dp_peer(e)),
            device_id_type=MESH,
        )
        for e in range(1, NDP)
    ]
    for c in learn_copies:
        c.start()
    learn_in[mine, :] = slots[mine, :]
    outward = [
        pltpu.make_async_copy(src, dst, loc_sem.at[18 + n])
        for n, (src, dst) in enumerate(
            ((next_ref, next_hbm), (learn_ref, learn_hbm), (ratio_ref, ratio_hbm), (grad_ref, grad_hbm))
        )
    ]
    outward[0].start()

    def grad_part(half, s):
        u = r2[half, s, 0:CH]
        shift = nt(u, r2[half, s, CH : CH + 16])
        return nn(u, att[tokens_of(s, half), :]) - (shift[:, 0:1] + shift[:, 1:2])

    grad = grad_part(0, me) + grad_part(1, me)
    for half in range(2):
        for i in range(NP):
            unit_copies[half][i].wait_recv()
        for i in range(NP):
            grad = grad + grad_part(half, source(i))
    sides = r2[0, 0, CH : CH + 16].astype(F32) + r2[1, 0, CH : CH + 16].astype(F32)
    for s in range(1, NSP):
        sides = sides + r2[0, s, CH : CH + 16].astype(F32) + r2[1, s, CH : CH + 16].astype(F32)
    log_gain = jnp.sum(sides[2:3] + sides[3:4] + sides[4:5], axis=1, keepdims=True)
    log_gain = jnp.broadcast_to(log_gain, (8, HD))
    ratio = jnp.exp(log_gain)
    advantage = adv_ref[vid]
    clipped = jnp.clip(ratio, 1.0 - CLIP, 1.0 + CLIP)
    active = jnp.where(ratio * advantage <= clipped * advantage, 1.0, 0.0)
    pull = -(LOSS_SCALE / NDP) * advantage * ratio * active
    grad_high = grad.astype(BF16)
    grad_rest = (grad - grad_high.astype(F32)).astype(BF16)
    product = tn(jnp.concatenate([grad_high, grad_rest], axis=0), jnp.concatenate([up, up], axis=0))
    product = product * pull[0:1]
    high = log_gain.astype(BF16).astype(F32)
    middle = (log_gain - high).astype(BF16).astype(F32)
    line = lax.broadcasted_iota(jnp.int32, (8, HD), 0)
    gain_rows = jnp.where(line == 0, high, jnp.where(line == 1, middle, jnp.where(line == 2, log_gain - high - middle, 0.0)))
    for k in range(NDP):
        g_out[k] = jnp.concatenate([product[k * OWN : (k + 1) * OWN], gain_rows], axis=0).astype(BF16)
    grad_copies = [
        pltpu.make_async_remote_copy(
            src_ref=g_out.at[dp_peer(e)],
            dst_ref=g_in.at[vid],
            send_sem=s3.at[e],
            recv_sem=r3.at[e],
            device_id=(me, dp_peer(e)),
            device_id_type=MESH,
        )
        for e in range(1, NDP)
    ]
    for c in grad_copies:
        c.start()
    g_in[vid] = g_out[vid]

    for c in learn_copies:
        c.wait()
    select = lax.broadcasted_iota(jnp.int32, (CH, HD), 0) == lax.broadcasted_iota(jnp.int32, (CH, HD), 1)
    learn_ref[...] = nt(select.astype(F32).astype(BF16), learn_in[...])
    outward[1].start()
    for c in unit_copies[0] + unit_copies[1] + part_copies[0] + part_copies[1]:
        c.wait_send()

    for c in grad_copies:
        c.wait()
    summed = g_in[0].astype(F32)
    column = lax.broadcasted_iota(jnp.int32, (8, HD), 1)
    gains = jnp.where(column == 0, summed[OWN:], 0.0)
    for k in range(1, NDP):
        block = g_in[k].astype(F32)
        summed = summed + block
        gains = jnp.where(column == k, block[OWN:], gains)
    grad_ref[...] = summed[:OWN]
    outward[3].start()
    ratio_ref[...] = jnp.exp(jnp.broadcast_to(gains[0:1] + gains[1:2] + gains[2:3], (8, HD)))
    outward[2].start()
    for c in outward:
        c.wait()


def hand_over(next_in, learn_in, ratio_in, grad_in, next_out, learn_out, ratio_out, grad_out):
    next_out[...] = next_in[...]
    learn_out[...] = learn_in[...]
    grad_out[...] = grad_in[...]
    ratio_out[...] = ratio_in[0, :NDP]


def on_device(
    queries, keys, values, latents, noise, head_weight, adapter_down, adapter_up, advantages, lengths, timesteps,
    destinations,
):
    hbm = pl.BlockSpec(memory_space=pl.ANY)
    vmem = pl.BlockSpec(memory_space=pltpu.VMEM)
    dma = pltpu.SemaphoreType.DMA
    nxt, learn, ratio, grad = pl.pallas_call(
        kernel,
        out_shape=(
            jax.ShapeDtypeStruct((CH, ROWS), F32),
            jax.ShapeDtypeStruct((CH, 512), F32),
            jax.ShapeDtypeStruct((8, HD), F32),
            jax.ShapeDtypeStruct((OWN, HD), F32),
        ),
        in_specs=[hbm] * 6 + [vmem] + [hbm] * 5,
        out_specs=(hbm,) * 4,
        scratch_shapes=[
            pltpu.VMEM((HEADS, SEQ, HD), BF16),
            pltpu.VMEM((HEADS, SEQ, HD), BF16),
            pltpu.VMEM((HEADS, SEQ, 2 * HD), BF16),
            pltpu.VMEM((SEQ, FEAT), BF16),
            pltpu.VMEM((SEQ, SEQ), BF16),
            pltpu.VMEM((2, ROWS, SEQ), F32),
            pltpu.VMEM((CH, ROWS), F32),
            pltpu.VMEM((CH, ROWS), F32),
            pltpu.VMEM((CH, FEAT), BF16),
            pltpu.VMEM((CH, HD), BF16),
            pltpu.SMEM((NDP,), F32),
            pltpu.SMEM((NDP,), jnp.int32),
            pltpu.SMEM((NDP,), jnp.int32),
            pltpu.SMEM((1, 16), jnp.int32),
            pltpu.VMEM((CH, ROWS), F32),
            pltpu.VMEM((CH, 512), F32),
            pltpu.VMEM((8, HD), F32),
            pltpu.VMEM((OWN, HD), F32),
            pltpu.VMEM((144, FEAT), BF16),
            pltpu.VMEM((NSP, 144, ROWS), F32),
            pltpu.VMEM((NSP, 8, ROWS), F32),
            pltpu.VMEM((OWN, HD), F32),
            pltpu.VMEM((FEAT, HD), F32),
            pltpu.VMEM((8, HD), F32),
            pltpu.VMEM((NSP, 8, HD), F32),
            pltpu.VMEM((NSP, CH, HD), F32),
            pltpu.VMEM((CH, ROWS), F32),
            pltpu.VMEM((512, ROWS), BF16),
            pltpu.VMEM((2, NP, 144, HALF), BF16),
            pltpu.VMEM((2, NSP, 144, HALF), BF16),
            pltpu.VMEM((2, NSP, CH + 16, HALF), BF16),
            pltpu.VMEM((512, HD), BF16),
            pltpu.VMEM((512, HD), BF16),
            pltpu.VMEM((NDP, OWN + 8, HD), BF16),
            pltpu.VMEM((NDP, OWN + 8, HD), BF16),
            dma((22,)),
            dma((9, NP)), dma((9, NP)),
            dma((NDP,)), dma((NDP,)),
            dma((NP,)), dma((NP,)),
            dma((2, NP)), dma((2, NP)),
            dma((2, NP)), dma((2, NP)),
            dma((NDP,)), dma((NDP,)),
            dma((NDP,)), dma((NDP,)),
        ],
        compiler_params=pltpu.CompilerParams(
            collective_id=0, has_side_effects=True, vmem_limit_bytes=60 * 2**20
        ),
        cost_estimate=pl.CostEstimate(
            flops=7 * 10**9, bytes_accessed=6 * 10**6, transcendentals=13 * 10**6
        ),
        name="policy_step",
    )(
        queries, keys, values, latents[0].T, noise[0].T, head_weight.T, adapter_down, adapter_up.T, advantages,
        lengths, timesteps, destinations.reshape(1, 16),
    )
    nxt, learn, ratio, grad = pl.pallas_call(
        hand_over,
        out_shape=(
            jax.ShapeDtypeStruct((CH, ROWS), F32),
            jax.ShapeDtypeStruct((CH, 512), F32),
            jax.ShapeDtypeStruct((NDP,), F32),
            jax.ShapeDtypeStruct((OWN, HD), F32),
        ),
        in_specs=[vmem] * 4,
        out_specs=(vmem,) * 4,
        name="hand_over",
    )(nxt, learn, ratio, grad)
    return nxt.T[None], learn.T[None, None], ratio, grad


def solution(mesh):
    wide = P("dp", "sp", None)
    in_specs = (
        wide, wide, wide, wide, wide, P(), P(("sp", "dp"), None), P(), P(), P(), P(), P("dp", "sp", None, None),
    )
    out_specs = (wide, P("dp", "sp", None, None), P(), P(("sp", "dp"), None))
    return jax.shard_map(on_device, mesh=mesh, in_specs=in_specs, out_specs=out_specs, check_vma=False)
```

```python
import functools

import jax
import jax.numpy as jnp
from jax import lax
from jax.experimental import pallas as pl
from jax.experimental.pallas import tpu as pltpu
from jax.sharding import PartitionSpec as P

MESH = pl.DeviceIdType.MESH
F32 = jnp.float32
BF16 = jnp.bfloat16

HD = 128
CH = 64
STEPS = 16
ETA = 0.3
CLIP = 0.2
LOSS_SCALE = 4096.0
NORM_EPS = 1e-06
NSP = 8
NDP = 16
ROWS = 256
HALF = 128
SEQ = 2048
HEADS = 3
FEAT = HEADS * HD
OWN = 24
LOG2E = 1.4426950408889634
STEP = 1.0 / STEPS

OFFSETS = ((2, 1), (2, 0), (1, 1), (3, 1), (1, 0), (3, 0), (0, 1))
NP = len(OFFSETS)


def nt(a, b):
    return lax.dot_general(a, b, (((1,), (1,)), ((), ())), preferred_element_type=F32)


def tn(a, b):
    return lax.dot_general(a, b, (((0,), (0,)), ((), ())), preferred_element_type=F32)


def nn(a, b):
    return jnp.dot(a, b, preferred_element_type=F32)


def kernel(
    q_hbm, k_hbm, v_hbm, lat_hbm, noise_hbm, hw_hbm, ad_ref, up_hbm, adv_hbm, len_hbm, time_hbm, dest_hbm,
    next_hbm, learn_hbm, ratio_hbm, grad_hbm,
    qland, kland, vland, att, prob, held, lat, noise, hw, up_ref, adv_ref, len_ref, time_ref, dest_ref,
    next_ref, learn_ref, ratio_ref, grad_ref,
    weight, early, early_square, piece, wg, cs_out, cs_in, csb, offs, placing,
    r1s, r1r, vs, vr, r2, slots, learn_in, g_out, g_in,
    loc_sem, s0, r0, sa, ra, sc, rc, s1, r1, s2, rr2, sv, rv, sl, rl, s3, r3,
):
    me = lax.axis_index("sp")
    vid = lax.axis_index("dp")
    mx, my = me // 2, me % 2

    def peer(i):
        dx, dy = OFFSETS[i]
        return ((mx + dx) % 4) * 2 + (my + dy) % 2

    def source(i):
        dx, dy = OFFSETS[i]
        return ((mx + 4 - dx) % 4) * 2 + (my + 2 - dy) % 2

    def dp_peer(e):
        return (vid + e) % NDP

    def dp_source(e):
        return (vid + NDP - e) % NDP

    def rows_of(s):
        return pl.ds(pl.multiple_of(s * ROWS, ROWS), ROWS)

    def columns_of(s, h):
        return pl.ds(pl.multiple_of(s * FEAT + h * HD, HD), HD)

    barrier = pltpu.get_barrier_semaphore()
    for i in range(NP):
        pl.semaphore_signal(barrier, inc=1, device_id=(peer(i), vid), device_id_type=MESH)
    for e in range(1, NDP):
        pl.semaphore_signal(barrier, inc=1, device_id=(me, dp_peer(e)), device_id_type=MESH)

    sources = (k_hbm, q_hbm, v_hbm)

    def landing(t, h, s):
        if t == 2:
            return vland.at[h, rows_of(s), pl.ds(0, HD)]
        return (kland, qland)[t].at[h, rows_of(s), :]

    local = []
    for g in range(9):
        h, t = g // 3, g % 3
        local.append(
            pltpu.make_async_copy(sources[t].at[0, :, columns_of(me, h)], landing(t, h, me), loc_sem.at[g])
        )
    hw_copy = pltpu.make_async_copy(
        hw_hbm.at[:, pl.ds(pl.multiple_of(me * FEAT, HD), FEAT)], hw, loc_sem.at[9]
    )
    small = [
        pltpu.make_async_copy(src, dst, loc_sem.at[10 + n])
        for n, (src, dst) in enumerate(
            (
                (up_hbm, up_ref),
                (lat_hbm, lat),
                (noise_hbm, noise),
                (adv_hbm, adv_ref),
                (len_hbm, len_ref),
                (time_hbm, time_ref),
                (dest_hbm, dest_ref),
            )
        )
    ]
    for c in small + [hw_copy]:
        c.start()

    pl.semaphore_wait(barrier, NP + NDP - 1)

    order = (0, 1, 2, 3, 4, 5, 7, 6, 8)
    groups = []
    for g in order:
        h, t = g // 3, g % 3
        groups.append(
            [
                pltpu.make_async_remote_copy(
                    src_ref=sources[t].at[0, :, columns_of(peer(i), h)],
                    dst_ref=landing(t, h, me),
                    send_sem=s0.at[g, i],
                    recv_sem=r0.at[g, i],
                    device_id=(peer(i), vid),
                    device_id_type=MESH,
                )
                for i in range(NP)
            ]
        )

    def issue(n):
        for c in groups[n]:
            c.start()

    def sent(n):
        for c in groups[n]:
            c.wait_send()

    def arrived(n):
        for c in groups[n]:
            c.wait_recv()

    for n in range(3):
        issue(n)
    for c in local:
        c.start()
    for c in small:
        c.wait()

    up = up_ref[...]
    up_low = jnp.concatenate([jnp.zeros_like(up), up], axis=0)
    piece[...] = nt(ad_ref[...], up_low)
    own_rows = pl.ds(pl.multiple_of(vid * OWN, 8), OWN)
    gather = [
        pltpu.make_async_remote_copy(
            src_ref=piece,
            dst_ref=wg.at[own_rows, :],
            send_sem=sa.at[e],
            recv_sem=ra.at[e],
            device_id=(me, dp_peer(e)),
            device_id_type=MESH,
        )
        for e in range(1, NDP)
    ]
    for c in gather:
        c.start()
    wg[own_rows, :] = piece[...]
    for h in range(HEADS):
        vland[h, :, HD:] = jnp.ones((SEQ, HD), BF16)

    length = len_ref[vid]
    moment = time_ref[vid].astype(F32)
    noise_scale = jnp.full((1, ROWS), (ETA * 0.25) * (0.5 + (1.0 - moment * STEP)), F32)
    inverse = 1.0 / (2.0 * noise_scale * noise_scale)
    token = me * ROWS + lax.broadcasted_iota(jnp.int32, (1, ROWS), 1)
    live = jnp.where(token < length, 1.0, 0.0).astype(F32)
    row_weight = live / (jnp.full((1, ROWS), length.astype(F32), F32) * CH)
    gain = row_weight * inverse
    offs[...] = noise_scale * noise[...]
    lane = lax.broadcasted_iota(jnp.int32, (1, ROWS), 1)
    targets = [dest_ref[0, b] for b in range(16)]
    place = jnp.zeros((1, ROWS), jnp.int32)
    for b in range(16):
        rank = jnp.int32(0)
        for a in range(b):
            rank = rank + jnp.where(targets[a] == targets[b], 1, 0)
        place = jnp.where(lane // 16 == b, targets[b] * 2 + rank, place)
    place = place * 16 + lane % 16
    placing[...] = (lax.broadcasted_iota(jnp.int32, (512, ROWS), 0) == place).astype(F32).astype(BF16)
    key_at = SEQ // 2 + lax.broadcasted_iota(jnp.int32, (1, SEQ // 2), 1)
    cap = jnp.where(key_at < length, 3e38, -1e30).astype(F32)

    def score(h, rows):
        return nt(qland[h, rows, :], kland[h]) * (LOG2E * HD**-0.5)

    def soften(scores):
        first = scores[:, : SEQ // 2]
        second = jnp.minimum(scores[:, SEQ // 2 :], cap)
        highest = jnp.maximum(
            jnp.max(first, axis=1, keepdims=True), jnp.max(second, axis=1, keepdims=True)
        )
        low = jnp.exp2(first - highest).astype(BF16)
        high = jnp.exp2(second - highest).astype(BF16)
        return jnp.concatenate([low, high], axis=1)

    def finish(h, rows, mixed):
        feature = (mixed[:, :HD] / mixed[:, HD:]).astype(BF16)
        att[rows, h * HD : (h + 1) * HD] = feature
        return feature

    def squares_of(feature):
        wide = feature.astype(F32)
        average = jnp.sum(wide, axis=1, keepdims=True) * (1.0 / feature.shape[1])
        centred = wide - average
        return nt(jnp.ones((16, feature.shape[1]), BF16), (centred * centred).astype(BF16))

    def block(h, b, scores):
        rows = rows_of(b)
        chances = soften(scores)
        if h == 2:
            prob[rows, :] = chances
            return
        finish(h, rows, nn(chances, vland[h]))
        if h == 1:
            feature = att[rows, 0 : 2 * HD]
            early[b] = nt(weight[:, 0 : 2 * HD], feature)
            early_square[b] = squares_of(feature)[0:8]

    def attend_all(h):
        held[0] = score(h, rows_of(0))

        @pl.loop(0, NSP // 2)
        def _(pair):
            for half in range(2):
                b = 2 * pair + half
                held[1 - half] = score(h, rows_of((b + 1) % NSP))
                block(h, b, held[half])

    for c in local + [hw_copy]:
        c.wait()
    for n in range(3):
        sent(n)
        issue(n + 3)
    for n in range(3):
        arrived(n)
    attend_all(0)

    for c in gather:
        c.wait()
    weight[0:CH, :] = hw[...]
    weight[CH : 2 * CH, :] = jnp.transpose(wg[...])[CH:, :].astype(BF16)
    weight[2 * CH :, :] = jnp.ones((16, FEAT), BF16)
    cs_out[...] = nt(jnp.ones((16, FEAT), BF16), weight[0 : 2 * CH, :])[0:8]
    cs_copies = [
        pltpu.make_async_remote_copy(
            src_ref=cs_out,
            dst_ref=cs_in.at[i],
            send_sem=sc.at[i],
            recv_sem=rc.at[i],
            device_id=(peer(i), vid),
            device_id_type=MESH,
        )
        for i in range(NP)
    ]
    for c in cs_copies:
        c.start()
    cs_in[NP] = cs_out[...]
    for n in range(3, 6):
        sent(n)
        issue(n + 3)
    for n in range(3, 6):
        arrived(n)
    attend_all(1)

    for c in cs_copies:
        c.wait()
    for i in range(NP + 1):
        spread = jnp.transpose(jnp.broadcast_to(cs_in[i][0:1], (HD, HD)))
        csb[i] = spread[CH:]

    for n in (6, 7):
        arrived(n)
    attend_all(2)
    arrived(8)

    owners = [peer(i) for i in range(NP)] + [me]
    part_copies = [
        [
            pltpu.make_async_remote_copy(
                src_ref=r1s.at[half, i],
                dst_ref=r1r.at[half, i],
                send_sem=s1.at[half, i],
                recv_sem=r1.at[half, i],
                device_id=(peer(i), vid),
                device_id_type=MESH,
            )
            for i in range(NP)
        ]
        for half in range(2)
    ]

    def tokens_of(s, half):
        return pl.ds(pl.multiple_of(s * ROWS + half * HALF, HALF), HALF)

    def mix(half, pair):
        chances = [prob[tokens_of(owners[2 * pair + one], half), :] for one in range(2)]
        return nn(jnp.concatenate(chances, axis=0), vland[2])

    row16 = lax.broadcasted_iota(jnp.int32, (16, HALF), 0)

    def partial_sums(half, pair, mixed):
        feature = (mixed[:, :HD] / mixed[:, HD:]).astype(BF16)
        sums = nt(weight[:, 2 * HD :], feature)
        late_square = squares_of(feature)
        for one in range(2):
            n = 2 * pair + one
            part = slice(one * HALF, (one + 1) * HALF)
            span = slice(half * HALF, (half + 1) * HALF)
            att[tokens_of(owners[n], half), 2 * HD :] = feature[part, :]
            before = early[owners[n], :, span]
            late = sums[:, part]
            whole = before + late
            mean = whole[2 * CH : 2 * CH + 1] * (1.0 / FEAT)
            apart = before[2 * CH : 2 * CH + 1] * (0.5 / HD) - late[2 * CH : 2 * CH + 1] * (1.0 / HD)
            square = early_square[owners[n], 0:1, span] + late_square[0:1, part]
            square = square + apart * apart * (2.0 * HD / 3.0)
            mean_high = mean.astype(BF16).astype(F32)
            square_high = square.astype(BF16).astype(F32)
            stats = jnp.where(row16 == 0, mean_high, jnp.where(row16 == 1, mean - mean_high, 0.0))
            stats = jnp.where(row16 == 2, square_high, jnp.where(row16 == 3, square - square_high, stats))
            message = jnp.concatenate([whole[CH : 2 * CH] - csb[NP] * mean, stats], axis=0).astype(BF16)
            if n < NP:
                vs[n, :, span] = whole[:CH].astype(BF16)
                r1s[half, n] = message
                part_copies[half][n].start()
            else:
                vr[NP, :, span] = whole[:CH].astype(BF16)
                r1r[half, NP] = message

    steps = [(half, pair) for half in range(2) for pair in range(NSP // 2)]
    mixed = mix(*steps[0])
    for n, step in enumerate(steps):
        following = mix(*steps[n + 1]) if n + 1 < len(steps) else None
        partial_sums(*step, mixed)
        mixed = following
    for n in (6, 7, 8):
        sent(n)

    def own_tokens(half):
        for c in part_copies[half]:
            c.wait_recv()
        span = slice(half * HALF, (half + 1) * HALF)
        parts = [r1r[half, i].astype(F32) for i in range(NP + 1)]
        means = [p[CH : CH + 1] + p[CH + 1 : CH + 2] for p in parts]
        squares = [p[CH + 2 : CH + 3] + p[CH + 3 : CH + 4] for p in parts]
        mean = functools.reduce(jnp.add, means) * (1.0 / NSP)
        gaps = [m - mean for m in means]
        variance = functools.reduce(jnp.add, squares) + FEAT * functools.reduce(jnp.add, [g * g for g in gaps])
        rstd = lax.rsqrt(variance * (1.0 / (FEAT * NSP)) + NORM_EPS)
        inner = functools.reduce(jnp.add, [p[:CH] for p in parts])
        for i in range(NP + 1):
            inner = inner + csb[i] * gaps[i]
        delta = inner * rstd
        offset = offs[:, span]
        gap = offset - STEP * delta
        unit = (gap * (gain[:, span] * (2.0 * STEP) * rstd)).astype(BF16)
        terms = gain[:, span] * jnp.sum(offset * offset - gap * gap, axis=0, keepdims=True)
        mean_high = mean.astype(BF16).astype(F32)
        terms_high = terms.astype(BF16).astype(F32)
        terms_rest = terms - terms_high
        terms_mid = terms_rest.astype(BF16).astype(F32)
        side = jnp.where(row16 == 0, mean_high, jnp.where(row16 == 1, mean - mean_high, 0.0))
        side = jnp.where(row16 == 2, terms_high, side)
        side = jnp.where(row16 == 3, terms_mid, jnp.where(row16 == 4, terms_rest - terms_mid, side))
        r2[half, me] = jnp.concatenate([unit.astype(F32), side], axis=0).astype(BF16)
        copies = [
            pltpu.make_async_remote_copy(
                src_ref=r2.at[half, me],
                dst_ref=r2.at[half, me],
                send_sem=s2.at[half, i],
                recv_sem=rr2.at[half, i],
                device_id=(peer(i), vid),
                device_id_type=MESH,
            )
            for i in range(NP)
        ]
        for c in copies:
            c.start()
        return delta.astype(BF16), copies

    delta_first, copies_first = own_tokens(0)
    delta_second, copies_second = own_tokens(1)
    unit_copies = [copies_first, copies_second]

    delta_low = jnp.concatenate([delta_first, delta_second], axis=1)
    slots[...] = nt(placing[...], jnp.concatenate([delta_low, jnp.zeros_like(delta_low)], axis=0)).astype(BF16)
    mine = pl.ds(pl.multiple_of(vid * 32, 32), 32)
    learn_copies = [
        pltpu.make_async_remote_copy(
            src_ref=slots.at[pl.ds(pl.multiple_of(dp_peer(e) * 32, 32), 32), :],
            dst_ref=learn_in.at[mine, :],
            send_sem=sl.at[e],
            recv_sem=rl.at[e],
            device_id=(me, dp_peer(e)),
            device_id_type=MESH,
        )
        for e in range(1, NDP)
    ]
    for c in learn_copies:
        c.start()
    learn_in[mine, :] = slots[mine, :]
    outward = [
        pltpu.make_async_copy(src, dst, loc_sem.at[18 + n])
        for n, (src, dst) in enumerate(
            ((next_ref, next_hbm), (learn_ref, learn_hbm), (ratio_ref, ratio_hbm), (grad_ref, grad_hbm))
        )
    ]
    velocity_copies = [
        pltpu.make_async_remote_copy(
            src_ref=vs.at[i],
            dst_ref=vr.at[i],
            send_sem=sv.at[i],
            recv_sem=rv.at[i],
            device_id=(peer(i), vid),
            device_id_type=MESH,
        )
        for i in range(NP)
    ]
    for c in velocity_copies:
        c.start()

    def grad_part(half, s):
        u = r2[half, s, 0:CH]
        shift = nt(u, r2[half, s, CH : CH + 16])
        return nn(u, att[tokens_of(s, half), :]) - (shift[:, 0:1] + shift[:, 1:2])

    grad = grad_part(0, me) + grad_part(1, me)
    for half in range(2):
        for i in range(NP):
            unit_copies[half][i].wait_recv()
        for i in range(NP):
            grad = grad + grad_part(half, source(i))
    sides = r2[0, 0, CH : CH + 16].astype(F32) + r2[1, 0, CH : CH + 16].astype(F32)
    for s in range(1, NSP):
        sides = sides + r2[0, s, CH : CH + 16].astype(F32) + r2[1, s, CH : CH + 16].astype(F32)
    log_gain = jnp.sum(sides[2:3] + sides[3:4] + sides[4:5], axis=1, keepdims=True)
    log_gain = jnp.broadcast_to(log_gain, (8, HD))
    ratio = jnp.exp(log_gain)
    advantage = adv_ref[vid]
    clipped = jnp.clip(ratio, 1.0 - CLIP, 1.0 + CLIP)
    active = jnp.where(ratio * advantage <= clipped * advantage, 1.0, 0.0)
    pull = -(LOSS_SCALE / NDP) * advantage * ratio * active
    grad_high = grad.astype(BF16)
    grad_rest = (grad - grad_high.astype(F32)).astype(BF16)
    product = tn(jnp.concatenate([grad_high, grad_rest], axis=0), jnp.concatenate([up, up], axis=0))
    product = product * pull[0:1]
    high = log_gain.astype(BF16).astype(F32)
    middle = (log_gain - high).astype(BF16).astype(F32)
    line = lax.broadcasted_iota(jnp.int32, (8, HD), 0)
    gain_rows = jnp.where(line == 0, high, jnp.where(line == 1, middle, jnp.where(line == 2, log_gain - high - middle, 0.0)))
    for k in range(NDP):
        g_out[k] = jnp.concatenate([product[k * OWN : (k + 1) * OWN], gain_rows], axis=0).astype(BF16)
    grad_copies = [
        pltpu.make_async_remote_copy(
            src_ref=g_out.at[dp_peer(e)],
            dst_ref=g_in.at[vid],
            send_sem=s3.at[e],
            recv_sem=r3.at[e],
            device_id=(me, dp_peer(e)),
            device_id_type=MESH,
        )
        for e in range(1, NDP)
    ]
    for c in grad_copies:
        c.start()
    g_in[vid] = g_out[vid]

    for c in learn_copies:
        c.wait()
    select = lax.broadcasted_iota(jnp.int32, (CH, HD), 0) == lax.broadcasted_iota(jnp.int32, (CH, HD), 1)
    learn_ref[...] = nt(select.astype(F32).astype(BF16), learn_in[...])
    outward[1].start()
    for c in velocity_copies:
        c.wait()
    velocity = functools.reduce(jnp.add, [vr[i].astype(F32) for i in range(NP + 1)])
    next_ref[...] = (lat[...] - STEP * velocity) + offs[...]
    outward[0].start()
    for c in unit_copies[0] + unit_copies[1] + part_copies[0] + part_copies[1]:
        c.wait_send()

    for c in grad_copies:
        c.wait()
    summed = g_in[0].astype(F32)
    column = lax.broadcasted_iota(jnp.int32, (8, HD), 1)
    gains = jnp.where(column == 0, summed[OWN:], 0.0)
    for k in range(1, NDP):
        block = g_in[k].astype(F32)
        summed = summed + block
        gains = jnp.where(column == k, block[OWN:], gains)
    grad_ref[...] = summed[:OWN]
    outward[3].start()
    ratio_ref[...] = jnp.exp(jnp.broadcast_to(gains[0:1] + gains[1:2] + gains[2:3], (8, HD)))
    outward[2].start()
    for c in outward:
        c.wait()


def hand_over(next_in, learn_in, ratio_in, grad_in, next_out, learn_out, ratio_out, grad_out):
    next_out[...] = next_in[...]
    learn_out[...] = learn_in[...]
    grad_out[...] = grad_in[...]
    ratio_out[...] = ratio_in[0, :NDP]


def on_device(
    queries, keys, values, latents, noise, head_weight, adapter_down, adapter_up, advantages, lengths, timesteps,
    destinations,
):
    hbm = pl.BlockSpec(memory_space=pl.ANY)
    vmem = pl.BlockSpec(memory_space=pltpu.VMEM)
    dma = pltpu.SemaphoreType.DMA
    nxt, learn, ratio, grad = pl.pallas_call(
        kernel,
        out_shape=(
            jax.ShapeDtypeStruct((CH, ROWS), F32),
            jax.ShapeDtypeStruct((CH, 512), F32),
            jax.ShapeDtypeStruct((8, HD), F32),
            jax.ShapeDtypeStruct((OWN, HD), F32),
        ),
        in_specs=[hbm] * 6 + [vmem] + [hbm] * 5,
        out_specs=(hbm,) * 4,
        scratch_shapes=[
            pltpu.VMEM((HEADS, SEQ, HD), BF16),
            pltpu.VMEM((HEADS, SEQ, HD), BF16),
            pltpu.VMEM((HEADS, SEQ, 2 * HD), BF16),
            pltpu.VMEM((SEQ, FEAT), BF16),
            pltpu.VMEM((SEQ, SEQ), BF16),
            pltpu.VMEM((2, ROWS, SEQ), F32),
            pltpu.VMEM((CH, ROWS), F32),
            pltpu.VMEM((CH, ROWS), F32),
            pltpu.VMEM((CH, FEAT), BF16),
            pltpu.VMEM((CH, HD), BF16),
            pltpu.SMEM((NDP,), F32),
            pltpu.SMEM((NDP,), jnp.int32),
            pltpu.SMEM((NDP,), jnp.int32),
            pltpu.SMEM((1, 16), jnp.int32),
            pltpu.VMEM((CH, ROWS), F32),
            pltpu.VMEM((CH, 512), F32),
            pltpu.VMEM((8, HD), F32),
            pltpu.VMEM((OWN, HD), F32),
            pltpu.VMEM((144, FEAT), BF16),
            pltpu.VMEM((NSP, 144, ROWS), F32),
            pltpu.VMEM((NSP, 8, ROWS), F32),
            pltpu.VMEM((OWN, HD), F32),
            pltpu.VMEM((FEAT, HD), F32),
            pltpu.VMEM((8, HD), F32),
            pltpu.VMEM((NSP, 8, HD), F32),
            pltpu.VMEM((NSP, CH, HD), F32),
            pltpu.VMEM((CH, ROWS), F32),
            pltpu.VMEM((512, ROWS), BF16),
            pltpu.VMEM((2, NP, CH + 16, HALF), BF16),
            pltpu.VMEM((2, NSP, CH + 16, HALF), BF16),
            pltpu.VMEM((NP, CH, ROWS), BF16),
            pltpu.VMEM((NSP, CH, ROWS), BF16),
            pltpu.VMEM((2, NSP, CH + 16, HALF), BF16),
            pltpu.VMEM((512, HD), BF16),
            pltpu.VMEM((512, HD), BF16),
            pltpu.VMEM((NDP, OWN + 8, HD), BF16),
            pltpu.VMEM((NDP, OWN + 8, HD), BF16),
            dma((22,)),
            dma((9, NP)), dma((9, NP)),
            dma((NDP,)), dma((NDP,)),
            dma((NP,)), dma((NP,)),
            dma((2, NP)), dma((2, NP)),
            dma((2, NP)), dma((2, NP)),
            dma((NP,)), dma((NP,)),
            dma((NDP,)), dma((NDP,)),
            dma((NDP,)), dma((NDP,)),
        ],
        compiler_params=pltpu.CompilerParams(
            collective_id=0, has_side_effects=True, vmem_limit_bytes=60 * 2**20
        ),
        cost_estimate=pl.CostEstimate(
            flops=7 * 10**9, bytes_accessed=6 * 10**6, transcendentals=13 * 10**6
        ),
        name="policy_step",
    )(
        queries, keys, values, latents[0].T, noise[0].T, head_weight.T, adapter_down, adapter_up.T, advantages,
        lengths, timesteps, destinations.reshape(1, 16),
    )
    nxt, learn, ratio, grad = pl.pallas_call(
        hand_over,
        out_shape=(
            jax.ShapeDtypeStruct((CH, ROWS), F32),
            jax.ShapeDtypeStruct((CH, 512), F32),
            jax.ShapeDtypeStruct((NDP,), F32),
            jax.ShapeDtypeStruct((OWN, HD), F32),
        ),
        in_specs=[vmem] * 4,
        out_specs=(vmem,) * 4,
        name="hand_over",
    )(nxt, learn, ratio, grad)
    return nxt.T[None], learn.T[None, None], ratio, grad


def solution(mesh):
    wide = P("dp", "sp", None)
    in_specs = (
        wide, wide, wide, wide, wide, P(), P(("sp", "dp"), None), P(), P(), P(), P(), P("dp", "sp", None, None),
    )
    out_specs = (wide, P("dp", "sp", None, None), P(), P(("sp", "dp"), None))
    return jax.shard_map(on_device, mesh=mesh, in_specs=in_specs, out_specs=out_specs, check_vma=False)
```

```python
import functools

import jax
import jax.numpy as jnp
from jax import lax
from jax.experimental import pallas as pl
from jax.experimental.pallas import tpu as pltpu
from jax.sharding import PartitionSpec as P

MESH = pl.DeviceIdType.MESH
F32 = jnp.float32
BF16 = jnp.bfloat16

HD = 128
CH = 64
STEPS = 16
ETA = 0.3
CLIP = 0.2
LOSS_SCALE = 4096.0
NORM_EPS = 1e-06
NSP = 8
NDP = 16
ROWS = 256
HALF = 128
SEQ = 2048
HEADS = 3
FEAT = HEADS * HD
OWN = 24
LOG2E = 1.4426950408889634
STEP = 1.0 / STEPS

OFFSETS = ((2, 1), (2, 0), (1, 1), (3, 1), (1, 0), (3, 0), (0, 1))
NP = len(OFFSETS)


def nt(a, b):
    return lax.dot_general(a, b, (((1,), (1,)), ((), ())), preferred_element_type=F32)


def tn(a, b):
    return lax.dot_general(a, b, (((0,), (0,)), ((), ())), preferred_element_type=F32)


def nn(a, b):
    return jnp.dot(a, b, preferred_element_type=F32)


def kernel(
    q_hbm, k_hbm, v_hbm, lat_hbm, noise_hbm, hw_hbm, ad_ref, up_hbm, adv_hbm, len_hbm, time_hbm, dest_hbm,
    next_hbm, learn_hbm, ratio_hbm, grad_hbm,
    qland, kland, vland, att, prob, held, lat, noise, hw, up_ref, adv_ref, len_ref, time_ref, dest_ref,
    next_ref, learn_ref, ratio_ref, grad_ref,
    weight, early, early_square, piece, wg, cs_out, cs_in, csb, offs, placing,
    r1s, r1r, vs, vr, r2, slots, learn_in, g_out, g_in,
    loc_sem, s0, r0, sa, ra, sc, rc, s1, r1, s2, rr2, sv, rv, sl, rl, s3, r3,
):
    me = lax.axis_index("sp")
    vid = lax.axis_index("dp")
    mx, my = me // 2, me % 2

    def peer(i):
        dx, dy = OFFSETS[i]
        return ((mx + dx) % 4) * 2 + (my + dy) % 2

    def source(i):
        dx, dy = OFFSETS[i]
        return ((mx + 4 - dx) % 4) * 2 + (my + 2 - dy) % 2

    def dp_peer(e):
        return (vid + e) % NDP

    def dp_source(e):
        return (vid + NDP - e) % NDP

    def rows_of(s):
        return pl.ds(pl.multiple_of(s * ROWS, ROWS), ROWS)

    def columns_of(s, h):
        return pl.ds(pl.multiple_of(s * FEAT + h * HD, HD), HD)

    barrier = pltpu.get_barrier_semaphore()
    for i in range(NP):
        pl.semaphore_signal(barrier, inc=1, device_id=(peer(i), vid), device_id_type=MESH)
    for e in range(1, NDP):
        pl.semaphore_signal(barrier, inc=1, device_id=(me, dp_peer(e)), device_id_type=MESH)

    sources = (k_hbm, q_hbm, v_hbm)

    def landing(t, h, s):
        if t == 2:
            return vland.at[h, rows_of(s), pl.ds(0, HD)]
        return (kland, qland)[t].at[h, rows_of(s), :]

    local = []
    for g in range(9):
        h, t = g // 3, g % 3
        local.append(
            pltpu.make_async_copy(sources[t].at[0, :, columns_of(me, h)], landing(t, h, me), loc_sem.at[g])
        )
    hw_copy = pltpu.make_async_copy(
        hw_hbm.at[:, pl.ds(pl.multiple_of(me * FEAT, HD), FEAT)], hw, loc_sem.at[9]
    )
    small = [
        pltpu.make_async_copy(src, dst, loc_sem.at[10 + n])
        for n, (src, dst) in enumerate(
            (
                (up_hbm, up_ref),
                (lat_hbm, lat),
                (noise_hbm, noise),
                (adv_hbm, adv_ref),
                (len_hbm, len_ref),
                (time_hbm, time_ref),
                (dest_hbm, dest_ref),
            )
        )
    ]
    for c in small + [hw_copy]:
        c.start()

    pl.semaphore_wait(barrier, NP + NDP - 1)

    order = (0, 1, 2, 3, 4, 5, 7, 6, 8)
    groups = []
    for g in order:
        h, t = g // 3, g % 3
        groups.append(
            [
                pltpu.make_async_remote_copy(
                    src_ref=sources[t].at[0, :, columns_of(peer(i), h)],
                    dst_ref=landing(t, h, me),
                    send_sem=s0.at[g, i],
                    recv_sem=r0.at[g, i],
                    device_id=(peer(i), vid),
                    device_id_type=MESH,
                )
                for i in range(NP)
            ]
        )

    def issue(n):
        for c in groups[n]:
            c.start()

    def sent(n):
        for c in groups[n]:
            c.wait_send()

    def arrived(n):
        for c in groups[n]:
            c.wait_recv()

    for n in range(2):
        issue(n)
    for c in local:
        c.start()
    for c in small:
        c.wait()

    up = up_ref[...]
    up_low = jnp.concatenate([jnp.zeros_like(up), up], axis=0)
    piece[...] = nt(ad_ref[...], up_low)
    own_rows = pl.ds(pl.multiple_of(vid * OWN, 8), OWN)
    gather = [
        pltpu.make_async_remote_copy(
            src_ref=piece,
            dst_ref=wg.at[own_rows, :],
            send_sem=sa.at[e],
            recv_sem=ra.at[e],
            device_id=(me, dp_peer(e)),
            device_id_type=MESH,
        )
        for e in range(1, NDP)
    ]
    for c in gather:
        c.start()
    wg[own_rows, :] = piece[...]
    for h in range(HEADS):
        vland[h, :, HD:] = jnp.ones((SEQ, HD), BF16)

    length = len_ref[vid]
    moment = time_ref[vid].astype(F32)
    noise_scale = jnp.full((1, ROWS), (ETA * 0.25) * (0.5 + (1.0 - moment * STEP)), F32)
    inverse = 1.0 / (2.0 * noise_scale * noise_scale)
    token = me * ROWS + lax.broadcasted_iota(jnp.int32, (1, ROWS), 1)
    live = jnp.where(token < length, 1.0, 0.0).astype(F32)
    row_weight = live / (jnp.full((1, ROWS), length.astype(F32), F32) * CH)
    gain = row_weight * inverse
    offs[...] = noise_scale * noise[...]
    lane = lax.broadcasted_iota(jnp.int32, (1, ROWS), 1)
    targets = [dest_ref[0, b] for b in range(16)]
    place = jnp.zeros((1, ROWS), jnp.int32)
    for b in range(16):
        rank = jnp.int32(0)
        for a in range(b):
            rank = rank + jnp.where(targets[a] == targets[b], 1, 0)
        place = jnp.where(lane // 16 == b, targets[b] * 2 + rank, place)
    place = place * 16 + lane % 16
    placing[...] = (lax.broadcasted_iota(jnp.int32, (512, ROWS), 0) == place).astype(F32).astype(BF16)
    key_at = SEQ // 2 + lax.broadcasted_iota(jnp.int32, (1, SEQ // 2), 1)
    cap = jnp.where(key_at < length, 3e38, -1e30).astype(F32)

    def score(h, rows):
        return nt(qland[h, rows, :], kland[h]) * (LOG2E * HD**-0.5)

    def soften(scores):
        first = scores[:, : SEQ // 2]
        second = jnp.minimum(scores[:, SEQ // 2 :], cap)
        highest = jnp.maximum(
            jnp.max(first, axis=1, keepdims=True), jnp.max(second, axis=1, keepdims=True)
        )
        low = jnp.exp2(first - highest).astype(BF16)
        high = jnp.exp2(second - highest).astype(BF16)
        return jnp.concatenate([low, high], axis=1)

    def finish(h, rows, mixed):
        feature = (mixed[:, :HD] / mixed[:, HD:]).astype(BF16)
        att[rows, h * HD : (h + 1) * HD] = feature
        return feature

    def squares_of(feature):
        wide = feature.astype(F32)
        average = jnp.sum(wide, axis=1, keepdims=True) * (1.0 / feature.shape[1])
        centred = wide - average
        return nt(jnp.ones((16, feature.shape[1]), BF16), (centred * centred).astype(BF16))

    def block(h, b, scores):
        rows = rows_of(b)
        chances = soften(scores)
        if h == 2:
            prob[rows, :] = chances
            return
        finish(h, rows, nn(chances, vland[h]))
        if h == 1:
            feature = att[rows, 0 : 2 * HD]
            early[b] = nt(weight[:, 0 : 2 * HD], feature)
            early_square[b] = squares_of(feature)[0:8]

    def attend_all(h):
        held[0] = score(h, rows_of(0))

        @pl.loop(0, NSP // 2)
        def _(pair):
            for half in range(2):
                b = 2 * pair + half
                held[1 - half] = score(h, rows_of((b + 1) % NSP))
                block(h, b, held[half])

    for c in local + [hw_copy]:
        c.wait()
    for n in range(3):
        sent(n)
        issue(n + 2)
    for n in range(3):
        arrived(n)
    attend_all(0)

    for c in gather:
        c.wait()
    weight[0:CH, :] = hw[...]
    weight[CH : 2 * CH, :] = jnp.transpose(wg[...])[CH:, :].astype(BF16)
    weight[2 * CH :, :] = jnp.ones((16, FEAT), BF16)
    cs_out[...] = nt(jnp.ones((16, FEAT), BF16), weight[0 : 2 * CH, :])[0:8]
    cs_copies = [
        pltpu.make_async_remote_copy(
            src_ref=cs_out,
            dst_ref=cs_in.at[i],
            send_sem=sc.at[i],
            recv_sem=rc.at[i],
            device_id=(peer(i), vid),
            device_id_type=MESH,
        )
        for i in range(NP)
    ]
    for c in cs_copies:
        c.start()
    cs_in[NP] = cs_out[...]
    for n in range(3, 6):
        sent(n)
        issue(n + 2)
    for n in range(3, 6):
        arrived(n)
    attend_all(1)

    for c in cs_copies:
        c.wait()
    for i in range(NP + 1):
        spread = jnp.transpose(jnp.broadcast_to(cs_in[i][0:1], (HD, HD)))
        csb[i] = spread[CH:]

    sent(6)
    issue(8)
    for n in (6, 7):
        arrived(n)
    attend_all(2)
    arrived(8)

    owners = [peer(i) for i in range(NP)] + [me]
    part_copies = [
        [
            pltpu.make_async_remote_copy(
                src_ref=r1s.at[half, i],
                dst_ref=r1r.at[half, i],
                send_sem=s1.at[half, i],
                recv_sem=r1.at[half, i],
                device_id=(peer(i), vid),
                device_id_type=MESH,
            )
            for i in range(NP)
        ]
        for half in range(2)
    ]

    def tokens_of(s, half):
        return pl.ds(pl.multiple_of(s * ROWS + half * HALF, HALF), HALF)

    def mix(half, pair):
        chances = [prob[tokens_of(owners[2 * pair + one], half), :] for one in range(2)]
        return nn(jnp.concatenate(chances, axis=0), vland[2])

    row16 = lax.broadcasted_iota(jnp.int32, (16, HALF), 0)

    def partial_sums(half, pair, mixed):
        feature = (mixed[:, :HD] / mixed[:, HD:]).astype(BF16)
        sums = nt(weight[:, 2 * HD :], feature)
        late_square = squares_of(feature)
        for one in range(2):
            n = 2 * pair + one
            part = slice(one * HALF, (one + 1) * HALF)
            span = slice(half * HALF, (half + 1) * HALF)
            att[tokens_of(owners[n], half), 2 * HD :] = feature[part, :]
            before = early[owners[n], :, span]
            late = sums[:, part]
            whole = before + late
            mean = whole[2 * CH : 2 * CH + 1] * (1.0 / FEAT)
            apart = before[2 * CH : 2 * CH + 1] * (0.5 / HD) - late[2 * CH : 2 * CH + 1] * (1.0 / HD)
            square = early_square[owners[n], 0:1, span] + late_square[0:1, part]
            square = square + apart * apart * (2.0 * HD / 3.0)
            mean_high = mean.astype(BF16).astype(F32)
            square_high = square.astype(BF16).astype(F32)
            stats = jnp.where(row16 == 0, mean_high, jnp.where(row16 == 1, mean - mean_high, 0.0))
            stats = jnp.where(row16 == 2, square_high, jnp.where(row16 == 3, square - square_high, stats))
            message = jnp.concatenate([whole[CH : 2 * CH] - csb[NP] * mean, stats], axis=0).astype(BF16)
            if n < NP:
                vs[n, :, span] = whole[:CH].astype(BF16)
                r1s[half, n] = message
                part_copies[half][n].start()
            else:
                vr[NP, :, span] = whole[:CH].astype(BF16)
                r1r[half, NP] = message

    steps = [(half, pair) for half in range(2) for pair in range(NSP // 2)]
    mixed = mix(*steps[0])
    for n, step in enumerate(steps):
        following = mix(*steps[n + 1]) if n + 1 < len(steps) else None
        partial_sums(*step, mixed)
        mixed = following
    for n in (7, 8):
        sent(n)

    def own_tokens(half):
        for c in part_copies[half]:
            c.wait_recv()
        span = slice(half * HALF, (half + 1) * HALF)
        parts = [r1r[half, i].astype(F32) for i in range(NP + 1)]
        means = [p[CH : CH + 1] + p[CH + 1 : CH + 2] for p in parts]
        squares = [p[CH + 2 : CH + 3] + p[CH + 3 : CH + 4] for p in parts]
        mean = functools.reduce(jnp.add, means) * (1.0 / NSP)
        gaps = [m - mean for m in means]
        variance = functools.reduce(jnp.add, squares) + FEAT * functools.reduce(jnp.add, [g * g for g in gaps])
        rstd = lax.rsqrt(variance * (1.0 / (FEAT * NSP)) + NORM_EPS)
        inner = functools.reduce(jnp.add, [p[:CH] for p in parts])
        for i in range(NP + 1):
            inner = inner + csb[i] * gaps[i]
        delta = inner * rstd
        offset = offs[:, span]
        gap = offset - STEP * delta
        unit = (gap * (gain[:, span] * (2.0 * STEP) * rstd)).astype(BF16)
        terms = gain[:, span] * jnp.sum(offset * offset - gap * gap, axis=0, keepdims=True)
        mean_high = mean.astype(BF16).astype(F32)
        terms_high = terms.astype(BF16).astype(F32)
        terms_rest = terms - terms_high
        terms_mid = terms_rest.astype(BF16).astype(F32)
        side = jnp.where(row16 == 0, mean_high, jnp.where(row16 == 1, mean - mean_high, 0.0))
        side = jnp.where(row16 == 2, terms_high, side)
        side = jnp.where(row16 == 3, terms_mid, jnp.where(row16 == 4, terms_rest - terms_mid, side))
        r2[half, me] = jnp.concatenate([unit.astype(F32), side], axis=0).astype(BF16)
        copies = [
            pltpu.make_async_remote_copy(
                src_ref=r2.at[half, me],
                dst_ref=r2.at[half, me],
                send_sem=s2.at[half, i],
                recv_sem=rr2.at[half, i],
                device_id=(peer(i), vid),
                device_id_type=MESH,
            )
            for i in range(NP)
        ]
        for c in copies:
            c.start()
        return delta.astype(BF16), copies

    delta_first, copies_first = own_tokens(0)
    delta_second, copies_second = own_tokens(1)
    unit_copies = [copies_first, copies_second]

    delta_low = jnp.concatenate([delta_first, delta_second], axis=1)
    slots[...] = nt(placing[...], jnp.concatenate([delta_low, jnp.zeros_like(delta_low)], axis=0)).astype(BF16)
    mine = pl.ds(pl.multiple_of(vid * 32, 32), 32)
    learn_copies = [
        pltpu.make_async_remote_copy(
            src_ref=slots.at[pl.ds(pl.multiple_of(dp_peer(e) * 32, 32), 32), :],
            dst_ref=learn_in.at[mine, :],
            send_sem=sl.at[e],
            recv_sem=rl.at[e],
            device_id=(me, dp_peer(e)),
            device_id_type=MESH,
        )
        for e in range(1, NDP)
    ]
    for c in learn_copies:
        c.start()
    learn_in[mine, :] = slots[mine, :]
    outward = [
        pltpu.make_async_copy(src, dst, loc_sem.at[18 + n])
        for n, (src, dst) in enumerate(
            ((next_ref, next_hbm), (learn_ref, learn_hbm), (ratio_ref, ratio_hbm), (grad_ref, grad_hbm))
        )
    ]
    velocity_copies = [
        pltpu.make_async_remote_copy(
            src_ref=vs.at[i],
            dst_ref=vr.at[i],
            send_sem=sv.at[i],
            recv_sem=rv.at[i],
            device_id=(peer(i), vid),
            device_id_type=MESH,
        )
        for i in range(NP)
    ]
    for c in velocity_copies:
        c.start()

    def grad_part(half, s):
        u = r2[half, s, 0:CH]
        shift = nt(u, r2[half, s, CH : CH + 16])
        return nn(u, att[tokens_of(s, half), :]) - (shift[:, 0:1] + shift[:, 1:2])

    grad = grad_part(0, me) + grad_part(1, me)
    for half in range(2):
        for i in range(NP):
            unit_copies[half][i].wait_recv()
        for i in range(NP):
            grad = grad + grad_part(half, source(i))
    sides = r2[0, 0, CH : CH + 16].astype(F32) + r2[1, 0, CH : CH + 16].astype(F32)
    for s in range(1, NSP):
        sides = sides + r2[0, s, CH : CH + 16].astype(F32) + r2[1, s, CH : CH + 16].astype(F32)
    log_gain = jnp.sum(sides[2:3] + sides[3:4] + sides[4:5], axis=1, keepdims=True)
    log_gain = jnp.broadcast_to(log_gain, (8, HD))
    ratio = jnp.exp(log_gain)
    advantage = adv_ref[vid]
    clipped = jnp.clip(ratio, 1.0 - CLIP, 1.0 + CLIP)
    active = jnp.where(ratio * advantage <= clipped * advantage, 1.0, 0.0)
    pull = -(LOSS_SCALE / NDP) * advantage * ratio * active
    grad_high = grad.astype(BF16)
    grad_rest = (grad - grad_high.astype(F32)).astype(BF16)
    product = tn(jnp.concatenate([grad_high, grad_rest], axis=0), jnp.concatenate([up, up], axis=0))
    product = product * pull[0:1]
    high = log_gain.astype(BF16).astype(F32)
    middle = (log_gain - high).astype(BF16).astype(F32)
    line = lax.broadcasted_iota(jnp.int32, (8, HD), 0)
    gain_rows = jnp.where(line == 0, high, jnp.where(line == 1, middle, jnp.where(line == 2, log_gain - high - middle, 0.0)))
    for k in range(NDP):
        g_out[k] = jnp.concatenate([product[k * OWN : (k + 1) * OWN], gain_rows], axis=0).astype(BF16)
    grad_copies = [
        pltpu.make_async_remote_copy(
            src_ref=g_out.at[dp_peer(e)],
            dst_ref=g_in.at[vid],
            send_sem=s3.at[e],
            recv_sem=r3.at[e],
            device_id=(me, dp_peer(e)),
            device_id_type=MESH,
        )
        for e in range(1, NDP)
    ]
    for c in grad_copies:
        c.start()
    g_in[vid] = g_out[vid]

    for c in learn_copies:
        c.wait()
    select = lax.broadcasted_iota(jnp.int32, (CH, HD), 0) == lax.broadcasted_iota(jnp.int32, (CH, HD), 1)
    learn_ref[...] = nt(select.astype(F32).astype(BF16), learn_in[...])
    outward[1].start()
    for c in velocity_copies:
        c.wait()
    velocity = functools.reduce(jnp.add, [vr[i].astype(F32) for i in range(NP + 1)])
    next_ref[...] = (lat[...] - STEP * velocity) + offs[...]
    outward[0].start()
    for c in unit_copies[0] + unit_copies[1] + part_copies[0] + part_copies[1]:
        c.wait_send()

    for c in grad_copies:
        c.wait()
    summed = g_in[0].astype(F32)
    column = lax.broadcasted_iota(jnp.int32, (8, HD), 1)
    gains = jnp.where(column == 0, summed[OWN:], 0.0)
    for k in range(1, NDP):
        block = g_in[k].astype(F32)
        summed = summed + block
        gains = jnp.where(column == k, block[OWN:], gains)
    grad_ref[...] = summed[:OWN]
    outward[3].start()
    ratio_ref[...] = jnp.exp(jnp.broadcast_to(gains[0:1] + gains[1:2] + gains[2:3], (8, HD)))
    outward[2].start()
    for c in outward:
        c.wait()


def hand_over(next_in, learn_in, ratio_in, grad_in, next_out, learn_out, ratio_out, grad_out):
    next_out[...] = next_in[...]
    learn_out[...] = learn_in[...]
    grad_out[...] = grad_in[...]
    ratio_out[...] = ratio_in[0, :NDP]


def on_device(
    queries, keys, values, latents, noise, head_weight, adapter_down, adapter_up, advantages, lengths, timesteps,
    destinations,
):
    hbm = pl.BlockSpec(memory_space=pl.ANY)
    vmem = pl.BlockSpec(memory_space=pltpu.VMEM)
    dma = pltpu.SemaphoreType.DMA
    nxt, learn, ratio, grad = pl.pallas_call(
        kernel,
        out_shape=(
            jax.ShapeDtypeStruct((CH, ROWS), F32),
            jax.ShapeDtypeStruct((CH, 512), F32),
            jax.ShapeDtypeStruct((8, HD), F32),
            jax.ShapeDtypeStruct((OWN, HD), F32),
        ),
        in_specs=[hbm] * 6 + [vmem] + [hbm] * 5,
        out_specs=(hbm,) * 4,
        scratch_shapes=[
            pltpu.VMEM((HEADS, SEQ, HD), BF16),
            pltpu.VMEM((HEADS, SEQ, HD), BF16),
            pltpu.VMEM((HEADS, SEQ, 2 * HD), BF16),
            pltpu.VMEM((SEQ, FEAT), BF16),
            pltpu.VMEM((SEQ, SEQ), BF16),
            pltpu.VMEM((2, ROWS, SEQ), F32),
            pltpu.VMEM((CH, ROWS), F32),
            pltpu.VMEM((CH, ROWS), F32),
            pltpu.VMEM((CH, FEAT), BF16),
            pltpu.VMEM((CH, HD), BF16),
            pltpu.SMEM((NDP,), F32),
            pltpu.SMEM((NDP,), jnp.int32),
            pltpu.SMEM((NDP,), jnp.int32),
            pltpu.SMEM((1, 16), jnp.int32),
            pltpu.VMEM((CH, ROWS), F32),
            pltpu.VMEM((CH, 512), F32),
            pltpu.VMEM((8, HD), F32),
            pltpu.VMEM((OWN, HD), F32),
            pltpu.VMEM((144, FEAT), BF16),
            pltpu.VMEM((NSP, 144, ROWS), F32),
            pltpu.VMEM((NSP, 8, ROWS), F32),
            pltpu.VMEM((OWN, HD), F32),
            pltpu.VMEM((FEAT, HD), F32),
            pltpu.VMEM((8, HD), F32),
            pltpu.VMEM((NSP, 8, HD), F32),
            pltpu.VMEM((NSP, CH, HD), F32),
            pltpu.VMEM((CH, ROWS), F32),
            pltpu.VMEM((512, ROWS), BF16),
            pltpu.VMEM((2, NP, CH + 16, HALF), BF16),
            pltpu.VMEM((2, NSP, CH + 16, HALF), BF16),
            pltpu.VMEM((NP, CH, ROWS), BF16),
            pltpu.VMEM((NSP, CH, ROWS), BF16),
            pltpu.VMEM((2, NSP, CH + 16, HALF), BF16),
            pltpu.VMEM((512, HD), BF16),
            pltpu.VMEM((512, HD), BF16),
            pltpu.VMEM((NDP, OWN + 8, HD), BF16),
            pltpu.VMEM((NDP, OWN + 8, HD), BF16),
            dma((22,)),
            dma((9, NP)), dma((9, NP)),
            dma((NDP,)), dma((NDP,)),
            dma((NP,)), dma((NP,)),
            dma((2, NP)), dma((2, NP)),
            dma((2, NP)), dma((2, NP)),
            dma((NP,)), dma((NP,)),
            dma((NDP,)), dma((NDP,)),
            dma((NDP,)), dma((NDP,)),
        ],
        compiler_params=pltpu.CompilerParams(
            collective_id=0, has_side_effects=True, vmem_limit_bytes=60 * 2**20
        ),
        cost_estimate=pl.CostEstimate(
            flops=7 * 10**9, bytes_accessed=6 * 10**6, transcendentals=13 * 10**6
        ),
        name="policy_step",
    )(
        queries, keys, values, latents[0].T, noise[0].T, head_weight.T, adapter_down, adapter_up.T, advantages,
        lengths, timesteps, destinations.reshape(1, 16),
    )
    nxt, learn, ratio, grad = pl.pallas_call(
        hand_over,
        out_shape=(
            jax.ShapeDtypeStruct((CH, ROWS), F32),
            jax.ShapeDtypeStruct((CH, 512), F32),
            jax.ShapeDtypeStruct((NDP,), F32),
            jax.ShapeDtypeStruct((OWN, HD), F32),
        ),
        in_specs=[vmem] * 4,
        out_specs=(vmem,) * 4,
        name="hand_over",
    )(nxt, learn, ratio, grad)
    return nxt.T[None], learn.T[None, None], ratio, grad


def solution(mesh):
    wide = P("dp", "sp", None)
    in_specs = (
        wide, wide, wide, wide, wide, P(), P(("sp", "dp"), None), P(), P(), P(), P(), P("dp", "sp", None, None),
    )
    out_specs = (wide, P("dp", "sp", None, None), P(), P(("sp", "dp"), None))
    return jax.shard_map(on_device, mesh=mesh, in_specs=in_specs, out_specs=out_specs, check_vma=False)
```

```python
import functools

import jax
import jax.numpy as jnp
from jax import lax
from jax.experimental import pallas as pl
from jax.experimental.pallas import tpu as pltpu
from jax.sharding import PartitionSpec as P

MESH = pl.DeviceIdType.MESH
F32 = jnp.float32
BF16 = jnp.bfloat16

HD = 128
CH = 64
STEPS = 16
ETA = 0.3
CLIP = 0.2
LOSS_SCALE = 4096.0
NORM_EPS = 1e-06
NSP = 8
NDP = 16
ROWS = 256
HALF = 128
SEQ = 2048
HEADS = 3
FEAT = HEADS * HD
OWN = 24
LOG2E = 1.4426950408889634
STEP = 1.0 / STEPS

OFFSETS = ((2, 1), (2, 0), (1, 1), (3, 1), (1, 0), (3, 0), (0, 1))
NP = len(OFFSETS)


def nt(a, b):
    return lax.dot_general(a, b, (((1,), (1,)), ((), ())), preferred_element_type=F32)


def tn(a, b):
    return lax.dot_general(a, b, (((0,), (0,)), ((), ())), preferred_element_type=F32)


def nn(a, b):
    return jnp.dot(a, b, preferred_element_type=F32)


def kernel(
    q_hbm, k_hbm, v_hbm, lat_hbm, noise_hbm, hw_hbm, ad_ref, up_hbm, adv_hbm, len_hbm, time_hbm, dest_hbm,
    next_hbm, learn_hbm, ratio_hbm, grad_hbm,
    qland, kland, vland, att, prob, held, lat, noise, hw, up_ref, adv_ref, len_ref, time_ref, dest_ref,
    next_ref, learn_ref, ratio_ref, grad_ref,
    weight, early, early_square, piece, wg, cs_out, cs_in, csb, offs, placing,
    r1s, r1r, vs, vr, r2, slots, learn_in, g_out, g_in,
    loc_sem, s0, r0, sa, ra, sc, rc, s1, r1, s2, rr2, sv, rv, sl, rl, s3, r3,
):
    me = lax.axis_index("sp")
    vid = lax.axis_index("dp")
    mx, my = me // 2, me % 2

    def peer(i):
        dx, dy = OFFSETS[i]
        return ((mx + dx) % 4) * 2 + (my + dy) % 2

    def source(i):
        dx, dy = OFFSETS[i]
        return ((mx + 4 - dx) % 4) * 2 + (my + 2 - dy) % 2

    def dp_peer(e):
        return (vid + e) % NDP

    def dp_source(e):
        return (vid + NDP - e) % NDP

    def rows_of(s):
        return pl.ds(pl.multiple_of(s * ROWS, ROWS), ROWS)

    def columns_of(s, h):
        return pl.ds(pl.multiple_of(s * FEAT + h * HD, HD), HD)

    barrier = pltpu.get_barrier_semaphore()
    for i in range(NP):
        pl.semaphore_signal(barrier, inc=1, device_id=(peer(i), vid), device_id_type=MESH)
    for e in range(1, NDP):
        pl.semaphore_signal(barrier, inc=1, device_id=(me, dp_peer(e)), device_id_type=MESH)

    sources = (k_hbm, q_hbm, v_hbm)

    def landing(t, h, s):
        if t == 2:
            return vland.at[h, rows_of(s), pl.ds(0, HD)]
        return (kland, qland)[t].at[h, rows_of(s), :]

    local = []
    for g in range(9):
        h, t = g // 3, g % 3
        local.append(
            pltpu.make_async_copy(sources[t].at[0, :, columns_of(me, h)], landing(t, h, me), loc_sem.at[g])
        )
    hw_copy = pltpu.make_async_copy(
        hw_hbm.at[:, pl.ds(pl.multiple_of(me * FEAT, HD), FEAT)], hw, loc_sem.at[9]
    )
    small = [
        pltpu.make_async_copy(src, dst, loc_sem.at[10 + n])
        for n, (src, dst) in enumerate(
            (
                (up_hbm, up_ref),
                (lat_hbm, lat),
                (noise_hbm, noise),
                (adv_hbm, adv_ref),
                (len_hbm, len_ref),
                (time_hbm, time_ref),
                (dest_hbm, dest_ref),
            )
        )
    ]
    for c in small + [hw_copy]:
        c.start()

    pl.semaphore_wait(barrier, NP + NDP - 1)

    order = (0, 1, 2, 3, 4, 6, 7, 5, 8)
    groups = []
    for g in order:
        h, t = g // 3, g % 3
        groups.append(
            [
                pltpu.make_async_remote_copy(
                    src_ref=sources[t].at[0, :, columns_of(peer(i), h)],
                    dst_ref=landing(t, h, me),
                    send_sem=s0.at[g, i],
                    recv_sem=r0.at[g, i],
                    device_id=(peer(i), vid),
                    device_id_type=MESH,
                )
                for i in range(NP)
            ]
        )

    def issue(n):
        for c in groups[n]:
            c.start()

    def sent(n):
        for c in groups[n]:
            c.wait_send()

    def arrived(n):
        for c in groups[n]:
            c.wait_recv()

    for n in range(2):
        issue(n)
    for c in local:
        c.start()
    for c in small:
        c.wait()

    up = up_ref[...]
    up_low = jnp.concatenate([jnp.zeros_like(up), up], axis=0)
    piece[...] = nt(ad_ref[...], up_low)
    own_rows = pl.ds(pl.multiple_of(vid * OWN, 8), OWN)
    gather = [
        pltpu.make_async_remote_copy(
            src_ref=piece,
            dst_ref=wg.at[own_rows, :],
            send_sem=sa.at[e],
            recv_sem=ra.at[e],
            device_id=(me, dp_peer(e)),
            device_id_type=MESH,
        )
        for e in range(1, NDP)
    ]
    for c in gather:
        c.start()
    wg[own_rows, :] = piece[...]
    for h in range(HEADS):
        vland[h, :, HD:] = jnp.ones((SEQ, HD), BF16)

    length = len_ref[vid]
    moment = time_ref[vid].astype(F32)
    noise_scale = jnp.full((1, ROWS), (ETA * 0.25) * (0.5 + (1.0 - moment * STEP)), F32)
    inverse = 1.0 / (2.0 * noise_scale * noise_scale)
    token = me * ROWS + lax.broadcasted_iota(jnp.int32, (1, ROWS), 1)
    live = jnp.where(token < length, 1.0, 0.0).astype(F32)
    row_weight = live / (jnp.full((1, ROWS), length.astype(F32), F32) * CH)
    gain = row_weight * inverse
    offs[...] = noise_scale * noise[...]
    lane = lax.broadcasted_iota(jnp.int32, (1, ROWS), 1)
    targets = [dest_ref[0, b] for b in range(16)]
    place = jnp.zeros((1, ROWS), jnp.int32)
    for b in range(16):
        rank = jnp.int32(0)
        for a in range(b):
            rank = rank + jnp.where(targets[a] == targets[b], 1, 0)
        place = jnp.where(lane // 16 == b, targets[b] * 2 + rank, place)
    place = place * 16 + lane % 16
    placing[...] = (lax.broadcasted_iota(jnp.int32, (512, ROWS), 0) == place).astype(F32).astype(BF16)
    key_at = SEQ // 2 + lax.broadcasted_iota(jnp.int32, (1, SEQ // 2), 1)
    cap = jnp.where(key_at < length, 3e38, -1e30).astype(F32)

    def score(h, rows):
        return nt(qland[h, rows, :], kland[h]) * (LOG2E * HD**-0.5)

    def soften(scores):
        first = scores[:, : SEQ // 2]
        second = jnp.minimum(scores[:, SEQ // 2 :], cap)
        highest = jnp.maximum(
            jnp.max(first, axis=1, keepdims=True), jnp.max(second, axis=1, keepdims=True)
        )
        low = jnp.exp2(first - highest).astype(BF16)
        high = jnp.exp2(second - highest).astype(BF16)
        return jnp.concatenate([low, high], axis=1)

    def finish(h, rows, mixed):
        feature = (mixed[:, :HD] / mixed[:, HD:]).astype(BF16)
        att[rows, h * HD : (h + 1) * HD] = feature
        return feature

    def squares_of(feature):
        wide = feature.astype(F32)
        average = jnp.sum(wide, axis=1, keepdims=True) * (1.0 / feature.shape[1])
        centred = wide - average
        return nt(jnp.ones((16, feature.shape[1]), BF16), (centred * centred).astype(BF16))

    def block(h, b, scores):
        rows = rows_of(b)
        chances = soften(scores)
        if h > 0:
            prob[h - 1, rows, :] = chances
        else:
            finish(0, rows, nn(chances, vland[0]))

    def second_head(b):
        rows = rows_of(b)
        finish(1, rows, nn(prob[0, rows, :], vland[1]))
        feature = att[rows, 0 : 2 * HD]
        early[b] = nt(weight[:, 0 : 2 * HD], feature)
        early_square[b] = squares_of(feature)[0:8]

    def attend_all(h):
        held[0] = score(h, rows_of(0))

        @pl.loop(0, NSP // 2)
        def _(pair):
            for half in range(2):
                b = 2 * pair + half
                held[1 - half] = score(h, rows_of((b + 1) % NSP))
                block(h, b, held[half])

    for c in local + [hw_copy]:
        c.wait()
    for n in range(3):
        sent(n)
        issue(n + 2)
    for n in range(3):
        arrived(n)
    attend_all(0)

    for c in gather:
        c.wait()
    weight[0:CH, :] = hw[...]
    weight[CH : 2 * CH, :] = jnp.transpose(wg[...])[CH:, :].astype(BF16)
    weight[2 * CH :, :] = jnp.ones((16, FEAT), BF16)
    cs_out[...] = nt(jnp.ones((16, FEAT), BF16), weight[0 : 2 * CH, :])[0:8]
    cs_copies = [
        pltpu.make_async_remote_copy(
            src_ref=cs_out,
            dst_ref=cs_in.at[i],
            send_sem=sc.at[i],
            recv_sem=rc.at[i],
            device_id=(peer(i), vid),
            device_id_type=MESH,
        )
        for i in range(NP)
    ]
    for c in cs_copies:
        c.start()
    cs_in[NP] = cs_out[...]
    for n in (3, 4):
        sent(n)
        issue(n + 2)
        arrived(n)
    attend_all(1)

    for c in cs_copies:
        c.wait()
    for i in range(NP + 1):
        spread = jnp.transpose(jnp.broadcast_to(cs_in[i][0:1], (HD, HD)))
        csb[i] = spread[CH:]

    for n in (5, 6):
        sent(n)
        issue(n + 2)
        arrived(n)
    attend_all(2)
    arrived(7)

    @pl.loop(0, NSP // 2)
    def _(pair):
        second_head(2 * pair)
        second_head(2 * pair + 1)

    arrived(8)

    owners = [peer(i) for i in range(NP)] + [me]
    part_copies = [
        [
            pltpu.make_async_remote_copy(
                src_ref=r1s.at[half, i],
                dst_ref=r1r.at[half, i],
                send_sem=s1.at[half, i],
                recv_sem=r1.at[half, i],
                device_id=(peer(i), vid),
                device_id_type=MESH,
            )
            for i in range(NP)
        ]
        for half in range(2)
    ]

    def tokens_of(s, half):
        return pl.ds(pl.multiple_of(s * ROWS + half * HALF, HALF), HALF)

    def mix(half, pair):
        chances = [prob[1, tokens_of(owners[2 * pair + one], half), :] for one in range(2)]
        return nn(jnp.concatenate(chances, axis=0), vland[2])

    row16 = lax.broadcasted_iota(jnp.int32, (16, HALF), 0)

    def partial_sums(half, pair, mixed):
        feature = (mixed[:, :HD] / mixed[:, HD:]).astype(BF16)
        sums = nt(weight[:, 2 * HD :], feature)
        late_square = squares_of(feature)
        for one in range(2):
            n = 2 * pair + one
            part = slice(one * HALF, (one + 1) * HALF)
            span = slice(half * HALF, (half + 1) * HALF)
            att[tokens_of(owners[n], half), 2 * HD :] = feature[part, :]
            before = early[owners[n], :, span]
            late = sums[:, part]
            whole = before + late
            mean = whole[2 * CH : 2 * CH + 1] * (1.0 / FEAT)
            apart = before[2 * CH : 2 * CH + 1] * (0.5 / HD) - late[2 * CH : 2 * CH + 1] * (1.0 / HD)
            square = early_square[owners[n], 0:1, span] + late_square[0:1, part]
            square = square + apart * apart * (2.0 * HD / 3.0)
            mean_high = mean.astype(BF16).astype(F32)
            square_high = square.astype(BF16).astype(F32)
            stats = jnp.where(row16 == 0, mean_high, jnp.where(row16 == 1, mean - mean_high, 0.0))
            stats = jnp.where(row16 == 2, square_high, jnp.where(row16 == 3, square - square_high, stats))
            message = jnp.concatenate([whole[CH : 2 * CH] - csb[NP] * mean, stats], axis=0).astype(BF16)
            if n < NP:
                vs[n, :, span] = whole[:CH].astype(BF16)
                r1s[half, n] = message
                part_copies[half][n].start()
            else:
                vr[NP, :, span] = whole[:CH].astype(BF16)
                r1r[half, NP] = message

    steps = [(half, pair) for half in range(2) for pair in range(NSP // 2)]
    mixed = mix(*steps[0])
    for n, step in enumerate(steps):
        following = mix(*steps[n + 1]) if n + 1 < len(steps) else None
        partial_sums(*step, mixed)
        mixed = following
    for n in (7, 8):
        sent(n)

    def own_tokens(half):
        for c in part_copies[half]:
            c.wait_recv()
        span = slice(half * HALF, (half + 1) * HALF)
        parts = [r1r[half, i].astype(F32) for i in range(NP + 1)]
        means = [p[CH : CH + 1] + p[CH + 1 : CH + 2] for p in parts]
        squares = [p[CH + 2 : CH + 3] + p[CH + 3 : CH + 4] for p in parts]
        mean = functools.reduce(jnp.add, means) * (1.0 / NSP)
        gaps = [m - mean for m in means]
        variance = functools.reduce(jnp.add, squares) + FEAT * functools.reduce(jnp.add, [g * g for g in gaps])
        rstd = lax.rsqrt(variance * (1.0 / (FEAT * NSP)) + NORM_EPS)
        inner = functools.reduce(jnp.add, [p[:CH] for p in parts])
        for i in range(NP + 1):
            inner = inner + csb[i] * gaps[i]
        delta = inner * rstd
        offset = offs[:, span]
        gap = offset - STEP * delta
        unit = (gap * (gain[:, span] * (2.0 * STEP) * rstd)).astype(BF16)
        terms = gain[:, span] * jnp.sum(offset * offset - gap * gap, axis=0, keepdims=True)
        mean_high = mean.astype(BF16).astype(F32)
        terms_high = terms.astype(BF16).astype(F32)
        terms_rest = terms - terms_high
        terms_mid = terms_rest.astype(BF16).astype(F32)
        side = jnp.where(row16 == 0, mean_high, jnp.where(row16 == 1, mean - mean_high, 0.0))
        side = jnp.where(row16 == 2, terms_high, side)
        side = jnp.where(row16 == 3, terms_mid, jnp.where(row16 == 4, terms_rest - terms_mid, side))
        r2[half, me] = jnp.concatenate([unit.astype(F32), side], axis=0).astype(BF16)
        copies = [
            pltpu.make_async_remote_copy(
                src_ref=r2.at[half, me],
                dst_ref=r2.at[half, me],
                send_sem=s2.at[half, i],
                recv_sem=rr2.at[half, i],
                device_id=(peer(i), vid),
                device_id_type=MESH,
            )
            for i in range(NP)
        ]
        for c in copies:
            c.start()
        return delta.astype(BF16), copies

    delta_first, copies_first = own_tokens(0)
    delta_second, copies_second = own_tokens(1)
    unit_copies = [copies_first, copies_second]

    delta_low = jnp.concatenate([delta_first, delta_second], axis=1)
    slots[...] = nt(placing[...], jnp.concatenate([delta_low, jnp.zeros_like(delta_low)], axis=0)).astype(BF16)
    mine = pl.ds(pl.multiple_of(vid * 32, 32), 32)
    learn_copies = [
        pltpu.make_async_remote_copy(
            src_ref=slots.at[pl.ds(pl.multiple_of(dp_peer(e) * 32, 32), 32), :],
            dst_ref=learn_in.at[mine, :],
            send_sem=sl.at[e],
            recv_sem=rl.at[e],
            device_id=(me, dp_peer(e)),
            device_id_type=MESH,
        )
        for e in range(1, NDP)
    ]
    for c in learn_copies:
        c.start()
    learn_in[mine, :] = slots[mine, :]
    outward = [
        pltpu.make_async_copy(src, dst, loc_sem.at[18 + n])
        for n, (src, dst) in enumerate(
            ((next_ref, next_hbm), (learn_ref, learn_hbm), (ratio_ref, ratio_hbm), (grad_ref, grad_hbm))
        )
    ]
    velocity_copies = [
        pltpu.make_async_remote_copy(
            src_ref=vs.at[i],
            dst_ref=vr.at[i],
            send_sem=sv.at[i],
            recv_sem=rv.at[i],
            device_id=(peer(i), vid),
            device_id_type=MESH,
        )
        for i in range(NP)
    ]
    for c in velocity_copies:
        c.start()

    def grad_part(half, s):
        u = r2[half, s, 0:CH]
        shift = nt(u, r2[half, s, CH : CH + 16])
        return nn(u, att[tokens_of(s, half), :]) - (shift[:, 0:1] + shift[:, 1:2])

    grad = grad_part(0, me) + grad_part(1, me)
    for half in range(2):
        for i in range(NP):
            unit_copies[half][i].wait_recv()
        for i in range(NP):
            grad = grad + grad_part(half, source(i))
    sides = r2[0, 0, CH : CH + 16].astype(F32) + r2[1, 0, CH : CH + 16].astype(F32)
    for s in range(1, NSP):
        sides = sides + r2[0, s, CH : CH + 16].astype(F32) + r2[1, s, CH : CH + 16].astype(F32)
    log_gain = jnp.sum(sides[2:3] + sides[3:4] + sides[4:5], axis=1, keepdims=True)
    log_gain = jnp.broadcast_to(log_gain, (8, HD))
    ratio = jnp.exp(log_gain)
    advantage = adv_ref[vid]
    clipped = jnp.clip(ratio, 1.0 - CLIP, 1.0 + CLIP)
    active = jnp.where(ratio * advantage <= clipped * advantage, 1.0, 0.0)
    pull = -(LOSS_SCALE / NDP) * advantage * ratio * active
    grad_high = grad.astype(BF16)
    grad_rest = (grad - grad_high.astype(F32)).astype(BF16)
    product = tn(jnp.concatenate([grad_high, grad_rest], axis=0), jnp.concatenate([up, up], axis=0))
    product = product * pull[0:1]
    high = log_gain.astype(BF16).astype(F32)
    middle = (log_gain - high).astype(BF16).astype(F32)
    line = lax.broadcasted_iota(jnp.int32, (8, HD), 0)
    gain_rows = jnp.where(line == 0, high, jnp.where(line == 1, middle, jnp.where(line == 2, log_gain - high - middle, 0.0)))
    for k in range(NDP):
        g_out[k] = jnp.concatenate([product[k * OWN : (k + 1) * OWN], gain_rows], axis=0).astype(BF16)
    grad_copies = [
        pltpu.make_async_remote_copy(
            src_ref=g_out.at[dp_peer(e)],
            dst_ref=g_in.at[vid],
            send_sem=s3.at[e],
            recv_sem=r3.at[e],
            device_id=(me, dp_peer(e)),
            device_id_type=MESH,
        )
        for e in range(1, NDP)
    ]
    for c in grad_copies:
        c.start()
    g_in[vid] = g_out[vid]

    for c in learn_copies:
        c.wait()
    select = lax.broadcasted_iota(jnp.int32, (CH, HD), 0) == lax.broadcasted_iota(jnp.int32, (CH, HD), 1)
    learn_ref[...] = nt(select.astype(F32).astype(BF16), learn_in[...])
    outward[1].start()
    for c in velocity_copies:
        c.wait()
    velocity = functools.reduce(jnp.add, [vr[i].astype(F32) for i in range(NP + 1)])
    next_ref[...] = (lat[...] - STEP * velocity) + offs[...]
    outward[0].start()
    for c in unit_copies[0] + unit_copies[1] + part_copies[0] + part_copies[1]:
        c.wait_send()

    for c in grad_copies:
        c.wait()
    summed = g_in[0].astype(F32)
    column = lax.broadcasted_iota(jnp.int32, (8, HD), 1)
    gains = jnp.where(column == 0, summed[OWN:], 0.0)
    for k in range(1, NDP):
        block = g_in[k].astype(F32)
        summed = summed + block
        gains = jnp.where(column == k, block[OWN:], gains)
    grad_ref[...] = summed[:OWN]
    outward[3].start()
    ratio_ref[...] = jnp.exp(jnp.broadcast_to(gains[0:1] + gains[1:2] + gains[2:3], (8, HD)))
    outward[2].start()
    for c in outward:
        c.wait()


def hand_over(next_in, learn_in, ratio_in, grad_in, next_out, learn_out, ratio_out, grad_out):
    next_out[...] = next_in[...]
    learn_out[...] = learn_in[...]
    grad_out[...] = grad_in[...]
    ratio_out[...] = ratio_in[0, :NDP]


def on_device(
    queries, keys, values, latents, noise, head_weight, adapter_down, adapter_up, advantages, lengths, timesteps,
    destinations,
):
    hbm = pl.BlockSpec(memory_space=pl.ANY)
    vmem = pl.BlockSpec(memory_space=pltpu.VMEM)
    dma = pltpu.SemaphoreType.DMA
    nxt, learn, ratio, grad = pl.pallas_call(
        kernel,
        out_shape=(
            jax.ShapeDtypeStruct((CH, ROWS), F32),
            jax.ShapeDtypeStruct((CH, 512), F32),
            jax.ShapeDtypeStruct((8, HD), F32),
            jax.ShapeDtypeStruct((OWN, HD), F32),
        ),
        in_specs=[hbm] * 6 + [vmem] + [hbm] * 5,
        out_specs=(hbm,) * 4,
        scratch_shapes=[
            pltpu.VMEM((HEADS, SEQ, HD), BF16),
            pltpu.VMEM((HEADS, SEQ, HD), BF16),
            pltpu.VMEM((HEADS, SEQ, 2 * HD), BF16),
            pltpu.VMEM((SEQ, FEAT), BF16),
            pltpu.VMEM((2, SEQ, SEQ), BF16),
            pltpu.VMEM((2, ROWS, SEQ), F32),
            pltpu.VMEM((CH, ROWS), F32),
            pltpu.VMEM((CH, ROWS), F32),
            pltpu.VMEM((CH, FEAT), BF16),
            pltpu.VMEM((CH, HD), BF16),
            pltpu.SMEM((NDP,), F32),
            pltpu.SMEM((NDP,), jnp.int32),
            pltpu.SMEM((NDP,), jnp.int32),
            pltpu.SMEM((1, 16), jnp.int32),
            pltpu.VMEM((CH, ROWS), F32),
            pltpu.VMEM((CH, 512), F32),
            pltpu.VMEM((8, HD), F32),
            pltpu.VMEM((OWN, HD), F32),
            pltpu.VMEM((144, FEAT), BF16),
            pltpu.VMEM((NSP, 144, ROWS), F32),
            pltpu.VMEM((NSP, 8, ROWS), F32),
            pltpu.VMEM((OWN, HD), F32),
            pltpu.VMEM((FEAT, HD), F32),
            pltpu.VMEM((8, HD), F32),
            pltpu.VMEM((NSP, 8, HD), F32),
            pltpu.VMEM((NSP, CH, HD), F32),
            pltpu.VMEM((CH, ROWS), F32),
            pltpu.VMEM((512, ROWS), BF16),
            pltpu.VMEM((2, NP, CH + 16, HALF), BF16),
            pltpu.VMEM((2, NSP, CH + 16, HALF), BF16),
            pltpu.VMEM((NP, CH, ROWS), BF16),
            pltpu.VMEM((NSP, CH, ROWS), BF16),
            pltpu.VMEM((2, NSP, CH + 16, HALF), BF16),
            pltpu.VMEM((512, HD), BF16),
            pltpu.VMEM((512, HD), BF16),
            pltpu.VMEM((NDP, OWN + 8, HD), BF16),
            pltpu.VMEM((NDP, OWN + 8, HD), BF16),
            dma((22,)),
            dma((9, NP)), dma((9, NP)),
            dma((NDP,)), dma((NDP,)),
            dma((NP,)), dma((NP,)),
            dma((2, NP)), dma((2, NP)),
            dma((2, NP)), dma((2, NP)),
            dma((NP,)), dma((NP,)),
            dma((NDP,)), dma((NDP,)),
            dma((NDP,)), dma((NDP,)),
        ],
        compiler_params=pltpu.CompilerParams(
            collective_id=0, has_side_effects=True, vmem_limit_bytes=60 * 2**20
        ),
        cost_estimate=pl.CostEstimate(
            flops=7 * 10**9, bytes_accessed=6 * 10**6, transcendentals=13 * 10**6
        ),
        name="policy_step",
    )(
        queries, keys, values, latents[0].T, noise[0].T, head_weight.T, adapter_down, adapter_up.T, advantages,
        lengths, timesteps, destinations.reshape(1, 16),
    )
    nxt, learn, ratio, grad = pl.pallas_call(
        hand_over,
        out_shape=(
            jax.ShapeDtypeStruct((CH, ROWS), F32),
            jax.ShapeDtypeStruct((CH, 512), F32),
            jax.ShapeDtypeStruct((NDP,), F32),
            jax.ShapeDtypeStruct((OWN, HD), F32),
        ),
        in_specs=[vmem] * 4,
        out_specs=(vmem,) * 4,
        name="hand_over",
    )(nxt, learn, ratio, grad)
    return nxt.T[None], learn.T[None, None], ratio, grad


def solution(mesh):
    wide = P("dp", "sp", None)
    in_specs = (
        wide, wide, wide, wide, wide, P(), P(("sp", "dp"), None), P(), P(), P(), P(), P("dp", "sp", None, None),
    )
    out_specs = (wide, P("dp", "sp", None, None), P(), P(("sp", "dp"), None))
    return jax.shard_map(on_device, mesh=mesh, in_specs=in_specs, out_specs=out_specs, check_vma=False)
```

```python
import functools

import jax
import jax.numpy as jnp
from jax import lax
from jax.experimental import pallas as pl
from jax.experimental.pallas import tpu as pltpu
from jax.sharding import PartitionSpec as P

MESH = pl.DeviceIdType.MESH
F32 = jnp.float32
BF16 = jnp.bfloat16

HD = 128
CH = 64
STEPS = 16
ETA = 0.3
CLIP = 0.2
LOSS_SCALE = 4096.0
NORM_EPS = 1e-06
NSP = 8
NDP = 16
ROWS = 256
HALF = 128
SEQ = 2048
HEADS = 3
FEAT = HEADS * HD
OWN = 24
LOG2E = 1.4426950408889634
STEP = 1.0 / STEPS

OFFSETS = ((2, 1), (2, 0), (1, 1), (3, 1), (1, 0), (3, 0), (0, 1))
NP = len(OFFSETS)


def nt(a, b):
    return lax.dot_general(a, b, (((1,), (1,)), ((), ())), preferred_element_type=F32)


def tn(a, b):
    return lax.dot_general(a, b, (((0,), (0,)), ((), ())), preferred_element_type=F32)


def nn(a, b):
    return jnp.dot(a, b, preferred_element_type=F32)


def kernel(
    q_hbm, k_hbm, v_hbm, lat_hbm, noise_hbm, hw_hbm, ad_ref, up_hbm, adv_hbm, len_hbm, time_hbm, dest_hbm,
    next_hbm, learn_hbm, ratio_hbm, grad_hbm,
    qland, kland, vland, att, prob, held, lat, noise, hw, up_ref, adv_ref, len_ref, time_ref, dest_ref,
    next_ref, learn_ref, ratio_ref, grad_ref,
    weight, early, early_square, piece, wg, cs_out, cs_in, csb, offs, placing,
    r1s, r1r, vs, vr, r2, slots, learn_in, g_out, g_in,
    loc_sem, s0, r0, sa, ra, sc, rc, s1, r1, s2, rr2, sv, rv, sl, rl, s3, r3,
):
    me = lax.axis_index("sp")
    vid = lax.axis_index("dp")
    mx, my = me // 2, me % 2

    def peer(i):
        dx, dy = OFFSETS[i]
        return ((mx + dx) % 4) * 2 + (my + dy) % 2

    def source(i):
        dx, dy = OFFSETS[i]
        return ((mx + 4 - dx) % 4) * 2 + (my + 2 - dy) % 2

    def dp_peer(e):
        return (vid + e) % NDP

    def dp_source(e):
        return (vid + NDP - e) % NDP

    def rows_of(s):
        return pl.ds(pl.multiple_of(s * ROWS, ROWS), ROWS)

    def columns_of(s, h):
        return pl.ds(pl.multiple_of(s * FEAT + h * HD, HD), HD)

    barrier = pltpu.get_barrier_semaphore()
    for i in range(NP):
        pl.semaphore_signal(barrier, inc=1, device_id=(peer(i), vid), device_id_type=MESH)
    for e in range(1, NDP):
        pl.semaphore_signal(barrier, inc=1, device_id=(me, dp_peer(e)), device_id_type=MESH)

    sources = (k_hbm, q_hbm, v_hbm)

    def landing(t, h, s):
        if t == 2:
            return vland.at[h, rows_of(s), pl.ds(0, HD)]
        return (kland, qland)[t].at[h, rows_of(s), :]

    local = []
    for g in range(9):
        h, t = g // 3, g % 3
        local.append(
            pltpu.make_async_copy(sources[t].at[0, :, columns_of(me, h)], landing(t, h, me), loc_sem.at[g])
        )
    hw_copy = pltpu.make_async_copy(
        hw_hbm.at[:, pl.ds(pl.multiple_of(me * FEAT, HD), FEAT)], hw, loc_sem.at[9]
    )
    small = [
        pltpu.make_async_copy(src, dst, loc_sem.at[10 + n])
        for n, (src, dst) in enumerate(
            (
                (up_hbm, up_ref),
                (lat_hbm, lat),
                (noise_hbm, noise),
                (adv_hbm, adv_ref),
                (len_hbm, len_ref),
                (time_hbm, time_ref),
                (dest_hbm, dest_ref),
            )
        )
    ]
    for c in small + [hw_copy]:
        c.start()

    pl.semaphore_wait(barrier, NP + NDP - 1)

    order = (0, 1, 2, 3, 4, 6, 7, 5, 8)
    groups = []
    for g in order:
        h, t = g // 3, g % 3
        groups.append(
            [
                pltpu.make_async_remote_copy(
                    src_ref=sources[t].at[0, :, columns_of(peer(i), h)],
                    dst_ref=landing(t, h, me),
                    send_sem=s0.at[g, i],
                    recv_sem=r0.at[g, i],
                    device_id=(peer(i), vid),
                    device_id_type=MESH,
                )
                for i in range(NP)
            ]
        )

    def issue(n):
        for c in groups[n]:
            c.start()

    def sent(n):
        for c in groups[n]:
            c.wait_send()

    def arrived(n):
        for c in groups[n]:
            c.wait_recv()

    for n in range(2):
        issue(n)
    for c in local:
        c.start()
    for c in small:
        c.wait()

    up = up_ref[...]
    up_low = jnp.concatenate([jnp.zeros_like(up), up], axis=0)
    piece[...] = nt(ad_ref[...], up_low)
    own_rows = pl.ds(pl.multiple_of(vid * OWN, 8), OWN)
    gather = [
        pltpu.make_async_remote_copy(
            src_ref=piece,
            dst_ref=wg.at[own_rows, :],
            send_sem=sa.at[e],
            recv_sem=ra.at[e],
            device_id=(me, dp_peer(e)),
            device_id_type=MESH,
        )
        for e in range(1, NDP)
    ]
    for c in gather:
        c.start()
    wg[own_rows, :] = piece[...]
    for h in range(HEADS):
        vland[h, :, HD:] = jnp.ones((SEQ, HD), BF16)

    length = len_ref[vid]
    moment = time_ref[vid].astype(F32)
    noise_scale = jnp.full((1, ROWS), (ETA * 0.25) * (0.5 + (1.0 - moment * STEP)), F32)
    inverse = 1.0 / (2.0 * noise_scale * noise_scale)
    token = me * ROWS + lax.broadcasted_iota(jnp.int32, (1, ROWS), 1)
    live = jnp.where(token < length, 1.0, 0.0).astype(F32)
    row_weight = live / (jnp.full((1, ROWS), length.astype(F32), F32) * CH)
    gain = row_weight * inverse
    offs[...] = noise_scale * noise[...]
    lane = lax.broadcasted_iota(jnp.int32, (1, ROWS), 1)
    targets = [dest_ref[0, b] for b in range(16)]
    place = jnp.zeros((1, ROWS), jnp.int32)
    for b in range(16):
        rank = jnp.int32(0)
        for a in range(b):
            rank = rank + jnp.where(targets[a] == targets[b], 1, 0)
        place = jnp.where(lane // 16 == b, targets[b] * 2 + rank, place)
    place = place * 16 + lane % 16
    placing[...] = (lax.broadcasted_iota(jnp.int32, (512, ROWS), 0) == place).astype(F32).astype(BF16)
    key_at = SEQ // 2 + lax.broadcasted_iota(jnp.int32, (1, SEQ // 2), 1)
    cap = jnp.where(key_at < length, 3e38, -1e30).astype(F32)

    def score(h, rows):
        return nt(qland[h, rows, :], kland[h]) * (LOG2E * HD**-0.5)

    def soften(scores):
        first = scores[:, : SEQ // 2]
        second = jnp.minimum(scores[:, SEQ // 2 :], cap)
        highest = jnp.maximum(
            jnp.max(first, axis=1, keepdims=True), jnp.max(second, axis=1, keepdims=True)
        )
        low = jnp.exp2(first - highest).astype(BF16)
        high = jnp.exp2(second - highest).astype(BF16)
        return jnp.concatenate([low, high], axis=1)

    def finish(h, rows, mixed):
        feature = (mixed[:, :HD] / mixed[:, HD:]).astype(BF16)
        att[rows, h * HD : (h + 1) * HD] = feature
        return feature

    def squares_of(feature):
        wide = feature.astype(F32)
        average = jnp.sum(wide, axis=1, keepdims=True) * (1.0 / feature.shape[1])
        centred = wide - average
        return nt(jnp.ones((16, feature.shape[1]), BF16), (centred * centred).astype(BF16))

    def block(h, b, scores):
        rows = rows_of(b)
        chances = soften(scores)
        if h > 0:
            prob[h - 1, rows, :] = chances
        else:
            finish(0, rows, nn(chances, vland[0]))

    def second_head(b):
        rows = rows_of(b)
        finish(1, rows, nn(prob[0, rows, :], vland[1]))
        feature = att[rows, 0 : 2 * HD]
        early[b] = nt(weight[:, 0 : 2 * HD], feature)
        early_square[b] = squares_of(feature)[0:8]

    def attend_all(h):
        held[0] = score(h, rows_of(0))

        @pl.loop(0, NSP // 2)
        def _(pair):
            for half in range(2):
                b = 2 * pair + half
                held[1 - half] = score(h, rows_of((b + 1) % NSP))
                block(h, b, held[half])

    for c in local + [hw_copy]:
        c.wait()
    for n in range(3):
        sent(n)
        issue(n + 2)
    for n in range(3):
        arrived(n)
    attend_all(0)

    for c in gather:
        c.wait()
    weight[0:CH, :] = hw[...]
    weight[CH : 2 * CH, :] = jnp.transpose(wg[...])[CH:, :].astype(BF16)
    weight[2 * CH :, :] = jnp.ones((16, FEAT), BF16)
    cs_out[...] = nt(jnp.ones((16, FEAT), BF16), weight[0 : 2 * CH, :])[0:8]
    cs_copies = [
        pltpu.make_async_remote_copy(
            src_ref=cs_out,
            dst_ref=cs_in.at[i],
            send_sem=sc.at[i],
            recv_sem=rc.at[i],
            device_id=(peer(i), vid),
            device_id_type=MESH,
        )
        for i in range(NP)
    ]
    for c in cs_copies:
        c.start()
    cs_in[NP] = cs_out[...]
    for n in (3, 4):
        sent(n)
        issue(n + 2)
        arrived(n)
    attend_all(1)

    for c in cs_copies:
        c.wait()
    for i in range(NP + 1):
        spread = jnp.transpose(jnp.broadcast_to(cs_in[i][0:1], (HD, HD)))
        csb[i] = spread[CH:]

    for n in (5, 6):
        sent(n)
        issue(n + 2)
        arrived(n)
    attend_all(2)
    arrived(7)

    @pl.loop(0, NSP // 2)
    def _(pair):
        second_head(2 * pair)
        second_head(2 * pair + 1)

    arrived(8)

    owners = [peer(i) for i in range(NP)] + [me]
    part_copies = [
        [
            pltpu.make_async_remote_copy(
                src_ref=r1s.at[half, i],
                dst_ref=r1r.at[half, i],
                send_sem=s1.at[half, i],
                recv_sem=r1.at[half, i],
                device_id=(peer(i), vid),
                device_id_type=MESH,
            )
            for i in range(NP)
        ]
        for half in range(2)
    ]

    def tokens_of(s, half):
        return pl.ds(pl.multiple_of(s * ROWS + half * HALF, HALF), HALF)

    def mix(half, pair):
        chances = [prob[1, tokens_of(owners[2 * pair + one], half), :] for one in range(2)]
        return nn(jnp.concatenate(chances, axis=0), vland[2])

    row16 = lax.broadcasted_iota(jnp.int32, (16, HALF), 0)

    def partial_sums(half, pair, mixed):
        feature = (mixed[:, :HD] / mixed[:, HD:]).astype(BF16)
        sums = nt(weight[:, 2 * HD :], feature)
        late_square = squares_of(feature)
        for one in range(2):
            n = 2 * pair + one
            part = slice(one * HALF, (one + 1) * HALF)
            span = slice(half * HALF, (half + 1) * HALF)
            att[tokens_of(owners[n], half), 2 * HD :] = feature[part, :]
            before = early[owners[n], :, span]
            late = sums[:, part]
            whole = before + late
            mean = whole[2 * CH : 2 * CH + 1] * (1.0 / FEAT)
            apart = before[2 * CH : 2 * CH + 1] * (0.5 / HD) - late[2 * CH : 2 * CH + 1] * (1.0 / HD)
            square = early_square[owners[n], 0:1, span] + late_square[0:1, part]
            square = square + apart * apart * (2.0 * HD / 3.0)
            mean_high = mean.astype(BF16).astype(F32)
            square_high = square.astype(BF16).astype(F32)
            stats = jnp.where(row16 == 0, mean_high, jnp.where(row16 == 1, mean - mean_high, 0.0))
            stats = jnp.where(row16 == 2, square_high, jnp.where(row16 == 3, square - square_high, stats))
            message = jnp.concatenate([whole[CH : 2 * CH] - csb[NP] * mean, stats], axis=0).astype(BF16)
            if n < NP:
                vs[n, :, span] = whole[:CH].astype(BF16)
                r1s[half, n] = message
                part_copies[half][n].start()
            else:
                vr[NP, :, span] = whole[:CH].astype(BF16)
                r1r[half, NP] = message

    steps = [(half, pair) for half in range(2) for pair in range(NSP // 2)]
    mixed = mix(*steps[0])
    for n, step in enumerate(steps):
        following = mix(*steps[n + 1]) if n + 1 < len(steps) else None
        partial_sums(*step, mixed)
        mixed = following
    for n in (7, 8):
        sent(n)

    def own_tokens(half):
        for c in part_copies[half]:
            c.wait_recv()
        span = slice(half * HALF, (half + 1) * HALF)
        parts = [r1r[half, i].astype(F32) for i in range(NP + 1)]
        means = [p[CH : CH + 1] + p[CH + 1 : CH + 2] for p in parts]
        squares = [p[CH + 2 : CH + 3] + p[CH + 3 : CH + 4] for p in parts]
        mean = functools.reduce(jnp.add, means) * (1.0 / NSP)
        gaps = [m - mean for m in means]
        variance = functools.reduce(jnp.add, squares) + FEAT * functools.reduce(jnp.add, [g * g for g in gaps])
        rstd = lax.rsqrt(variance * (1.0 / (FEAT * NSP)) + NORM_EPS)
        inner = functools.reduce(jnp.add, [p[:CH] for p in parts])
        for i in range(NP + 1):
            inner = inner + csb[i] * gaps[i]
        delta = inner * rstd
        offset = offs[:, span]
        gap = offset - STEP * delta
        unit = (gap * (gain[:, span] * (2.0 * STEP) * rstd)).astype(BF16)
        terms = gain[:, span] * jnp.sum(offset * offset - gap * gap, axis=0, keepdims=True)
        mean_high = mean.astype(BF16).astype(F32)
        terms_high = terms.astype(BF16).astype(F32)
        terms_rest = terms - terms_high
        terms_mid = terms_rest.astype(BF16).astype(F32)
        side = jnp.where(row16 == 0, mean_high, jnp.where(row16 == 1, mean - mean_high, 0.0))
        side = jnp.where(row16 == 2, terms_high, side)
        side = jnp.where(row16 == 3, terms_mid, jnp.where(row16 == 4, terms_rest - terms_mid, side))
        r2[half, me] = jnp.concatenate([unit.astype(F32), side], axis=0).astype(BF16)
        copies = [
            pltpu.make_async_remote_copy(
                src_ref=r2.at[half, me],
                dst_ref=r2.at[half, me],
                send_sem=s2.at[half, i],
                recv_sem=rr2.at[half, i],
                device_id=(peer(i), vid),
                device_id_type=MESH,
            )
            for i in range(NP)
        ]
        for c in copies:
            c.start()
        return delta.astype(BF16), copies

    delta_first, copies_first = own_tokens(0)
    delta_second, copies_second = own_tokens(1)
    unit_copies = [copies_first, copies_second]

    delta_low = jnp.concatenate([delta_first, delta_second], axis=1)
    slots[...] = nt(placing[...], jnp.concatenate([delta_low, jnp.zeros_like(delta_low)], axis=0)).astype(BF16)
    mine = pl.ds(pl.multiple_of(vid * 32, 32), 32)
    learn_copies = [
        pltpu.make_async_remote_copy(
            src_ref=slots.at[pl.ds(pl.multiple_of(dp_peer(e) * 32, 32), 32), :],
            dst_ref=learn_in.at[mine, :],
            send_sem=sl.at[e],
            recv_sem=rl.at[e],
            device_id=(me, dp_peer(e)),
            device_id_type=MESH,
        )
        for e in range(1, NDP)
    ]
    for c in learn_copies:
        c.start()
    learn_in[mine, :] = slots[mine, :]
    outward = [
        pltpu.make_async_copy(src, dst, loc_sem.at[18 + n])
        for n, (src, dst) in enumerate(
            ((next_ref, next_hbm), (learn_ref, learn_hbm), (ratio_ref, ratio_hbm), (grad_ref, grad_hbm))
        )
    ]
    velocity_copies = [
        pltpu.make_async_remote_copy(
            src_ref=vs.at[i],
            dst_ref=vr.at[i],
            send_sem=sv.at[i],
            recv_sem=rv.at[i],
            device_id=(peer(i), vid),
            device_id_type=MESH,
        )
        for i in range(NP)
    ]

    def grad_part(half, s):
        u = r2[half, s, 0:CH]
        shift = nt(u, r2[half, s, CH : CH + 16])
        return nn(u, att[tokens_of(s, half), :]) - (shift[:, 0:1] + shift[:, 1:2])

    grad = grad_part(0, me) + grad_part(1, me)
    for half in range(2):
        for i in range(NP):
            unit_copies[half][i].wait_recv()
        if half == 1:
            for c in velocity_copies:
                c.start()
        for i in range(NP):
            grad = grad + grad_part(half, source(i))
    sides = r2[0, 0, CH : CH + 16].astype(F32) + r2[1, 0, CH : CH + 16].astype(F32)
    for s in range(1, NSP):
        sides = sides + r2[0, s, CH : CH + 16].astype(F32) + r2[1, s, CH : CH + 16].astype(F32)
    log_gain = jnp.sum(sides[2:3] + sides[3:4] + sides[4:5], axis=1, keepdims=True)
    log_gain = jnp.broadcast_to(log_gain, (8, HD))
    ratio = jnp.exp(log_gain)
    advantage = adv_ref[vid]
    clipped = jnp.clip(ratio, 1.0 - CLIP, 1.0 + CLIP)
    active = jnp.where(ratio * advantage <= clipped * advantage, 1.0, 0.0)
    pull = -(LOSS_SCALE / NDP) * advantage * ratio * active
    grad_high = grad.astype(BF16)
    grad_rest = (grad - grad_high.astype(F32)).astype(BF16)
    product = tn(jnp.concatenate([grad_high, grad_rest], axis=0), jnp.concatenate([up, up], axis=0))
    product = product * pull[0:1]
    high = log_gain.astype(BF16).astype(F32)
    middle = (log_gain - high).astype(BF16).astype(F32)
    line = lax.broadcasted_iota(jnp.int32, (8, HD), 0)
    gain_rows = jnp.where(line == 0, high, jnp.where(line == 1, middle, jnp.where(line == 2, log_gain - high - middle, 0.0)))
    for k in range(NDP):
        g_out[k] = jnp.concatenate([product[k * OWN : (k + 1) * OWN], gain_rows], axis=0).astype(BF16)
    grad_copies = [
        pltpu.make_async_remote_copy(
            src_ref=g_out.at[dp_peer(e)],
            dst_ref=g_in.at[vid],
            send_sem=s3.at[e],
            recv_sem=r3.at[e],
            device_id=(me, dp_peer(e)),
            device_id_type=MESH,
        )
        for e in range(1, NDP)
    ]
    for c in grad_copies:
        c.start()
    g_in[vid] = g_out[vid]

    for c in learn_copies:
        c.wait()
    select = lax.broadcasted_iota(jnp.int32, (CH, HD), 0) == lax.broadcasted_iota(jnp.int32, (CH, HD), 1)
    learn_ref[...] = nt(select.astype(F32).astype(BF16), learn_in[...])
    outward[1].start()
    for c in velocity_copies:
        c.wait()
    velocity = functools.reduce(jnp.add, [vr[i].astype(F32) for i in range(NP + 1)])
    next_ref[...] = (lat[...] - STEP * velocity) + offs[...]
    outward[0].start()
    for c in unit_copies[0] + unit_copies[1] + part_copies[0] + part_copies[1]:
        c.wait_send()

    for c in grad_copies:
        c.wait()
    summed = g_in[0].astype(F32)
    column = lax.broadcasted_iota(jnp.int32, (8, HD), 1)
    gains = jnp.where(column == 0, summed[OWN:], 0.0)
    for k in range(1, NDP):
        block = g_in[k].astype(F32)
        summed = summed + block
        gains = jnp.where(column == k, block[OWN:], gains)
    grad_ref[...] = summed[:OWN]
    outward[3].start()
    ratio_ref[...] = jnp.exp(jnp.broadcast_to(gains[0:1] + gains[1:2] + gains[2:3], (8, HD)))
    outward[2].start()
    for c in outward:
        c.wait()


def hand_over(next_in, learn_in, ratio_in, grad_in, next_out, learn_out, ratio_out, grad_out):
    next_out[...] = next_in[...]
    learn_out[...] = learn_in[...]
    grad_out[...] = grad_in[...]
    ratio_out[...] = ratio_in[0, :NDP]


def on_device(
    queries, keys, values, latents, noise, head_weight, adapter_down, adapter_up, advantages, lengths, timesteps,
    destinations,
):
    hbm = pl.BlockSpec(memory_space=pl.ANY)
    vmem = pl.BlockSpec(memory_space=pltpu.VMEM)
    dma = pltpu.SemaphoreType.DMA
    nxt, learn, ratio, grad = pl.pallas_call(
        kernel,
        out_shape=(
            jax.ShapeDtypeStruct((CH, ROWS), F32),
            jax.ShapeDtypeStruct((CH, 512), F32),
            jax.ShapeDtypeStruct((8, HD), F32),
            jax.ShapeDtypeStruct((OWN, HD), F32),
        ),
        in_specs=[hbm] * 6 + [vmem] + [hbm] * 5,
        out_specs=(hbm,) * 4,
        scratch_shapes=[
            pltpu.VMEM((HEADS, SEQ, HD), BF16),
            pltpu.VMEM((HEADS, SEQ, HD), BF16),
            pltpu.VMEM((HEADS, SEQ, 2 * HD), BF16),
            pltpu.VMEM((SEQ, FEAT), BF16),
            pltpu.VMEM((2, SEQ, SEQ), BF16),
            pltpu.VMEM((2, ROWS, SEQ), F32),
            pltpu.VMEM((CH, ROWS), F32),
            pltpu.VMEM((CH, ROWS), F32),
            pltpu.VMEM((CH, FEAT), BF16),
            pltpu.VMEM((CH, HD), BF16),
            pltpu.SMEM((NDP,), F32),
            pltpu.SMEM((NDP,), jnp.int32),
            pltpu.SMEM((NDP,), jnp.int32),
            pltpu.SMEM((1, 16), jnp.int32),
            pltpu.VMEM((CH, ROWS), F32),
            pltpu.VMEM((CH, 512), F32),
            pltpu.VMEM((8, HD), F32),
            pltpu.VMEM((OWN, HD), F32),
            pltpu.VMEM((144, FEAT), BF16),
            pltpu.VMEM((NSP, 144, ROWS), F32),
            pltpu.VMEM((NSP, 8, ROWS), F32),
            pltpu.VMEM((OWN, HD), F32),
            pltpu.VMEM((FEAT, HD), F32),
            pltpu.VMEM((8, HD), F32),
            pltpu.VMEM((NSP, 8, HD), F32),
            pltpu.VMEM((NSP, CH, HD), F32),
            pltpu.VMEM((CH, ROWS), F32),
            pltpu.VMEM((512, ROWS), BF16),
            pltpu.VMEM((2, NP, CH + 16, HALF), BF16),
            pltpu.VMEM((2, NSP, CH + 16, HALF), BF16),
            pltpu.VMEM((NP, CH, ROWS), BF16),
            pltpu.VMEM((NSP, CH, ROWS), BF16),
            pltpu.VMEM((2, NSP, CH + 16, HALF), BF16),
            pltpu.VMEM((512, HD), BF16),
            pltpu.VMEM((512, HD), BF16),
            pltpu.VMEM((NDP, OWN + 8, HD), BF16),
            pltpu.VMEM((NDP, OWN + 8, HD), BF16),
            dma((22,)),
            dma((9, NP)), dma((9, NP)),
            dma((NDP,)), dma((NDP,)),
            dma((NP,)), dma((NP,)),
            dma((2, NP)), dma((2, NP)),
            dma((2, NP)), dma((2, NP)),
            dma((NP,)), dma((NP,)),
            dma((NDP,)), dma((NDP,)),
            dma((NDP,)), dma((NDP,)),
        ],
        compiler_params=pltpu.CompilerParams(
            collective_id=0, has_side_effects=True, vmem_limit_bytes=60 * 2**20
        ),
        cost_estimate=pl.CostEstimate(
            flops=7 * 10**9, bytes_accessed=6 * 10**6, transcendentals=13 * 10**6
        ),
        name="policy_step",
    )(
        queries, keys, values, latents[0].T, noise[0].T, head_weight.T, adapter_down, adapter_up.T, advantages,
        lengths, timesteps, destinations.reshape(1, 16),
    )
    nxt, learn, ratio, grad = pl.pallas_call(
        hand_over,
        out_shape=(
            jax.ShapeDtypeStruct((CH, ROWS), F32),
            jax.ShapeDtypeStruct((CH, 512), F32),
            jax.ShapeDtypeStruct((NDP,), F32),
            jax.ShapeDtypeStruct((OWN, HD), F32),
        ),
        in_specs=[vmem] * 4,
        out_specs=(vmem,) * 4,
        name="hand_over",
    )(nxt, learn, ratio, grad)
    return nxt.T[None], learn.T[None, None], ratio, grad


def solution(mesh):
    wide = P("dp", "sp", None)
    in_specs = (
        wide, wide, wide, wide, wide, P(), P(("sp", "dp"), None), P(), P(), P(), P(), P("dp", "sp", None, None),
    )
    out_specs = (wide, P("dp", "sp", None, None), P(), P(("sp", "dp"), None))
    return jax.shard_map(on_device, mesh=mesh, in_specs=in_specs, out_specs=out_specs, check_vma=False)
```
